256 devices in a mesh: rows: 64 (over z, x, core), proj: 4 (over y).
Axes of the slice: x: 4, y: 4, z: 8, core: 2. Of those that a mesh axis runs over, the one named last changes fastest.
Arguments:
- q_nope: bfloat16 [4096, 8192], P('rows', 'proj'), may hold values from -6 to 6
- q_rope: bfloat16 [4096, 4096], P('rows', 'proj')
- w_uk: bfloat16 [64, 128, 512], P(None, None, 'proj'), may hold values from -0.5 to 0.5
- w_uv: bfloat16 [64, 128, 512], P(None, None, 'proj'), may hold values from -0.25 to 0.25
- prefix_latent: bfloat16 [128, 128, 512], P('rows'), may hold values from -6 to 6
- prefix_rope: bfloat16 [128, 8192], P('rows'), may hold values from -6 to 6
- suffix_latent: bfloat16 [4096, 64, 512], P('rows'), may hold values from -6 to 6
- suffix_rope: bfloat16 [4096, 4096], P('rows')
- page_slot: int32 [128], replicated, may hold values from 0 to 127, each once
- page_pattern: int32 [4096, 2], P('rows'), may hold values from 0 to 127, all different within a row; in each aligned block of 64 rows (0 to 63, 64 to 127, ...) at most 2 rows name the same one
- suffix_len: int32 [4096], P('rows'), may hold values from 1 to 64, 131072 in all
Outputs:
- attended: bfloat16 [4096, 8192], P('rows', 'proj')
The draws below stay inside these ranges and needn't reach their ends.
Inputs may be any that keep to these rules, and one draw needn't show every extreme that they name: Page p is stored at slot page_slot[p]; slots 2 * d to 2 * d + 1 lie on index d of rows. `page_pattern`: each row names 2 different pages. Among the rows of one device no page is named by more than 2 rows, and in some aligned blocks of 64 rows one page is named by exactly 2 rows. `suffix_len`: some row has all 64 slots live.
All inputs are finite; a program needn't handle non-finite values. No bound on the sum of `suffix_len` on one device may be relied on, other than what follows from the above.
Results may differ from the reference program's by a relative error of at most 0.011.
Values may be sent and summed in bfloat16 or wider, within the bound.
No kernel may reach another device: no remote copies, remote signals or barrier semaphores. Data moves between devices by JAX's collectives and lax.ppermute only.
A program may use at most 128 MiB of HBM per device.

```python
import math
import jax
import jax.numpy as jnp
import numpy as np
from jax import lax

H = 64
NOPE = 128
VDIM = 128
ROPE = 64
KVL = 512
ROWS_DEV = 64
PAGE = 128
TOPK = 2
SUF = 64
ROWS = 4096
NPAGES = 128
CAP = 2


def draw_suffix_rope(key, part):
    key = jax.random.fold_in(key, 11)
    rope_keys = jax.random.normal(key, (ROWS, SUF, ROPE), jnp.float32)
    return rope_keys.reshape(ROWS, SUF * ROPE).astype(jnp.bfloat16)


def draw_q_rope(key, part):
    key = jax.random.fold_in(key, 12)
    values = jax.random.normal(key, (ROWS, H, ROPE), jnp.float32)
    return values.reshape(ROWS, H * ROPE).astype(jnp.bfloat16)


def level_of(key, dims, pieces, smallest, largest):
    gain, own = 1.0, jax.random.fold_in(key, 6)
    for axis_at, blocks in pieces:
        steps = jnp.exp(jax.random.uniform(jax.random.fold_in(own, axis_at), (blocks,), jnp.float32, smallest / len(pieces), largest / len(pieces)))
        gain = gain * jnp.repeat(steps, dims[axis_at] // blocks).reshape([-1 if axis == axis_at else 1 for axis in range(len(dims))])
    return gain


def profile(amount, total, reach, slope):
    weights = [(1 << 20) // math.isqrt(rank ** slope) + 1 for rank in range(2, amount + 1)]
    rest, holding = total - reach - (amount - 1), [1] * (amount - 1)
    while rest > 0:
        movable = [i for i in range(amount - 1) if holding[i] < reach]
        mass, remaining = sum([weights[i] for i in movable]), rest
        for i in movable:
            more = min(reach - holding[i], max(1, remaining * weights[i] // mass), rest)
            holding[i] = holding[i] + more
            rest = rest - more
    return np.array([reach] + holding)


def ragged_sizes(stream_key, count, total, limit, skew):
    if count == 2:
        one = jax.random.randint(stream_key, (), max(1, total - limit), min(limit, total - 1) + 1)
        return jnp.stack([one, total - one])
    sizes = jnp.asarray(profile(count, total, limit, skew), jnp.int32)
    pairs = (count - 1) // 2
    giver, sink = sizes[1:1 + 2 * pairs:2], sizes[2:2 + 2 * pairs:2]
    margin = jnp.minimum(giver - 1, limit - sink)
    shifted = jax.random.randint(jax.random.fold_in(stream_key, 1), (pairs,), 0, 1 << 20) % (margin + 1)
    sizes = sizes.at[1:1 + 2 * pairs:2].set(giver - shifted).at[2:2 + 2 * pairs:2].set(sink + shifted)
    return sizes[jax.random.permutation(jax.random.fold_in(stream_key, 2), count)]


def routed_block(own_key, own, number, rows, number_of, top, most, lean):
    sequence = jax.random.permutation(own_key, number_of)
    packed, usual = shares(number_of, rows * top, most, lean, True), shares(number_of, rows * top, most, lean, False)
    places = jnp.arange(number_of)

    def named(tallies, rotation):
        used = int((tallies > 0).sum())
        fixed = max(1, used // 4)
        shifted = fixed + (places - fixed + rotation * (used - fixed)) % max(1, number_of - fixed)
        return jnp.zeros((number_of,), jnp.int32).at[sequence[jnp.where(places < fixed, places, shifted)]].set(jnp.asarray(tallies, jnp.int32))

    tallies = jnp.where(number % 4 == 0, named(packed, number // 4), named(usual, number - number // 4 - 1))
    mixed = jax.random.permutation(jax.random.fold_in(own, 3), number_of)
    donor, receiver = mixed[0:number_of // 2 * 2:2], mixed[1:number_of // 2 * 2:2]
    room = jnp.minimum(tallies[donor] - 1, most - tallies[receiver]) // 2
    room = jnp.where((donor == sequence[0]) | (receiver == sequence[0]) | (tallies[receiver] == 0), 0, jnp.maximum(room, 0))
    shifted = jax.random.randint(jax.random.fold_in(own, 4), (number_of // 2,), 0, 1 << 20) % (room + 1)
    tallies = tallies.at[donor].add(-shifted).at[receiver].add(shifted)
    labels = jnp.searchsorted(jnp.cumsum(tallies), jnp.arange(rows * top), side="right").astype(jnp.int32)
    table = labels.reshape(top, rows).T
    table = table[jax.random.permutation(jax.random.fold_in(own, 1), rows)]
    rotation = jax.random.randint(jax.random.fold_in(own, 2), (rows, 1), 0, top)
    return jnp.take_along_axis(table, (jnp.arange(top)[None, :] + rotation) % top, axis=1)


def shares(number_of, total, bound, lean, full):
    portions = [(1 << 20) // math.isqrt(standing ** lean) + 1 for standing in range(1, number_of + 1)]
    largest = bound if full else min(bound, max(-(-total // number_of), total * portions[0] // sum(portions)))
    least = 1 if total - largest >= number_of - 1 else 0
    holding, surplus = [largest] + [least] * (number_of - 1), total - largest - least * (number_of - 1)
    while surplus > 0:
        free = [i for i in range(1, number_of) if holding[i] < largest] or [i for i in range(1, number_of) if holding[i] < bound]
        whole, left = sum([portions[i] for i in free]), surplus
        for i in free:
            extra = min(bound - holding[i], max(1, left * portions[i] // whole), surplus)
            holding[i] = holding[i] + extra
            surplus = surplus - extra
    return np.array(holding)


def centred(key, shape, scale, most, pieces=(), kind=jnp.bfloat16):
    drawn = scale * jax.random.normal(key, shape, jnp.float32)
    if pieces:
        drawn = drawn * level_of(key, shape, pieces, -0.22, 0.18)
    return jnp.clip(drawn, -most, most).astype(kind)


def setup_inputs(seed: int = 0) -> dict:
    key_list = jax.random.split(jax.random.key(seed), 12)
    q_nope = centred(key_list[0], (ROWS, H * NOPE), 1.0, 6.0, ((0, 64), (1, 4)))
    q_rope = draw_q_rope(jax.random.fold_in(key_list[11], 71), 0)
    w_uk = centred(key_list[2], (H, NOPE, KVL), NOPE ** -0.5, 0.5, ((2, 4),))
    w_uv = centred(key_list[3], (H, VDIM, KVL), KVL ** -0.5, 0.25, ((2, 4),))
    prefix_latent = centred(key_list[4], (NPAGES, PAGE, KVL), 1.0, 6.0, ((0, 64),))
    prefix_rope = centred(key_list[5], (NPAGES, PAGE * ROPE), 1.0, 6.0, ((0, 64),))
    suffix_latent = centred(key_list[6], (ROWS, SUF, KVL), 1.0, 6.0, ((0, 64),))
    suffix_rope = draw_suffix_rope(jax.random.fold_in(key_list[11], 71), 0)
    page_slot = jax.random.permutation(key_list[8], NPAGES).astype(jnp.int32)
    page_pattern_keys = jax.random.split(jax.random.fold_in(key_list[9], 1), ROWS // ROWS_DEV)
    page_pattern_turns = jax.random.permutation(jax.random.fold_in(key_list[9], 3), ROWS // ROWS_DEV)
    page_pattern = jax.vmap(lambda own, number: routed_block(jax.random.fold_in(key_list[9], 2), own, number, ROWS_DEV, NPAGES, TOPK, CAP, 2))(page_pattern_keys, page_pattern_turns).reshape((ROWS, TOPK))
    suffix_len = ragged_sizes(key_list[10], ROWS, ROWS * SUF // 2, SUF, 2).astype(jnp.int32)
    return {"q_nope": q_nope, "q_rope": q_rope, "w_uk": w_uk, "w_uv": w_uv, "prefix_latent": prefix_latent, "prefix_rope": prefix_rope, "suffix_latent": suffix_latent, "suffix_rope": suffix_rope, "page_slot": page_slot, "page_pattern": page_pattern, "suffix_len": suffix_len}


def partial_attention(queries, query_rope, latents, rope_keys, visible, score_scale):
    scores = jnp.einsum('bgc,btc->bgt', queries.astype(jnp.float32), latents.astype(jnp.float32))
    scores = scores + jnp.einsum('bge,bte->bgt', query_rope.astype(jnp.float32), rope_keys.astype(jnp.float32))
    scores = scores * score_scale
    scores = jnp.where(visible[:, None, :], scores, jnp.float32(-1e30))
    maxima = jnp.max(scores, axis=2, keepdims=True)
    raw_weights = jnp.exp(scores - maxima)
    totals = jnp.sum(raw_weights, axis=2)
    rounded = raw_weights.astype(jnp.bfloat16)
    summed = jnp.einsum('bgt,btc->bgc', rounded.astype(jnp.float32), latents.astype(jnp.float32))
    result = (summed / totals[:, :, None]).astype(jnp.bfloat16)
    return result, maxima[:, :, 0] + jnp.log(totals)


def combine_blocks(results, log_totals):
    stacked_logs = jnp.stack(log_totals)
    highest = jnp.max(stacked_logs, axis=0)
    factors = jnp.exp(stacked_logs - highest)
    summed = jnp.sum(factors[..., None] * jnp.stack(results).astype(jnp.float32), axis=0)
    return (summed / jnp.sum(factors, axis=0)[..., None]).astype(jnp.bfloat16)


def reference(q_nope, q_rope, w_uk, w_uv, prefix_latent, prefix_rope, suffix_latent, suffix_rope, page_slot, page_pattern, suffix_len):
    score_scale = (NOPE + ROPE) ** -0.5
    page_rope = prefix_rope.reshape(NPAGES, PAGE, ROPE)

    def one_block(block_index):
        start = (block_index * ROWS_DEV).astype(jnp.int32)
        nope_rows = lax.dynamic_slice_in_dim(q_nope, start, ROWS_DEV, 0).reshape(ROWS_DEV, H, NOPE)
        rope_rows = lax.dynamic_slice_in_dim(q_rope, start, ROWS_DEV, 0).reshape(ROWS_DEV, H, ROPE)
        queries = jnp.einsum('rhd,hdc->rhc', nope_rows.astype(jnp.float32), w_uk.astype(jnp.float32)).astype(jnp.bfloat16)
        lengths = lax.dynamic_slice_in_dim(suffix_len, start, ROWS_DEV, 0)
        visible = jnp.arange(SUF, dtype=jnp.int32)[None, :] < lengths[:, None]
        own_latent = lax.dynamic_slice_in_dim(suffix_latent, start, ROWS_DEV, 0)
        own_rope = lax.dynamic_slice_in_dim(suffix_rope, start, ROWS_DEV, 0).reshape(ROWS_DEV, SUF, ROPE)
        result, log_total = partial_attention(queries, rope_rows, own_latent, own_rope, visible, score_scale)
        results = [result]
        log_totals = [log_total]
        pattern_rows = lax.dynamic_slice_in_dim(page_pattern, start, ROWS_DEV, 0)
        chosen_slots = page_slot[pattern_rows]
        everywhere = jnp.ones((ROWS_DEV, PAGE), dtype=bool)
        for column in range(TOPK):
            picked = chosen_slots[:, column]
            result, log_total = partial_attention(queries, rope_rows, prefix_latent[picked], page_rope[picked], everywhere, score_scale)
            results.append(result)
            log_totals.append(log_total)
        mixed = combine_blocks(results, log_totals)
        final = jnp.einsum('rhc,hvc->rhv', mixed.astype(jnp.float32), w_uv.astype(jnp.float32)).astype(jnp.bfloat16)
        return final.reshape(ROWS_DEV, H * VDIM)

    stacked = lax.map(one_block, jnp.arange(ROWS // ROWS_DEV, dtype=jnp.int32))
    return stacked.reshape(ROWS, H * VDIM)
```

```python
import functools

import jax
import jax.numpy as jnp
from jax import lax
from jax.experimental import pallas as pl
from jax.experimental.pallas import tpu as pltpu
from jax.sharding import PartitionSpec as P

F32, BF16, I32 = jnp.float32, jnp.bfloat16, jnp.int32
LOW = -1e30

NZ, NX, NC, NY = 8, 4, 2, 4
HEADS = 16
ROWS = 64
NOPE = 128
VDIM = 128
ROPE = 64
KVL = 512
PAGE = 128
SUF = 64
UNIT = PAGE + PAGE * ROPE // KVL
QN = HEADS * NOPE
QR = HEADS * ROPE
PAY = QN + QR + 128
SLOTS = 256
PAIRS = 16
EARLY = 10
LATE = PAIRS - EARLY
SCALE = (NOPE + ROPE) ** -0.5
OUT = HEADS * VDIM
RET = OUT + 128
LAST = (((1,), (1,)), ((), ()))
FIRST = (((0,), (0,)), ((), ()))


def dot(a, b, dims=(((1,), (0,)), ((), ())), precision=None):
    return lax.dot_general(a, b, dims, preferred_element_type=F32, precision=precision)


def iota(shape, axis):
    return lax.broadcasted_iota(I32, shape, axis)


def params(mib):
    return pltpu.CompilerParams(vmem_limit_bytes=mib << 20)


VMEM = pl.BlockSpec(memory_space=pltpu.VMEM)
SMEM = pl.BlockSpec(memory_space=pltpu.SMEM)
ANY = pl.BlockSpec(memory_space=pl.ANY)


def prep_kernel(
    place, pattern, page_slot, latent, rope, q_nope, q_rope, w_uk, w_uv, pages, pay, ka, kb, va, vb, sems
):
    core, y = place[2], place[3]
    head_a = lax.rem(y + 1 + 2 * core, NY) * HEADS
    head_b = lax.rem(y + 2, NY) * HEADS + (HEADS // 2) * core
    copies = [
        pltpu.make_async_copy(w_uk.at[pl.ds(head_a, HEADS)], ka, sems.at[0]),
        pltpu.make_async_copy(w_uk.at[pl.ds(head_b, HEADS // 2)], kb, sems.at[1]),
        pltpu.make_async_copy(w_uv.at[pl.ds(head_a, HEADS)], va, sems.at[2]),
        pltpu.make_async_copy(w_uv.at[pl.ds(head_b, HEADS // 2)], vb, sems.at[3]),
    ]
    for copy in copies:
        copy.start()
    pages[:, :PAGE, :] = latent[...]
    flat = rope[...].astype(F32)
    half = PAGE // 2
    sub = iota((8, 128), 0)
    even = (iota((half, PAGE), 1) == 2 * iota((half, PAGE), 0)).astype(F32)
    odd = (iota((half, PAGE), 1) == 2 * iota((half, PAGE), 0) + 1).astype(F32)
    for page in range(2):
        tiles = []
        for tile in range(half // 8):
            piece = jnp.zeros((8, 128), F32)
            for row in range(8):
                at = (tile * 8 + row) * 128
                piece = jnp.where(sub == row, flat[page : page + 1, at : at + 128], piece)
            tiles.append(piece)
        two_tokens = jnp.concatenate(tiles, axis=0)
        turned = dot(two_tokens[:, :ROPE], even, FIRST) + dot(two_tokens[:, ROPE:], odd, FIRST)
        turned = jnp.concatenate([turned[16 * i : 16 * i + 16] for i in range(4)], axis=1)
        pages[page, PAGE:, :] = turned.astype(BF16)
    pay[:, :QN] = q_nope[...]
    pay[:, QN : QN + QR] = q_rope[...]
    lane = iota((ROWS, 128), 1)
    slot_row = page_slot[...].astype(F32)
    slots, owners = [], []
    for k in range(2):
        named = lane == pattern[:, k : k + 1]
        slot = jnp.sum(jnp.where(named, slot_row, 0.0), axis=1, keepdims=True)
        slots.append(slot)
        owners.append((lane == lax.shift_right_logical(slot.astype(I32), 1)).astype(F32))
    below = (iota((ROWS, ROWS), 0) > iota((ROWS, ROWS), 1)).astype(F32)
    before0 = dot(below, owners[0])
    before1 = dot(below, owners[1]) + jnp.sum(owners[0], axis=0, keepdims=True)
    rank0 = jnp.sum(owners[0] * before0, axis=1, keepdims=True)
    rank1 = jnp.sum(owners[1] * before1, axis=1, keepdims=True)
    code = jnp.zeros((ROWS, 128), F32)
    for at, value in enumerate((slots[0], slots[1], rank0, rank1)):
        code = jnp.where(lane == at, value, code)
    pay[:, QN + QR :] = code.astype(BF16)
    for copy in copies:
        copy.wait()


def gather_weights(place, full, a, a_swap, b, b_swap, whole, sems):
    core, y = place[2], place[3]

    def lanes(which):
        return pl.ds(pl.multiple_of(lax.rem(which, NY) * 128, 128), 128)

    half = HEADS // 2
    copies = [
        pltpu.make_async_copy(full.at[pl.ds(y * HEADS, HEADS)], whole.at[:, :, lanes(y)], sems.at[0]),
        pltpu.make_async_copy(a, whole.at[:, :, lanes(y + 3 - 2 * core)], sems.at[1]),
        pltpu.make_async_copy(a_swap, whole.at[:, :, lanes(y + 1 + 2 * core)], sems.at[2]),
        pltpu.make_async_copy(b, whole.at[pl.ds(half * core, half), :, lanes(y + 2)], sems.at[3]),
        pltpu.make_async_copy(b_swap, whole.at[pl.ds(half * (1 - core), half), :, lanes(y + 2)], sems.at[4]),
    ]
    for copy in copies:
        copy.start()
    return copies


def query_kernel(
    place, p0, p1, p2, p3, w_uk, ka, ka_swap, kb, kb_swap, q_lat, q_rot, own_lat, own_rot, page_bit, slot_of, whole, turned, sems
):
    copies = gather_weights(place, w_uk, ka, ka_swap, kb, kb_swap, whole, sems)
    z, x, core = place[0], place[1], place[2]
    pays = (p0, p1, p2, p3)
    lane = iota((ROWS, 128), 1)
    wide = iota((ROWS, SLOTS), 1)
    picks, bits, places = ([], []), ([], []), []
    for peer, pay in enumerate(pays):
        code = pay[:, QN + QR :].astype(F32)
        columns = [
            jnp.sum(jnp.where(lane == at, code, 0.0), axis=1, keepdims=True).astype(I32) for at in range(4)
        ]
        noted = jnp.zeros((ROWS, 128), F32)
        for k in range(2):
            slot, rank = columns[k], columns[2 + k]
            away = (z - lax.shift_right_logical(slot, 4)) * (1 - 2 * core)
            away = lax.bitwise_and(away, NZ - 1)
            order = jnp.where(away < 3, away, jnp.where(away >= 6, away - 3, away + 2))
            other = jnp.where(lax.bitwise_and(lax.shift_right_logical(slot, 1), 1) != core, 1, 0)
            here = lax.bitwise_and(lax.shift_right_logical(slot, 2), 3) == x
            at = jnp.where(here, (order * 2 + other) * 16 + peer * 4 + rank, -1)
            picks[k].append((wide == at).astype(F32))
            bits[k].append(lax.bitwise_and(slot, 1).astype(F32) * jnp.ones((1, 128), F32))
            noted = jnp.where(lane == k, at.astype(F32), noted)
        slot_of[peer * ROWS : (peer + 1) * ROWS, :] = noted
    pick = [jnp.concatenate(p, axis=0) for p in picks]
    bit = [jnp.concatenate(b, axis=0) for b in bits]
    page_bit[...] = dot(pick[0], bit[0], FIRST) + dot(pick[1], bit[1], FIRST)
    turned[...] = jnp.transpose(pick[0] + pick[1]).astype(BF16)
    for copy in copies:
        copy.wait()

    def two_heads(i, carry):
        rot = pl.ds(pl.multiple_of(QN + i * 128, 128), 128)
        gathered = dot(turned[...], jnp.concatenate([p[:, rot] for p in pays], axis=0))
        mine = p0[:, rot].astype(F32)
        for k in range(2):
            head = 2 * i + k
            q_rot[head] = gathered[:, k * ROPE : (k + 1) * ROPE].astype(BF16)
            own_rot[head] = mine[:, k * ROPE : (k + 1) * ROPE]
            at = pl.ds(pl.multiple_of(head * NOPE, 128), NOPE)
            left = dot(turned[...], jnp.concatenate([p[:, at] for p in pays], axis=0)).astype(BF16)
            left = jnp.concatenate([left, p0[:, at]], axis=0)
            latent = dot(left, whole[head]).astype(BF16)
            q_lat[head] = latent[:SLOTS]
            own_lat[head] = latent[SLOTS:].astype(F32)
        return carry

    lax.fori_loop(0, HEADS // 2, two_heads, 0)


def start_units(units, held, sems):
    copies = [pltpu.make_async_copy(unit, held.at[i], sems.at[i]) for i, unit in enumerate(units)]
    for copy in copies:
        copy.start()


def attend_units(count, base, unit0, q_lat, q_rot, page_bit, held, sems, result, logs):
    lane = iota((16, 128), 1)

    def body(i, carry):
        pltpu.make_async_copy(unit0, held.at[i], sems.at[i]).wait()
        unit = held.at[i]
        latent = unit[:, :PAGE, :].reshape(2 * PAGE, KVL)
        rot = unit[:, PAGE:, :]
        keys = jnp.concatenate(
            [
                jnp.concatenate([rot[page, :, 128 * j : 128 * j + 128] for j in range(4)], axis=0)
                for page in range(2)
            ],
            axis=1,
        )
        at = pl.ds(pl.multiple_of((base + i) * 16, 16), 16)
        query = q_lat[:, at, :].reshape(HEADS * 16, KVL)
        query_rot = q_rot[:, at, :].reshape(HEADS * 16, ROPE)
        scores = dot(query, latent, LAST) + dot(query_rot, keys)
        bit = page_bit[at, :]
        bias = jnp.concatenate(
            [jnp.where(bit < 0.5, 0.0, LOW), jnp.where(bit < 0.5, LOW, 0.0)], axis=1
        )
        scores = (scores * SCALE).reshape(HEADS, 16, 2 * PAGE) + bias[None]
        scores = scores.reshape(HEADS * 16, 2 * PAGE)
        top = jnp.max(scores, axis=1, keepdims=True)
        raw = jnp.exp(scores - top)
        total = jnp.sum(raw, axis=1, keepdims=True)
        summed = dot(raw.astype(BF16), latent) * (1.0 / total)
        out_at = pl.ds(pl.multiple_of(i * 16, 16), 16)
        result[:, out_at, :] = summed.astype(BF16).reshape(HEADS, 16, KVL)
        log = (top + jnp.log(total)).reshape(HEADS, 16, 1)
        spread = jnp.zeros((16, 128), F32)
        for head in range(HEADS):
            mine = (lax.bitwise_and(lane, 15) == head) & (lane < 48)
            spread = jnp.where(mine, log[head], spread)
        logs[out_at, :] = spread
        return carry

    lax.fori_loop(0, count, body, 0)


def early_kernel(*refs):
    units = refs[:EARLY]
    q_lat, q_rot, page_bit, result, logs, held, sems = refs[EARLY:]
    start_units(units, held, sems)
    attend_units(EARLY, 0, units[0], q_lat, q_rot, page_bit, held, sems, result, logs)


def late_kernel(*refs):
    units = refs[:LATE]
    (
        place, q_lat, q_rot, page_bit, slot_of, early, early_logs, w_uv, va, va_swap, vb, vb_swap,
        r0, r1, r2, r3, held, result, logs, whole, parts, sems, w_sems,
    ) = refs[LATE:]
    start_units(units, held, sems)
    copies = gather_weights(place, w_uv, va, va_swap, vb, vb_swap, whole, w_sems)
    attend_units(LATE, EARLY, units[0], q_lat, q_rot, page_bit, held, sems, result, logs)
    highest = lax.Precision.HIGHEST
    wide = iota((SLOTS, SLOTS), 1).astype(F32)
    at0, at1 = slot_of[:, 0:1], slot_of[:, 1:2]
    pick0, pick1 = (wide == at0).astype(F32), (wide == at1).astype(F32)
    partner = dot(pick0, pick1, FIRST) + dot(pick1, pick0, FIRST)
    has = jnp.sum(partner, axis=1, keepdims=True)
    log = jnp.concatenate([early_logs[...], logs[...]], axis=0)
    other = dot(partner, log, precision=highest) + (has - 1.0) * (-LOW)
    top = jnp.maximum(log, other)
    mine = jnp.exp(log - top)
    both = mine + jnp.exp(other - top)
    weight = mine / both
    merged = top + jnp.log(both)
    for copy in copies:
        copy.wait()
    for head in range(HEADS):
        mixed = jnp.concatenate([early[head], result[head]], axis=0)
        part = dot(mixed, whole[head], LAST) * weight[:, head : head + 1]
        parts[:, head * VDIM : (head + 1) * VDIM] = part.astype(BF16)
    first = jnp.where(at0 >= 0.0, 1.0, 0.0)
    row_log = dot(pick0 + pick1 * (1.0 - first), merged, precision=highest)
    none = (at0 < 0.0) & (at1 < 0.0)
    row_log = jnp.where(none, LOW, row_log)
    lane = iota((SLOTS, 128), 1)
    high = row_log.astype(BF16).astype(F32)
    rest = row_log - high
    middle = rest.astype(BF16).astype(F32)
    packed = jnp.where(lane < 16, high, jnp.where(lane < 32, middle, rest - middle))
    packed = jnp.where(lane < 48, packed, 0.0).astype(BF16)
    pick = (pick0 + pick1).astype(BF16)
    for peer, out in enumerate((r0, r1, r2, r3)):
        rows = slice(peer * ROWS, (peer + 1) * ROWS)
        out[:, :OUT] = dot(pick[rows], parts[...]).astype(BF16)
        out[:, OUT:] = packed[rows]


def suffix_kernel(
    place, own_lat, own_rot, latent, rope, live, w_uv, va, va_swap, vb, vb_swap, out, out_logs, rope32, result, whole, sems
):
    copies = gather_weights(place, w_uv, va, va_swap, vb, vb_swap, whole, sems)
    rope32[...] = rope[...].astype(F32)
    keys, pairs = 8 * SUF, 8 * SUF // 2
    key, pair = iota((keys, pairs), 0), iota((keys, pairs), 1)
    same = lax.shift_right_logical(key, 6) == lax.bitwise_and(pair, 7)
    first = 2 * lax.shift_right_logical(pair, 3)
    even = (same & (lax.bitwise_and(key, SUF - 1) == first)).astype(BF16)
    odd = (same & (lax.bitwise_and(key, SUF - 1) == first + 1)).astype(BF16)
    lane = iota((8, 128), 1)
    col, row = iota((8, keys), 1), iota((8, keys), 0)

    def body(i, carry):
        rows = pl.ds(pl.multiple_of(i * 8, 8), 8)
        query = own_lat[:, rows, :].reshape(HEADS * 8, KVL).astype(BF16)
        query_rot = own_rot[:, rows, :].reshape(HEADS * 8, ROPE).astype(BF16)
        lat = latent[rows].reshape(keys, KVL)
        rot = rope32[rows, :]
        rot = jnp.concatenate([rot[:, 128 * j : 128 * j + 128] for j in range(SUF // 2)], axis=0).astype(BF16)
        rot_keys = (dot(even, rot[:, :ROPE]) + dot(odd, rot[:, ROPE:])).astype(BF16)
        scores = dot(query, lat, LAST) + dot(query_rot, rot_keys, LAST)
        seen = (lax.shift_right_logical(col, 6) == row) & (lax.bitwise_and(col, SUF - 1) < live[rows, :])
        bias = jnp.where(seen, 0.0, LOW)
        scores = ((scores * SCALE).reshape(HEADS, 8, keys) + bias[None]).reshape(HEADS * 8, keys)
        top = jnp.max(scores, axis=1, keepdims=True)
        raw = jnp.exp(scores - top)
        total = jnp.sum(raw, axis=1, keepdims=True)
        summed = dot(raw.astype(BF16), lat) * (1.0 / total)
        result[:, rows, :] = summed.reshape(HEADS, 8, KVL)
        log = (top + jnp.log(total)).reshape(HEADS, 8, 1)
        spread = jnp.zeros((8, 128), F32)
        for head in range(HEADS):
            spread = jnp.where(lane == head, log[head], spread)
        out_logs[rows, :] = spread
        return carry

    lax.fori_loop(0, ROWS // 8, body, 0)
    for copy in copies:
        copy.wait()
    for head in range(HEADS):
        out[:, head * VDIM : (head + 1) * VDIM] = dot(result[head].astype(BF16), whole[head], LAST)


def final_kernel(own, own_logs, r0, r1, r2, r3, out):
    gather = (
        (lax.bitwise_and(iota((128, 128), 0), 15) == iota((128, 128), 1)) & (iota((128, 128), 0) < 48)
    ).astype(BF16)
    logs = [own_logs[...]] + [dot(r[:, OUT:], gather) for r in (r0, r1, r2, r3)]
    top = functools.reduce(jnp.maximum, logs)
    weights = [jnp.exp(log - top) for log in logs]
    total = 1.0 / functools.reduce(jnp.add, weights)
    weights = [w * total for w in weights]
    for head in range(HEADS):
        at = slice(head * VDIM, (head + 1) * VDIM)
        mixed = own[:, at] * weights[0][:, head : head + 1]
        for part, weight in zip((r0, r1, r2, r3), weights[1:]):
            mixed = mixed + part[:, at].astype(F32) * weight[:, head : head + 1]
        out[:, at] = mixed.astype(BF16)


def row_of(z, x, c):
    return ((z % NZ) * NX + x % NX) * NC + c


CHIPS = [(z, x, c) for z in range(NZ) for x in range(NX) for c in range(NC)]


def ring_z(a):
    return lax.ppermute(a, "rows", [(row_of(z, x, c), row_of(z + 1 - 2 * c, x, c)) for z, x, c in CHIPS])


def shift_x(a, by):
    return lax.ppermute(a, "rows", [(row_of(z, x, c), row_of(z, x + by, c)) for z, x, c in CHIPS])


def swap(a):
    return lax.ppermute(a, "rows", [(row_of(z, x, c), row_of(z, x, 1 - c)) for z, x, c in CHIPS])


def move_y(a, by):
    pairs = []
    for z, x, c in CHIPS:
        r = row_of(z, x, c)
        pairs += [(r * NY + y, r * NY + (y + by[c]) % NY) for y in range(NY)]
    return lax.ppermute(a, ("rows", "proj"), pairs)


def cost(us):
    return pl.CostEstimate(flops=int(us * 1e6), bytes_accessed=int(us * 3.0e6), transcendentals=0)


def struct(*shape, dtype=BF16):
    return jax.ShapeDtypeStruct(shape, dtype)


def shards(
    q_nope, q_rope, w_uk, w_uv, prefix_latent, prefix_rope, suffix_latent, suffix_rope, page_slot, page_pattern, suffix_len
):
    row, y = lax.axis_index("rows"), lax.axis_index("proj")
    place = jnp.stack([row // (NX * NC), row // NC % NX, row % NC, y]).astype(I32)
    half = HEADS // 2
    pages, pay, ka, kb, va, vb = pl.pallas_call(
        prep_kernel,
        out_shape=(
            struct(2, UNIT, KVL), struct(ROWS, PAY),
            struct(HEADS, NOPE, 128), struct(half, NOPE, 128), struct(HEADS, VDIM, 128), struct(half, VDIM, 128),
        ),
        in_specs=[SMEM] + [VMEM] * 6 + [ANY] * 2,
        out_specs=(VMEM, VMEM, ANY, ANY, ANY, ANY),
        scratch_shapes=[pltpu.SemaphoreType.DMA((4,))],
        compiler_params=params(16),
        cost_estimate=cost(2),
        name="prep",
    )(place, page_pattern, page_slot.reshape(1, -1), prefix_latent, prefix_rope, q_nope, q_rope, w_uk, w_uv)

    a, b = [pages], [swap(pages)]
    pays = [pay] + [shift_x(pay, by) for by in (1, 2, 3)]
    for step in range(1, 5):
        a.append(ring_z(a[-1]))
        if step < 4:
            b.append(ring_z(b[-1]))
    ka_y, kb_y = move_y(ka, (1, -1)), move_y(kb, (2, 2))
    va_y, vb_y = move_y(va, (1, -1)), move_y(vb, (2, 2))
    k_parts = (ka_y, swap(ka_y), kb_y, swap(kb_y))
    v_parts = (va_y, swap(va_y), vb_y, swap(vb_y))
    a_swap = [None] + [swap(u) for u in a[1:]]
    b_swap = [None] + [swap(u) for u in b[1:]]
    early_units = [a[0], b[0], a[1], b[1], a[2], b[2], b_swap[2], a_swap[2], b_swap[1], a_swap[1]]
    late_units = [a[3], b[3], a[4], a_swap[4], b_swap[3], a_swap[3]]

    q_lat, q_rot, own_lat, own_rot, page_bit, slot_of = pl.pallas_call(
        query_kernel,
        out_shape=(
            struct(HEADS, SLOTS, KVL), struct(HEADS, SLOTS, ROPE),
            struct(HEADS, ROWS, KVL, dtype=F32), struct(HEADS, ROWS, ROPE, dtype=F32),
            struct(SLOTS, 128, dtype=F32), struct(4 * ROWS, 128, dtype=F32),
        ),
        in_specs=[SMEM] + [VMEM] * 4 + [ANY] * 5,
        out_specs=(VMEM,) * 6,
        scratch_shapes=[
            pltpu.VMEM((HEADS, NOPE, KVL), BF16), pltpu.VMEM((SLOTS, 4 * ROWS), BF16), pltpu.SemaphoreType.DMA((5,)),
        ],
        compiler_params=params(32),
        cost_estimate=cost(4),
        name="queries",
    )(place, *pays, w_uk, *k_parts)

    early, early_logs = pl.pallas_call(
        early_kernel,
        out_shape=(struct(HEADS, EARLY * 16, KVL), struct(EARLY * 16, 128, dtype=F32)),
        in_specs=[ANY] * EARLY + [VMEM] * 3,
        out_specs=(VMEM, VMEM),
        scratch_shapes=[pltpu.VMEM((EARLY, 2, UNIT, KVL), BF16), pltpu.SemaphoreType.DMA((EARLY,))],
        compiler_params=params(32),
        cost_estimate=cost(6),
        name="early_pages",
    )(*early_units, q_lat, q_rot, page_bit)

    returns = pl.pallas_call(
        late_kernel,
        out_shape=(struct(ROWS, RET),) * 4,
        in_specs=[ANY] * LATE + [SMEM] + [VMEM] * 6 + [ANY] * 5,
        out_specs=(VMEM,) * 4,
        scratch_shapes=[
            pltpu.VMEM((LATE, 2, UNIT, KVL), BF16), pltpu.VMEM((HEADS, LATE * 16, KVL), BF16),
            pltpu.VMEM((LATE * 16, 128), F32), pltpu.VMEM((HEADS, VDIM, KVL), BF16), pltpu.VMEM((SLOTS, OUT), BF16),
            pltpu.SemaphoreType.DMA((LATE,)), pltpu.SemaphoreType.DMA((5,)),
        ],
        compiler_params=params(32),
        cost_estimate=cost(7),
        name="late_pages",
    )(*late_units, place, q_lat, q_rot, page_bit, slot_of, early, early_logs, w_uv, *v_parts)

    backs = [returns[0]] + [shift_x(returns[by], -by) for by in (1, 2, 3)]
    own_lat, returns = lax.optimization_barrier((own_lat, returns))
    own, own_logs = pl.pallas_call(
        suffix_kernel,
        out_shape=(struct(ROWS, OUT, dtype=F32), struct(ROWS, 128, dtype=F32)),
        in_specs=[SMEM] + [VMEM] * 5 + [ANY] * 5,
        out_specs=(VMEM, VMEM),
        scratch_shapes=[
            pltpu.VMEM((ROWS, SUF * ROPE), F32), pltpu.VMEM((HEADS, ROWS, KVL), F32),
            pltpu.VMEM((HEADS, VDIM, KVL), BF16), pltpu.SemaphoreType.DMA((5,)),
        ],
        compiler_params=params(32),
        cost_estimate=cost(8),
        name="suffix",
    )(place, own_lat, own_rot, suffix_latent, suffix_rope, suffix_len.reshape(-1, 1), w_uv, *v_parts)

    return pl.pallas_call(
        final_kernel,
        out_shape=struct(ROWS, OUT),
        in_specs=[VMEM] * 6,
        out_specs=VMEM,
        compiler_params=params(16),
        cost_estimate=cost(2),
        name="combine",
    )(own, own_logs, *backs)


def solution(mesh):
    return jax.shard_map(
        shards,
        mesh=mesh,
        in_specs=(
            P("rows", "proj"), P("rows", "proj"), P(None, None, "proj"), P(None, None, "proj"),
            P("rows", None, None), P("rows", None), P("rows", None, None), P("rows", None),
            P(), P("rows", None), P("rows"),
        ),
        out_specs=P("rows", "proj"),
        check_vma=False,
    )
```

```python
import functools

import jax
import jax.numpy as jnp
from jax import lax
from jax.experimental import pallas as pl
from jax.experimental.pallas import tpu as pltpu
from jax.sharding import PartitionSpec as P

F32, BF16, I32 = jnp.float32, jnp.bfloat16, jnp.int32
LOW = -1e30

NZ, NX, NC, NY = 8, 4, 2, 4
HEADS = 16
ROWS = 64
NOPE = 128
VDIM = 128
ROPE = 64
KVL = 512
PAGE = 128
SUF = 64
UNIT = PAGE + PAGE * ROPE // KVL
QN = HEADS * NOPE
QR = HEADS * ROPE
PAY = QN + QR + 128
SLOTS = 256
PAIRS = 16
EARLY = 10
LATE = PAIRS - EARLY
SCALE = (NOPE + ROPE) ** -0.5
OUT = HEADS * VDIM
RET = OUT + 128
LOG2E = 1.4426950408889634
LAST = (((1,), (1,)), ((), ()))
FIRST = (((0,), (0,)), ((), ()))


def dot(a, b, dims=(((1,), (0,)), ((), ())), precision=None):
    return lax.dot_general(a, b, dims, preferred_element_type=F32, precision=precision)


def iota(shape, axis):
    return lax.broadcasted_iota(I32, shape, axis)


def params(mib):
    return pltpu.CompilerParams(vmem_limit_bytes=mib << 20)


VMEM = pl.BlockSpec(memory_space=pltpu.VMEM)
SMEM = pl.BlockSpec(memory_space=pltpu.SMEM)
ANY = pl.BlockSpec(memory_space=pl.ANY)
HBM = pl.BlockSpec(memory_space=pltpu.HBM)


def load_all(pairs, sems):
    copies = [pltpu.make_async_copy(src, dst, sems.at[i]) for i, (src, dst) in enumerate(pairs)]
    for copy in copies:
        copy.start()
    return copies


def pack_kernel(pattern, page_slot, rope_in, latent_in, q_nope, q_rope, pages, pay, rope, sems):
    copies = load_all(
        [
            (rope_in, rope),
            (latent_in, pages.at[:, :PAGE, :]),
            (q_nope, pay.at[:, :QN]),
            (q_rope, pay.at[:, QN : QN + QR]),
        ],
        sems,
    )
    copies[0].wait()
    flat = rope[...].astype(F32)
    half = PAGE // 2
    sub = iota((8, 128), 0)
    even = (iota((half, PAGE), 1) == 2 * iota((half, PAGE), 0)).astype(F32)
    odd = (iota((half, PAGE), 1) == 2 * iota((half, PAGE), 0) + 1).astype(F32)
    for page in range(2):
        tiles = []
        for tile in range(half // 8):
            piece = jnp.zeros((8, 128), F32)
            for row in range(8):
                at = (tile * 8 + row) * 128
                piece = jnp.where(sub == row, flat[page : page + 1, at : at + 128], piece)
            tiles.append(piece)
        two_tokens = jnp.concatenate(tiles, axis=0)
        turned = dot(two_tokens[:, :ROPE], even, FIRST) + dot(two_tokens[:, ROPE:], odd, FIRST)
        turned = jnp.concatenate([turned[16 * i : 16 * i + 16] for i in range(4)], axis=1)
        pages[page, PAGE:, :] = turned.astype(BF16)
    lane = iota((ROWS, 128), 1)
    across = iota((ROWS, ROWS), 0) == iota((ROWS, ROWS), 1)
    slot_row = page_slot[...].astype(F32)
    slots, owners = [], []
    for k in range(2):
        names = pattern[k : k + 1, :].astype(F32)
        names = jnp.sum(jnp.where(across, names, 0.0), axis=1, keepdims=True).astype(I32)
        named = lane == names
        slot = jnp.sum(jnp.where(named, slot_row, 0.0), axis=1, keepdims=True)
        slots.append(slot)
        owners.append((lane == lax.shift_right_logical(slot.astype(I32), 1)).astype(F32))
    below = (iota((ROWS, ROWS), 0) > iota((ROWS, ROWS), 1)).astype(F32)
    before0 = dot(below, owners[0])
    before1 = dot(below, owners[1]) + jnp.sum(owners[0], axis=0, keepdims=True)
    rank0 = jnp.sum(owners[0] * before0, axis=1, keepdims=True)
    rank1 = jnp.sum(owners[1] * before1, axis=1, keepdims=True)
    code = jnp.zeros((ROWS, 128), F32)
    for at, value in enumerate((slots[0], slots[1], rank0, rank1)):
        code = jnp.where(lane == at, value, code)
    pay[:, QN + QR :] = code.astype(BF16)
    for copy in copies[1:]:
        copy.wait()


def gather_weights(place, both, half_swap, second, whole, sems):
    core, heads = place[2], HEADS // 2
    pairs = []
    for which, part in ((core, both), (1 - core, half_swap)):
        for y in range(NY):
            to = whole.at[pl.ds(which * heads, heads), :, y * 128 : (y + 1) * 128]
            at = (2 * y + second) * heads if part is both else y * heads
            pairs.append((part.at[pl.ds(at, heads)], to))
    return load_all(pairs, sems)


def query_kernel(
    place, p0_in, p1_in, p2_in, p3_in, both, k_swap, q_lat, q_rot, page_bit, slot_of,
    p0, p1, p2, p3, whole, turned, p_sems, sems,
):
    p_copies = load_all(list(zip((p0_in, p1_in, p2_in, p3_in), (p0, p1, p2, p3))), p_sems)
    copies = gather_weights(place, both, k_swap, 0, whole, sems)
    for copy in p_copies:
        copy.wait()
    z, x, core = place[0], place[1], place[2]
    pays = (p0, p1, p2, p3)
    lane = iota((ROWS, 128), 1)
    wide = iota((ROWS, SLOTS), 1)
    picks, bits, places = ([], []), ([], []), []
    for peer, part in enumerate(pays):
        code = part[:, QN + QR :].astype(F32)
        columns = [
            jnp.sum(jnp.where(lane == at, code, 0.0), axis=1, keepdims=True).astype(I32) for at in range(4)
        ]
        noted = jnp.zeros((ROWS, 128), F32)
        for k in range(2):
            slot, rank = columns[k], columns[2 + k]
            away = (z - lax.shift_right_logical(slot, 4)) * (1 - 2 * core)
            away = lax.bitwise_and(away, NZ - 1)
            order = jnp.where(away < 3, away, jnp.where(away >= 6, away - 3, away + 2))
            other = jnp.where(lax.bitwise_and(lax.shift_right_logical(slot, 1), 1) != core, 1, 0)
            here = lax.bitwise_and(lax.shift_right_logical(slot, 2), 3) == x
            at = jnp.where(here, (order * 2 + other) * 16 + peer * 4 + rank, -1)
            picks[k].append((wide == at).astype(F32))
            bits[k].append(lax.bitwise_and(slot, 1).astype(F32) * jnp.ones((1, 128), F32))
            noted = jnp.where(lane == k, at.astype(F32), noted)
        slot_of[peer * ROWS : (peer + 1) * ROWS, :] = noted
    pick = [jnp.concatenate(p, axis=0) for p in picks]
    bit = [jnp.concatenate(b, axis=0) for b in bits]
    page_bit[...] = dot(pick[0], bit[0], FIRST) + dot(pick[1], bit[1], FIRST)
    turned[...] = jnp.transpose(pick[0] + pick[1]).astype(BF16)
    for copy in copies:
        copy.wait()

    def two_heads(i, carry):
        rot = pl.ds(pl.multiple_of(QN + i * 128, 128), 128)
        gathered = dot(turned[...], jnp.concatenate([p[:, rot] for p in pays], axis=0)).astype(BF16)
        at = pl.ds(pl.multiple_of(i * 2 * NOPE, 128), 2 * NOPE)
        left = dot(turned[...], jnp.concatenate([p[:, at] for p in pays], axis=0)).astype(BF16)
        for k in range(2):
            q_rot[2 * i + k] = gathered[:, k * ROPE : (k + 1) * ROPE]
            q_lat[2 * i + k] = dot(left[:, k * NOPE : (k + 1) * NOPE], whole[2 * i + k]).astype(BF16)
        return carry

    lax.fori_loop(0, HEADS // 2, two_heads, 0)


def start_units(units, held, sems):
    copies = [pltpu.make_async_copy(unit, held.at[i], sems.at[i]) for i, unit in enumerate(units)]
    for copy in copies:
        copy.start()


def attend_units(count, base, unit0, q_lat, q_rot, page_bit, held, sems, result, logs):
    lane = iota((16, 128), 1)

    def block(i):
        unit = held.at[i]
        latent = unit[:, :PAGE, :].reshape(2 * PAGE, KVL)
        rot = unit[:, PAGE:, :]
        keys = jnp.concatenate(
            [
                jnp.concatenate([rot[page, :, 128 * j : 128 * j + 128] for j in range(4)], axis=0)
                for page in range(2)
            ],
            axis=1,
        )
        at = pl.ds(pl.multiple_of((base + i) * 16, 16), 16)
        query = q_lat[:, at, :].reshape(HEADS * 16, KVL)
        query_rot = q_rot[:, at, :].reshape(HEADS * 16, ROPE)
        scores = dot(query, latent, LAST) + dot(query_rot, keys)
        bit = page_bit[at, :]
        bias = jnp.concatenate(
            [jnp.where(bit < 0.5, 0.0, LOW), jnp.where(bit < 0.5, LOW, 0.0)], axis=1
        )
        scores = (scores.reshape(HEADS, 16, 2 * PAGE) + bias[None]).reshape(HEADS * 16, 2 * PAGE)
        top = jnp.max(scores, axis=1, keepdims=True)
        raw = jnp.exp2((scores - top) * (SCALE * LOG2E))
        total = jnp.sum(raw, axis=1, keepdims=True)
        summed = dot(raw.astype(BF16), latent) * (1.0 / total)
        out_at = pl.ds(pl.multiple_of(i * 16, 16), 16)
        result[:, out_at, :] = summed.astype(BF16).reshape(HEADS, 16, KVL)
        log = (top * SCALE + jnp.log(total)).reshape(HEADS, 16, 1)
        spread = jnp.zeros((16, 128), F32)
        for head in range(HEADS):
            mine = (lax.bitwise_and(lane, 15) == head) & (lane < 48)
            spread = jnp.where(mine, log[head], spread)
        logs[out_at, :] = spread

    def body(i, carry):
        for k in range(2):
            pltpu.make_async_copy(unit0, held.at[2 * i + k], sems.at[2 * i + k]).wait()
        for k in range(2):
            block(2 * i + k)
        return carry

    lax.fori_loop(0, count // 2, body, 0)


def early_kernel(*refs):
    units = refs[:EARLY]
    q_lat, q_rot, page_bit, result, logs, held, sems = refs[EARLY:]
    start_units(units, held, sems)
    attend_units(EARLY, 0, units[0], q_lat, q_rot, page_bit, held, sems, result, logs)


def pack_log(log):
    lane = iota(log.shape, 1)
    high = log.astype(BF16).astype(F32)
    rest = log - high
    middle = rest.astype(BF16).astype(F32)
    packed = jnp.where(lane < 16, high, jnp.where(lane < 32, middle, rest - middle))
    return jnp.where(lane < 48, packed, 0.0).astype(BF16)


def late_kernel(*refs):
    units = refs[:LATE]
    (
        place, q_lat, q_rot, page_bit, slot_of, early, early_logs, weights, v_swap,
        r0, r1, r2, r3, held, result, logs, whole, parts, sems, w_sems,
    ) = refs[LATE:]
    start_units(units, held, sems)
    copies = gather_weights(place, weights, v_swap, 1, whole, w_sems)
    attend_units(LATE, EARLY, units[0], q_lat, q_rot, page_bit, held, sems, result, logs)
    highest = lax.Precision.HIGHEST
    wide = iota((SLOTS, SLOTS), 1).astype(F32)
    at0, at1 = slot_of[:, 0:1], slot_of[:, 1:2]
    pick0, pick1 = (wide == at0).astype(F32), (wide == at1).astype(F32)
    partner = dot(pick0, pick1, FIRST) + dot(pick1, pick0, FIRST)
    has = jnp.sum(partner, axis=1, keepdims=True)
    log = jnp.concatenate([early_logs[...], logs[...]], axis=0)
    other = dot(partner, log, precision=highest) + (has - 1.0) * (-LOW)
    top = jnp.maximum(log, other)
    mine = jnp.exp(log - top)
    both = mine + jnp.exp(other - top)
    weight = mine / both
    merged = top + jnp.log(both)
    for copy in copies:
        copy.wait()
    for head in range(HEADS):
        mixed = jnp.concatenate([early[head], result[head]], axis=0)
        part = dot(mixed, whole[head], LAST) * weight[:, head : head + 1]
        parts[:, head * VDIM : (head + 1) * VDIM] = part.astype(BF16)
    first = jnp.where(at0 >= 0.0, 1.0, 0.0)
    row_log = dot(pick0 + pick1 * (1.0 - first), merged, precision=highest)
    none = (at0 < 0.0) & (at1 < 0.0)
    row_log = jnp.where(none, LOW, row_log)
    packed = pack_log(row_log)
    pick = (pick0 + pick1).astype(BF16)
    for peer, out in enumerate((r0, r1, r2, r3)):
        rows = slice(peer * ROWS, (peer + 1) * ROWS)
        out[:, :OUT] = dot(pick[rows], parts[...]).astype(BF16)
        out[:, OUT:] = packed[rows]


def suffix_kernel(
    place, live, q_nope_in, q_rope_in, latent_in, rope_in, both, k_swap, v_swap,
    out, q_nope, q_rope, latent, rope, rope32, query32, rot32, result, logs, whole_k, whole_v,
    k_sems, v_sems, q_sems, lat_sems,
):
    q_copies = load_all([(q_nope_in, q_nope), (q_rope_in, q_rope), (rope_in, rope)], q_sems)
    k_copies = gather_weights(place, both, k_swap, 0, whole_k, k_sems)
    for i in range(ROWS // 8):
        pltpu.make_async_copy(latent_in.at[pl.ds(8 * i, 8)], latent.at[pl.ds(8 * i, 8)], lat_sems.at[i]).start()
    v_copies = gather_weights(place, both, v_swap, 1, whole_v, v_sems)
    for copy in q_copies:
        copy.wait()
    rope32[...] = rope[...].astype(F32)
    across = iota((ROWS, ROWS), 0) == iota((ROWS, ROWS), 1)
    length = jnp.sum(jnp.where(across, live[...].astype(F32), 0.0), axis=1, keepdims=True)
    for copy in k_copies:
        copy.wait()
    for head in range(HEADS):
        projected = dot(q_nope[:, head * NOPE : (head + 1) * NOPE], whole_k[head])
        query32[head] = projected.astype(BF16).astype(F32)
        rot32[head] = q_rope[:, head * ROPE : (head + 1) * ROPE].astype(F32)
    keys, pairs = 8 * SUF, 8 * SUF // 2
    key, pair = iota((keys, pairs), 0), iota((keys, pairs), 1)
    same = lax.shift_right_logical(key, 6) == lax.bitwise_and(pair, 7)
    first = 2 * lax.shift_right_logical(pair, 3)
    even = (same & (lax.bitwise_and(key, SUF - 1) == first)).astype(BF16)
    odd = (same & (lax.bitwise_and(key, SUF - 1) == first + 1)).astype(BF16)
    lane = iota((8, 128), 1)
    col, row = iota((8, keys), 1), iota((8, keys), 0)

    def block(i, live_rows):
        rows = pl.ds(pl.multiple_of(i * 8, 8), 8)
        query = query32[:, rows, :].reshape(HEADS * 8, KVL).astype(BF16)
        query_rot = rot32[:, rows, :].reshape(HEADS * 8, ROPE).astype(BF16)
        lat = latent[rows].reshape(keys, KVL)
        rot = rope32[rows, :]
        rot = jnp.concatenate([rot[:, 128 * j : 128 * j + 128] for j in range(SUF // 2)], axis=0).astype(BF16)
        rot_keys = (dot(even, rot[:, :ROPE]) + dot(odd, rot[:, ROPE:])).astype(BF16)
        scores = dot(query, lat, LAST) + dot(query_rot, rot_keys, LAST)
        seen = (lax.shift_right_logical(col, 6) == row) & (lax.bitwise_and(col, SUF - 1).astype(F32) < live_rows)
        bias = jnp.where(seen, 0.0, LOW)
        scores = (scores.reshape(HEADS, 8, keys) + bias[None]).reshape(HEADS * 8, keys)
        top = jnp.max(scores, axis=1, keepdims=True)
        raw = jnp.exp2((scores - top) * (SCALE * LOG2E))
        total = jnp.sum(raw, axis=1, keepdims=True)
        summed = dot(raw.astype(BF16), lat) * (1.0 / total)
        result[:, rows, :] = summed.reshape(HEADS, 8, KVL)
        log = (top * SCALE + jnp.log(total)).reshape(HEADS, 8, 1)
        spread = jnp.zeros((8, 128), F32)
        for head in range(HEADS):
            spread = jnp.where(lax.bitwise_and(lane, 15) == head, log[head], spread)
        logs[rows, :] = spread

    for i in range(0, ROWS // 8, 2):
        for k in range(2):
            at = latent.at[pl.ds(8 * (i + k), 8)]
            pltpu.make_async_copy(latent_in.at[pl.ds(8 * (i + k), 8)], at, lat_sems.at[i + k]).wait()
        for k in range(2):
            block(i + k, length[8 * (i + k) : 8 * (i + k) + 8])
    for copy in v_copies:
        copy.wait()
    for head in range(HEADS):
        part = dot(result[head].astype(BF16), whole_v[head], LAST)
        out[:, head * VDIM : (head + 1) * VDIM] = part.astype(BF16)
    out[:, OUT:] = pack_log(logs[...])


def final_kernel(own, r0, r1, r2, r3, out):
    gather = (
        (lax.bitwise_and(iota((128, 128), 0), 15) == iota((128, 128), 1)) & (iota((128, 128), 0) < 48)
    ).astype(BF16)
    parts = (own, r0, r1, r2, r3)
    logs = [dot(part[:, OUT:], gather) for part in parts]
    top = functools.reduce(jnp.maximum, logs)
    weights = [jnp.exp(log - top) for log in logs]
    total = 1.0 / functools.reduce(jnp.add, weights)
    weights = [w * total for w in weights]
    for head in range(HEADS):
        at = slice(head * VDIM, (head + 1) * VDIM)
        scaled = [part[:, at].astype(F32) * weight[:, head : head + 1] for part, weight in zip(parts, weights)]
        out[:, at] = functools.reduce(jnp.add, scaled).astype(BF16)


def row_of(z, x, c):
    return ((z % NZ) * NX + x % NX) * NC + c


CHIPS = [(z, x, c) for z in range(NZ) for x in range(NX) for c in range(NC)]


def ring_z(a):
    return lax.ppermute(a, "rows", [(row_of(z, x, c), row_of(z + 1 - 2 * c, x, c)) for z, x, c in CHIPS])


def ring_x(a, steps=1):
    return lax.ppermute(a, "rows", [(row_of(z, x, c), row_of(z, x + steps * (1 - 2 * c), c)) for z, x, c in CHIPS])


def back_x(a, steps=1):
    return ring_x(a, -steps)


def swap(a):
    return lax.ppermute(a, "rows", [(row_of(z, x, c), row_of(z, x, 1 - c)) for z, x, c in CHIPS])


def cost(us):
    return pl.CostEstimate(flops=int(us * 1e6), bytes_accessed=int(us * 3.0e6), transcendentals=0)


def struct(*shape, dtype=BF16):
    return jax.ShapeDtypeStruct(shape, dtype)


def shards(
    q_nope, q_rope, w_uk, w_uv, prefix_latent, prefix_rope, suffix_latent, suffix_rope, page_slot, page_pattern, suffix_len
):
    row, y = lax.axis_index("rows"), lax.axis_index("proj")
    place = jnp.stack([row // (NX * NC), row // NC % NX, row % NC, y]).astype(I32)

    def exchange(a):
        return lax.all_to_all(a, "proj", split_axis=0, concat_axis=0, tiled=True)

    def after(a, *others):
        return lax.optimization_barrier((a, *others))[0]

    def halve(full):
        whole = full.reshape(NY, HEADS, *full.shape[1:])
        half = lax.dynamic_slice_in_dim(whole, (row % NC) * (HEADS // 2), HEADS // 2, 1)
        return half.reshape(NY * HEADS // 2, *full.shape[1:])

    half = (NY, HEADS // 2, NOPE, 128)
    both = jnp.concatenate([halve(w).reshape(half) for w in (w_uk, w_uv)], axis=1).reshape(NY * HEADS, NOPE, 128)
    page_pattern = after(page_pattern, both)
    both = exchange(both)
    pages, pay = pl.pallas_call(
        pack_kernel,
        out_shape=(struct(2, UNIT, KVL), struct(ROWS, PAY)),
        in_specs=[VMEM] * 2 + [HBM] * 4,
        out_specs=(VMEM,) * 2,
        scratch_shapes=[pltpu.VMEM((2, PAGE * ROPE), BF16), pltpu.SemaphoreType.DMA((4,))],
        compiler_params=params(60),
        cost_estimate=cost(2),
        name="pack",
    )(page_pattern.T, page_slot.reshape(1, -1), prefix_rope, prefix_latent, q_nope, q_rope)

    a, b = [pages], [swap(pages)]
    a_pay, b_pay = [pay], [swap(pay)]
    a.append(ring_z(a[0]))
    a_pay.append(ring_x(pay))
    b.append(ring_z(b[0]))
    b_pay.append(ring_x(b_pay[0]))
    a.append(ring_z(after(a[1], a_pay[1])))
    a_pay.append(ring_x(after(a_pay[1], a[1])))
    b.append(ring_z(after(b[1], b_pay[1])))
    pays = [pay, a_pay[1], a_pay[2], swap(b_pay[1])]
    a.append(ring_z(after(a[2], b[1], b_pay[1])))
    b.append(ring_z(b[2]))
    split = both.reshape(NY, HEADS, NOPE, 128)
    k_part, v_part = split[:, : HEADS // 2], split[:, HEADS // 2 :]
    k_swap = swap(after(k_part.reshape(NY * HEADS // 2, NOPE, 128), a[3], b[2], a_pay[2]))
    v_swap = swap(v_part.reshape(NY * HEADS // 2, NOPE, 128))

    q_lat, q_rot, page_bit, slot_of = pl.pallas_call(
        query_kernel,
        out_shape=(
            struct(HEADS, SLOTS, KVL), struct(HEADS, SLOTS, ROPE),
            struct(SLOTS, 128, dtype=F32), struct(4 * ROWS, 128, dtype=F32),
        ),
        in_specs=[SMEM] + [ANY] * 6,
        out_specs=(VMEM,) * 4,
        scratch_shapes=[
            *[pltpu.VMEM((ROWS, PAY), BF16)] * 4,
            pltpu.VMEM((HEADS, NOPE, KVL), BF16), pltpu.VMEM((SLOTS, 4 * ROWS), BF16),
            pltpu.SemaphoreType.DMA((4,)), pltpu.SemaphoreType.DMA((8,)),
        ],
        compiler_params=params(32),
        cost_estimate=cost(4),
        name="queries",
    )(place, *pays, both, k_swap)

    a.append(ring_z(after(a[3], b[2], a_pay[2])))
    a_swap = [None] + [swap(u) for u in a[1:4]]
    b_swap = [None] + [swap(u) for u in b[1:3]]
    early_units = [a[0], b[0], a[1], b[1], a[2], b[2], b_swap[2], a_swap[2], b_swap[1], a_swap[1]]

    early, early_logs = pl.pallas_call(
        early_kernel,
        out_shape=(struct(HEADS, EARLY * 16, KVL), struct(EARLY * 16, 128, dtype=F32)),
        in_specs=[ANY] * EARLY + [VMEM] * 3,
        out_specs=(VMEM, VMEM),
        scratch_shapes=[pltpu.VMEM((EARLY, 2, UNIT, KVL), BF16), pltpu.SemaphoreType.DMA((EARLY,))],
        compiler_params=params(32),
        cost_estimate=cost(1),
        name="early_pages",
    )(*early_units, q_lat, q_rot, page_bit)

    a_swap.append(swap(after(a[4], early_logs)))
    b_swap.append(swap(after(b[3], early_logs)))
    late_units = [a[3], b[3], a[4], a_swap[4], b_swap[3], a_swap[3]]
    returns = pl.pallas_call(
        late_kernel,
        out_shape=(struct(ROWS, RET),) * 4,
        in_specs=[ANY] * LATE + [SMEM] + [VMEM] * 6 + [ANY] * 2,
        out_specs=(VMEM,) * 4,
        scratch_shapes=[
            pltpu.VMEM((LATE, 2, UNIT, KVL), BF16), pltpu.VMEM((HEADS, LATE * 16, KVL), BF16),
            pltpu.VMEM((LATE * 16, 128), F32), pltpu.VMEM((HEADS, VDIM, KVL), BF16), pltpu.VMEM((SLOTS, OUT), BF16),
            pltpu.SemaphoreType.DMA((LATE,)), pltpu.SemaphoreType.DMA((8,)),
        ],
        compiler_params=params(32),
        cost_estimate=cost(7),
        name="late_pages",
    )(*late_units, place, q_lat, q_rot, page_bit, slot_of, early, early_logs, both, v_swap)

    backs = [returns[0], back_x(returns[1]), back_x(returns[2], 2), ring_x(returns[3])]
    k_swap, returns = lax.optimization_barrier((k_swap, returns))
    own = pl.pallas_call(
        suffix_kernel,
        out_shape=struct(ROWS, RET),
        in_specs=[SMEM, VMEM] + [HBM] * 4 + [ANY] * 3,
        out_specs=VMEM,
        scratch_shapes=[
            pltpu.VMEM((ROWS, QN), BF16), pltpu.VMEM((ROWS, QR), BF16),
            pltpu.VMEM((ROWS, SUF, KVL), BF16), pltpu.VMEM((ROWS, SUF * ROPE), BF16),
            pltpu.VMEM((ROWS, SUF * ROPE), F32), pltpu.VMEM((HEADS, ROWS, KVL), F32),
            pltpu.VMEM((HEADS, ROWS, ROPE), F32), pltpu.VMEM((HEADS, ROWS, KVL), F32), pltpu.VMEM((ROWS, 128), F32),
            pltpu.VMEM((HEADS, NOPE, KVL), BF16), pltpu.VMEM((HEADS, VDIM, KVL), BF16),
            pltpu.SemaphoreType.DMA((8,)), pltpu.SemaphoreType.DMA((8,)),
            pltpu.SemaphoreType.DMA((3,)), pltpu.SemaphoreType.DMA((8,)),
        ],
        compiler_params=params(60),
        cost_estimate=cost(8),
        name="suffix",
    )(place, suffix_len.reshape(1, -1), q_nope, q_rope, suffix_latent, suffix_rope, both, k_swap, v_swap)

    return pl.pallas_call(
        final_kernel,
        out_shape=struct(ROWS, OUT),
        in_specs=[VMEM] * 5,
        out_specs=VMEM,
        compiler_params=params(16),
        cost_estimate=cost(2),
        name="combine",
    )(own, *backs)


def solution(mesh):
    return jax.shard_map(
        shards,
        mesh=mesh,
        in_specs=(
            P("rows", "proj"), P("rows", "proj"), P(None, None, "proj"), P(None, None, "proj"),
            P("rows", None, None), P("rows", None), P("rows", None, None), P("rows", None),
            P(), P("rows", None), P("rows"),
        ),
        out_specs=P("rows", "proj"),
        check_vma=False,
    )
```

```python
import functools

import jax
import jax.numpy as jnp
from jax import lax
from jax.experimental import pallas as pl
from jax.experimental.pallas import tpu as pltpu
from jax.sharding import PartitionSpec as P

F32, BF16, I32 = jnp.float32, jnp.bfloat16, jnp.int32
LOW = -1e30

NZ, NX, NC, NY = 8, 4, 2, 4
HEADS = 16
ROWS = 64
NOPE = 128
VDIM = 128
ROPE = 64
KVL = 512
PAGE = 128
SUF = 64
UNIT = PAGE + PAGE * ROPE // KVL
QN = HEADS * NOPE
QR = HEADS * ROPE
PAY = QN + QR + 128
SLOTS = 256
PAIRS = 16
EARLY = 10
LATE = PAIRS - EARLY
SCALE = (NOPE + ROPE) ** -0.5
OUT = HEADS * VDIM
RET = OUT + 128
LOG2E = 1.4426950408889634
LAST = (((1,), (1,)), ((), ()))
FIRST = (((0,), (0,)), ((), ()))


def dot(a, b, dims=(((1,), (0,)), ((), ())), precision=None):
    return lax.dot_general(a, b, dims, preferred_element_type=F32, precision=precision)


def iota(shape, axis):
    return lax.broadcasted_iota(I32, shape, axis)


def params(mib):
    return pltpu.CompilerParams(vmem_limit_bytes=mib << 20)


VMEM = pl.BlockSpec(memory_space=pltpu.VMEM)
SMEM = pl.BlockSpec(memory_space=pltpu.SMEM)
ANY = pl.BlockSpec(memory_space=pl.ANY)
HBM = pl.BlockSpec(memory_space=pltpu.HBM)


def load_all(pairs, sems):
    copies = [pltpu.make_async_copy(src, dst, sems.at[i]) for i, (src, dst) in enumerate(pairs)]
    for copy in copies:
        copy.start()
    return copies


def pack_kernel(pattern, page_slot, rope_in, latent_in, q_nope, q_rope, pages, pay, rope, sems):
    copies = load_all(
        [
            (rope_in, rope),
            (latent_in, pages.at[:, :PAGE, :]),
            (q_nope, pay.at[:, :QN]),
            (q_rope, pay.at[:, QN : QN + QR]),
        ],
        sems,
    )
    copies[0].wait()
    flat = rope[...].astype(F32)
    half = PAGE // 2
    sub = iota((8, 128), 0)
    even = (iota((half, PAGE), 1) == 2 * iota((half, PAGE), 0)).astype(F32)
    odd = (iota((half, PAGE), 1) == 2 * iota((half, PAGE), 0) + 1).astype(F32)
    for page in range(2):
        tiles = []
        for tile in range(half // 8):
            piece = jnp.zeros((8, 128), F32)
            for row in range(8):
                at = (tile * 8 + row) * 128
                piece = jnp.where(sub == row, flat[page : page + 1, at : at + 128], piece)
            tiles.append(piece)
        two_tokens = jnp.concatenate(tiles, axis=0)
        turned = dot(two_tokens[:, :ROPE], even, FIRST) + dot(two_tokens[:, ROPE:], odd, FIRST)
        turned = jnp.concatenate([turned[16 * i : 16 * i + 16] for i in range(4)], axis=1)
        pages[page, PAGE:, :] = turned.astype(BF16)
    lane = iota((ROWS, 128), 1)
    across = iota((ROWS, ROWS), 0) == iota((ROWS, ROWS), 1)
    slot_row = page_slot[...].astype(F32)
    slots, owners = [], []
    for k in range(2):
        names = pattern[k : k + 1, :].astype(F32)
        names = jnp.sum(jnp.where(across, names, 0.0), axis=1, keepdims=True).astype(I32)
        named = lane == names
        slot = jnp.sum(jnp.where(named, slot_row, 0.0), axis=1, keepdims=True)
        slots.append(slot)
        owners.append((lane == lax.shift_right_logical(slot.astype(I32), 1)).astype(F32))
    below = (iota((ROWS, ROWS), 0) > iota((ROWS, ROWS), 1)).astype(F32)
    before0 = dot(below, owners[0])
    before1 = dot(below, owners[1]) + jnp.sum(owners[0], axis=0, keepdims=True)
    rank0 = jnp.sum(owners[0] * before0, axis=1, keepdims=True)
    rank1 = jnp.sum(owners[1] * before1, axis=1, keepdims=True)
    code = jnp.zeros((ROWS, 128), F32)
    for at, value in enumerate((slots[0], slots[1], rank0, rank1)):
        code = jnp.where(lane == at, value, code)
    pay[:, QN + QR :] = code.astype(BF16)
    for copy in copies[1:]:
        copy.wait()


def gather_weights(place, both, half_swap, second, whole, sems):
    core, heads = place[2], HEADS // 2
    pairs = []
    for which, part in ((core, both), (1 - core, half_swap)):
        for y in range(NY):
            to = whole.at[pl.ds(which * heads, heads), :, y * 128 : (y + 1) * 128]
            at = (2 * y + second) * heads if part is both else y * heads
            pairs.append((part.at[pl.ds(at, heads)], to))
    return load_all(pairs, sems)


def gather_kernel(
    place, p0, p1, p2, p3, q_nope, q_rot, page_bit, pick_out, partner_out, chosen_out, flags, turned
):
    z, x, core = place[0], place[1], place[2]
    pays = (p0, p1, p2, p3)
    missing = []
    lane = iota((ROWS, 128), 1)
    wide = iota((ROWS, SLOTS), 1)
    picks, bits, places = ([], []), ([], []), []
    for peer, part in enumerate(pays):
        code = part[:, QN + QR :].astype(F32)
        columns = [
            jnp.sum(jnp.where(lane == at, code, 0.0), axis=1, keepdims=True).astype(I32) for at in range(4)
        ]
        found = []
        for k in range(2):
            slot, rank = columns[k], columns[2 + k]
            away = (z - lax.shift_right_logical(slot, 4)) * (1 - 2 * core)
            away = lax.bitwise_and(away, NZ - 1)
            order = jnp.where(away < 3, away, jnp.where(away >= 6, away - 3, away + 2))
            other = jnp.where(lax.bitwise_and(lax.shift_right_logical(slot, 1), 1) != core, 1, 0)
            here = lax.bitwise_and(lax.shift_right_logical(slot, 2), 3) == x
            at = jnp.where(here, (order * 2 + other) * 16 + peer * 4 + rank, -1)
            picks[k].append((wide == at).astype(F32))
            bits[k].append(lax.bitwise_and(slot, 1).astype(F32) * jnp.ones((1, 128), F32))
            found.append(jnp.where(here, 1.0, 0.0))
        missing.append(jnp.concatenate(found, axis=1))
    pick = [jnp.concatenate(p, axis=0) for p in picks]
    bit = [jnp.concatenate(b, axis=0) for b in bits]
    page_bit[...] = dot(pick[0], bit[0], FIRST) + dot(pick[1], bit[1], FIRST)
    turned[...] = jnp.transpose(pick[0] + pick[1]).astype(BF16)
    pick_out[...] = (pick[0] + pick[1]).astype(BF16)
    pair = dot(pick[0], pick[1], FIRST) + dot(pick[1], pick[0], FIRST)
    partner_out[...] = pair.astype(BF16)
    found = jnp.concatenate(missing, axis=0)
    chosen_out[...] = (pick[0] + pick[1] * (1.0 - found[:, 0:1])).astype(BF16)
    flags[:, :128] = jnp.sum(pair, axis=1, keepdims=True) * jnp.ones((1, 128), F32)
    flags[:, 128:] = jnp.maximum(found[:, 0:1], found[:, 1:2]) * jnp.ones((1, 128), F32)

    def two_heads(i, carry):
        rot = pl.ds(pl.multiple_of(QN + i * 128, 128), 128)
        gathered = dot(turned[...], jnp.concatenate([p[:, rot] for p in pays], axis=0)).astype(BF16)
        at = pl.ds(pl.multiple_of(i * 2 * NOPE, 128), 2 * NOPE)
        q_nope[:, at] = dot(turned[...], jnp.concatenate([p[:, at] for p in pays], axis=0)).astype(BF16)
        for k in range(2):
            q_rot[2 * i + k] = gathered[:, k * ROPE : (k + 1) * ROPE]
        return carry

    lax.fori_loop(0, HEADS // 2, two_heads, 0)


def query_kernel(place, q_nope, both, k_swap, q_lat, whole, sems):
    for copy in gather_weights(place, both, k_swap, 0, whole, sems):
        copy.wait()

    def two_heads(i, carry):
        left = q_nope[:, pl.ds(pl.multiple_of(i * 2 * NOPE, 128), 2 * NOPE)]
        for k in range(2):
            q_lat[2 * i + k] = dot(left[:, k * NOPE : (k + 1) * NOPE], whole[2 * i + k]).astype(BF16)
        return carry

    lax.fori_loop(0, HEADS // 2, two_heads, 0)


def start_units(units, held, sems):
    copies = [pltpu.make_async_copy(unit, held.at[i], sems.at[i]) for i, unit in enumerate(units)]
    for copy in copies:
        copy.start()


def attend_units(count, base, unit0, q_lat, q_rot, page_bit, held, sems, result, logs):
    lane = iota((16, 128), 1)

    def block(i):
        unit = held.at[i]
        latent = unit[:, :PAGE, :].reshape(2 * PAGE, KVL)
        rot = unit[:, PAGE:, :]
        keys = jnp.concatenate(
            [
                jnp.concatenate([rot[page, :, 128 * j : 128 * j + 128] for j in range(4)], axis=0)
                for page in range(2)
            ],
            axis=1,
        )
        at = pl.ds(pl.multiple_of((base + i) * 16, 16), 16)
        query = q_lat[:, at, :].reshape(HEADS * 16, KVL)
        query_rot = q_rot[:, at, :].reshape(HEADS * 16, ROPE)
        scores = dot(query, latent, LAST) + dot(query_rot, keys)
        bit = page_bit[at, :]
        bias = jnp.concatenate(
            [jnp.where(bit < 0.5, 0.0, LOW), jnp.where(bit < 0.5, LOW, 0.0)], axis=1
        )
        scores = (scores.reshape(HEADS, 16, 2 * PAGE) + bias[None]).reshape(HEADS * 16, 2 * PAGE)
        top = jnp.max(scores, axis=1, keepdims=True)
        raw = jnp.exp2((scores - top) * (SCALE * LOG2E))
        total = jnp.sum(raw, axis=1, keepdims=True)
        summed = dot(raw.astype(BF16), latent) * (1.0 / total)
        out_at = pl.ds(pl.multiple_of(i * 16, 16), 16)
        result[:, out_at, :] = summed.astype(BF16).reshape(HEADS, 16, KVL)
        log = (top * SCALE + jnp.log(total)).reshape(HEADS, 16, 1)
        spread = jnp.zeros((16, 128), F32)
        for head in range(HEADS):
            mine = (lax.bitwise_and(lane, 15) == head) & (lane < 48)
            spread = jnp.where(mine, log[head], spread)
        logs[out_at, :] = spread

    def body(i, carry):
        for k in range(2):
            pltpu.make_async_copy(unit0, held.at[2 * i + k], sems.at[2 * i + k]).wait()
        for k in range(2):
            block(2 * i + k)
        return carry

    lax.fori_loop(0, count // 2, body, 0)


def early_kernel(*refs):
    units = refs[:EARLY]
    q_lat, q_rot, page_bit, result, logs, held, sems = refs[EARLY:]
    start_units(units, held, sems)
    attend_units(EARLY, 0, units[0], q_lat, q_rot, page_bit, held, sems, result, logs)


def pack_log(log):
    lane = iota(log.shape, 1)
    high = log.astype(BF16).astype(F32)
    rest = log - high
    middle = rest.astype(BF16).astype(F32)
    packed = jnp.where(lane < 16, high, jnp.where(lane < 32, middle, rest - middle))
    return jnp.where(lane < 48, packed, 0.0).astype(BF16)


def late_kernel(*refs):
    units = refs[:LATE]
    (
        place, q_lat, q_rot, page_bit, pick, partner, chosen, flags, early, early_logs, weights, v_swap,
        r0, r1, r2, r3, held, result, logs, whole, parts, sems, w_sems,
    ) = refs[LATE:]
    start_units(units, held, sems)
    copies = gather_weights(place, weights, v_swap, 1, whole, w_sems)
    attend_units(LATE, EARLY, units[0], q_lat, q_rot, page_bit, held, sems, result, logs)
    log = jnp.concatenate([early_logs[...], logs[...]], axis=0)
    other = (flags[:, :128] - 1.0) * (-LOW)
    rest = log
    for _ in range(3):
        part = rest.astype(BF16)
        rest = rest - part.astype(F32)
        other = other + dot(partner[...], part)
    top = jnp.maximum(log, other)
    mine = jnp.exp(log - top)
    both = mine + jnp.exp(other - top)
    weight = mine / both
    merged = top + jnp.log(both)
    for copy in copies:
        copy.wait()
    for head in range(HEADS):
        mixed = jnp.concatenate([early[head], result[head]], axis=0)
        part = dot(mixed, whole[head], LAST) * weight[:, head : head + 1]
        parts[:, head * VDIM : (head + 1) * VDIM] = part.astype(BF16)
    lane = iota((SLOTS, 128), 1)
    empty = jnp.where(lane < 16, LOW, 0.0)
    packed = dot(chosen[...], pack_log(merged))
    packed = jnp.where(flags[:, 128:] > 0.5, packed, empty).astype(BF16)
    for peer, out in enumerate((r0, r1, r2, r3)):
        rows = slice(peer * ROWS, (peer + 1) * ROWS)
        out[:, :OUT] = dot(pick[rows, :], parts[...]).astype(BF16)
        out[:, OUT:] = packed[rows]


def suffix_kernel(
    place, live, q_nope_in, q_rope_in, latent_in, rope_in, both, k_swap, v_swap,
    out, q_nope, q_rope, latent, rope, rope32, query32, rot32, result, logs, whole_k, whole_v,
    k_sems, v_sems, q_sems, lat_sems,
):
    q_copies = load_all([(q_nope_in, q_nope), (q_rope_in, q_rope), (rope_in, rope)], q_sems)
    k_copies = gather_weights(place, both, k_swap, 0, whole_k, k_sems)
    for i in range(ROWS // 8):
        pltpu.make_async_copy(latent_in.at[pl.ds(8 * i, 8)], latent.at[pl.ds(8 * i, 8)], lat_sems.at[i]).start()
    v_copies = gather_weights(place, both, v_swap, 1, whole_v, v_sems)
    for copy in q_copies:
        copy.wait()
    rope32[...] = rope[...].astype(F32)
    across = iota((ROWS, ROWS), 0) == iota((ROWS, ROWS), 1)
    length = jnp.sum(jnp.where(across, live[...].astype(F32), 0.0), axis=1, keepdims=True)
    for copy in k_copies:
        copy.wait()
    for head in range(HEADS):
        projected = dot(q_nope[:, head * NOPE : (head + 1) * NOPE], whole_k[head])
        query32[head] = projected.astype(BF16).astype(F32)
        rot32[head] = q_rope[:, head * ROPE : (head + 1) * ROPE].astype(F32)
    keys, pairs = 8 * SUF, 8 * SUF // 2
    key, pair = iota((keys, pairs), 0), iota((keys, pairs), 1)
    same = lax.shift_right_logical(key, 6) == lax.bitwise_and(pair, 7)
    first = 2 * lax.shift_right_logical(pair, 3)
    even = (same & (lax.bitwise_and(key, SUF - 1) == first)).astype(BF16)
    odd = (same & (lax.bitwise_and(key, SUF - 1) == first + 1)).astype(BF16)
    lane = iota((8, 128), 1)
    col, row = iota((8, keys), 1), iota((8, keys), 0)

    def block(i, live_rows):
        rows = pl.ds(pl.multiple_of(i * 8, 8), 8)
        query = query32[:, rows, :].reshape(HEADS * 8, KVL).astype(BF16)
        query_rot = rot32[:, rows, :].reshape(HEADS * 8, ROPE).astype(BF16)
        lat = latent[rows].reshape(keys, KVL)
        rot = rope32[rows, :]
        rot = jnp.concatenate([rot[:, 128 * j : 128 * j + 128] for j in range(SUF // 2)], axis=0).astype(BF16)
        rot_keys = (dot(even, rot[:, :ROPE]) + dot(odd, rot[:, ROPE:])).astype(BF16)
        scores = dot(query, lat, LAST) + dot(query_rot, rot_keys, LAST)
        seen = (lax.shift_right_logical(col, 6) == row) & (lax.bitwise_and(col, SUF - 1).astype(F32) < live_rows)
        bias = jnp.where(seen, 0.0, LOW)
        scores = (scores.reshape(HEADS, 8, keys) + bias[None]).reshape(HEADS * 8, keys)
        top = jnp.max(scores, axis=1, keepdims=True)
        raw = jnp.exp2((scores - top) * (SCALE * LOG2E))
        total = jnp.sum(raw, axis=1, keepdims=True)
        summed = dot(raw.astype(BF16), lat) * (1.0 / total)
        result[:, rows, :] = summed.reshape(HEADS, 8, KVL)
        log = (top * SCALE + jnp.log(total)).reshape(HEADS, 8, 1)
        spread = jnp.zeros((8, 128), F32)
        for head in range(HEADS):
            spread = jnp.where(lax.bitwise_and(lane, 15) == head, log[head], spread)
        logs[rows, :] = spread

    for i in range(0, ROWS // 8, 2):
        for k in range(2):
            at = latent.at[pl.ds(8 * (i + k), 8)]
            pltpu.make_async_copy(latent_in.at[pl.ds(8 * (i + k), 8)], at, lat_sems.at[i + k]).wait()
        for k in range(2):
            block(i + k, length[8 * (i + k) : 8 * (i + k) + 8])
    for copy in v_copies:
        copy.wait()
    for head in range(HEADS):
        part = dot(result[head].astype(BF16), whole_v[head], LAST)
        out[:, head * VDIM : (head + 1) * VDIM] = part.astype(BF16)
    out[:, OUT:] = pack_log(logs[...])


def final_kernel(own, r0, r1, r2, r3, out):
    gather = (
        (lax.bitwise_and(iota((128, 128), 0), 15) == iota((128, 128), 1)) & (iota((128, 128), 0) < 48)
    ).astype(BF16)
    parts = (own, r0, r1, r2, r3)
    logs = [dot(part[:, OUT:], gather) for part in parts]
    top = functools.reduce(jnp.maximum, logs)
    weights = [jnp.exp(log - top) for log in logs]
    total = 1.0 / functools.reduce(jnp.add, weights)
    weights = [w * total for w in weights]
    for head in range(HEADS):
        at = slice(head * VDIM, (head + 1) * VDIM)
        scaled = [part[:, at].astype(F32) * weight[:, head : head + 1] for part, weight in zip(parts, weights)]
        out[:, at] = functools.reduce(jnp.add, scaled).astype(BF16)


def row_of(z, x, c):
    return ((z % NZ) * NX + x % NX) * NC + c


CHIPS = [(z, x, c) for z in range(NZ) for x in range(NX) for c in range(NC)]


def ring_z(a):
    return lax.ppermute(a, "rows", [(row_of(z, x, c), row_of(z + 1 - 2 * c, x, c)) for z, x, c in CHIPS])


def ring_x(a, steps=1):
    return lax.ppermute(a, "rows", [(row_of(z, x, c), row_of(z, x + steps * (1 - 2 * c), c)) for z, x, c in CHIPS])


def back_x(a, steps=1):
    return ring_x(a, -steps)


def swap(a):
    return lax.ppermute(a, "rows", [(row_of(z, x, c), row_of(z, x, 1 - c)) for z, x, c in CHIPS])


def cost(us):
    return pl.CostEstimate(flops=int(us * 1e6), bytes_accessed=int(us * 3.0e6), transcendentals=0)


def struct(*shape, dtype=BF16):
    return jax.ShapeDtypeStruct(shape, dtype)


def shards(
    q_nope, q_rope, w_uk, w_uv, prefix_latent, prefix_rope, suffix_latent, suffix_rope, page_slot, page_pattern, suffix_len
):
    row, y = lax.axis_index("rows"), lax.axis_index("proj")
    place = jnp.stack([row // (NX * NC), row // NC % NX, row % NC, y]).astype(I32)

    def exchange(a):
        return lax.all_to_all(a, "proj", split_axis=0, concat_axis=0, tiled=True)

    def after(a, *others):
        return lax.optimization_barrier((a, *others))[0]

    def halve(full):
        whole = full.reshape(NY, HEADS, *full.shape[1:])
        half = lax.dynamic_slice_in_dim(whole, (row % NC) * (HEADS // 2), HEADS // 2, 1)
        return half.reshape(NY * HEADS // 2, *full.shape[1:])

    half = (NY, HEADS // 2, NOPE, 128)
    both = jnp.concatenate([halve(w).reshape(half) for w in (w_uk, w_uv)], axis=1).reshape(NY * HEADS, NOPE, 128)
    page_pattern = after(page_pattern, both)
    both = exchange(both)
    pages, pay = pl.pallas_call(
        pack_kernel,
        out_shape=(struct(2, UNIT, KVL), struct(ROWS, PAY)),
        in_specs=[VMEM] * 2 + [HBM] * 4,
        out_specs=(VMEM,) * 2,
        scratch_shapes=[pltpu.VMEM((2, PAGE * ROPE), BF16), pltpu.SemaphoreType.DMA((4,))],
        compiler_params=params(60),
        cost_estimate=cost(2),
        name="pack",
    )(page_pattern.T, page_slot.reshape(1, -1), prefix_rope, prefix_latent, q_nope, q_rope)

    a, b = [pages], [swap(pages)]
    a_pay, b_pay = [pay], [swap(pay)]
    a.append(ring_z(a[0]))
    a_pay.append(ring_x(pay))
    b.append(ring_z(b[0]))
    b_pay.append(ring_x(b_pay[0]))
    a.append(ring_z(after(a[1], a_pay[1])))
    a_pay.append(ring_x(after(a_pay[1], a[1])))
    b.append(ring_z(after(b[1], b_pay[1])))
    pays = [pay, a_pay[1], a_pay[2], swap(b_pay[1])]
    a.append(ring_z(after(a[2], b[1], b_pay[1])))
    b.append(ring_z(b[2]))
    square = (SLOTS, SLOTS)
    q_slots, q_rot, page_bit, *ties = pl.pallas_call(
        gather_kernel,
        out_shape=(
            struct(SLOTS, QN), struct(HEADS, SLOTS, ROPE), struct(SLOTS, 128, dtype=F32),
            struct(*square), struct(*square), struct(*square), struct(*square, dtype=F32),
        ),
        in_specs=[SMEM] + [VMEM] * 4,
        out_specs=(VMEM,) * 7,
        scratch_shapes=[pltpu.VMEM(square, BF16)],
        compiler_params=params(60),
        cost_estimate=cost(3),
        name="gather",
    )(place, *pays)

    split = both.reshape(NY, HEADS, NOPE, 128)
    k_part, v_part = split[:, : HEADS // 2], split[:, HEADS // 2 :]
    k_swap = swap(after(k_part.reshape(NY * HEADS // 2, NOPE, 128), a[3], b[2], q_slots))
    v_swap = swap(v_part.reshape(NY * HEADS // 2, NOPE, 128))

    q_lat = pl.pallas_call(
        query_kernel,
        out_shape=struct(HEADS, SLOTS, KVL),
        in_specs=[SMEM, VMEM] + [ANY] * 2,
        out_specs=VMEM,
        scratch_shapes=[pltpu.VMEM((HEADS, NOPE, KVL), BF16), pltpu.SemaphoreType.DMA((8,))],
        compiler_params=params(20),
        cost_estimate=cost(3),
        name="queries",
    )(place, q_slots, both, k_swap)

    a.append(ring_z(after(a[3], b[2], a_pay[2])))
    a_swap = [None] + [swap(u) for u in a[1:4]]
    b_swap = [None] + [swap(u) for u in b[1:3]]
    early_units = [a[0], b[0], a[1], b[1], a[2], b[2], b_swap[2], a_swap[2], b_swap[1], a_swap[1]]

    early, early_logs = pl.pallas_call(
        early_kernel,
        out_shape=(struct(HEADS, EARLY * 16, KVL), struct(EARLY * 16, 128, dtype=F32)),
        in_specs=[ANY] * EARLY + [VMEM] * 3,
        out_specs=(VMEM, VMEM),
        scratch_shapes=[pltpu.VMEM((EARLY, 2, UNIT, KVL), BF16), pltpu.SemaphoreType.DMA((EARLY,))],
        compiler_params=params(20),
        cost_estimate=cost(1),
        name="early_pages",
    )(*early_units, q_lat, q_rot, page_bit)

    a_swap.append(swap(after(a[4], early_logs)))
    b_swap.append(swap(after(b[3], early_logs)))
    late_units = [a[3], b[3], a[4], a_swap[4], b_swap[3], a_swap[3]]
    returns = pl.pallas_call(
        late_kernel,
        out_shape=(struct(ROWS, RET),) * 4,
        in_specs=[ANY] * LATE + [SMEM] + [VMEM] * 9 + [ANY] * 2,
        out_specs=(VMEM,) * 4,
        scratch_shapes=[
            pltpu.VMEM((LATE, 2, UNIT, KVL), BF16), pltpu.VMEM((HEADS, LATE * 16, KVL), BF16),
            pltpu.VMEM((LATE * 16, 128), F32), pltpu.VMEM((HEADS, VDIM, KVL), BF16), pltpu.VMEM((SLOTS, OUT), BF16),
            pltpu.SemaphoreType.DMA((LATE,)), pltpu.SemaphoreType.DMA((8,)),
        ],
        compiler_params=params(20),
        cost_estimate=cost(7),
        name="late_pages",
    )(*late_units, place, q_lat, q_rot, page_bit, *ties, early, early_logs, both, v_swap)

    backs = [returns[0], back_x(returns[1]), back_x(returns[2], 2), ring_x(returns[3])]
    k_swap, returns = lax.optimization_barrier((k_swap, returns))
    own = pl.pallas_call(
        suffix_kernel,
        out_shape=struct(ROWS, RET),
        in_specs=[SMEM, VMEM] + [HBM] * 4 + [ANY] * 3,
        out_specs=VMEM,
        scratch_shapes=[
            pltpu.VMEM((ROWS, QN), BF16), pltpu.VMEM((ROWS, QR), BF16),
            pltpu.VMEM((ROWS, SUF, KVL), BF16), pltpu.VMEM((ROWS, SUF * ROPE), BF16),
            pltpu.VMEM((ROWS, SUF * ROPE), F32), pltpu.VMEM((HEADS, ROWS, KVL), F32),
            pltpu.VMEM((HEADS, ROWS, ROPE), F32), pltpu.VMEM((HEADS, ROWS, KVL), F32), pltpu.VMEM((ROWS, 128), F32),
            pltpu.VMEM((HEADS, NOPE, KVL), BF16), pltpu.VMEM((HEADS, VDIM, KVL), BF16),
            pltpu.SemaphoreType.DMA((8,)), pltpu.SemaphoreType.DMA((8,)),
            pltpu.SemaphoreType.DMA((3,)), pltpu.SemaphoreType.DMA((8,)),
        ],
        compiler_params=params(34),
        cost_estimate=cost(8),
        name="suffix",
    )(place, suffix_len.reshape(1, -1), q_nope, q_rope, suffix_latent, suffix_rope, both, k_swap, v_swap)

    return pl.pallas_call(
        final_kernel,
        out_shape=struct(ROWS, OUT),
        in_specs=[VMEM] * 5,
        out_specs=VMEM,
        compiler_params=params(16),
        cost_estimate=cost(2),
        name="combine",
    )(own, *backs)


def solution(mesh):
    return jax.shard_map(
        shards,
        mesh=mesh,
        in_specs=(
            P("rows", "proj"), P("rows", "proj"), P(None, None, "proj"), P(None, None, "proj"),
            P("rows", None, None), P("rows", None), P("rows", None, None), P("rows", None),
            P(), P("rows", None), P("rows"),
        ),
        out_specs=P("rows", "proj"),
        check_vma=False,
    )
```

```python
import functools

import jax
import jax.numpy as jnp
from jax import lax
from jax.experimental import pallas as pl
from jax.experimental.pallas import tpu as pltpu
from jax.sharding import PartitionSpec as P

F32, BF16, I32 = jnp.float32, jnp.bfloat16, jnp.int32
LOW = -1e30

NZ, NX, NC, NY = 8, 4, 2, 4
HEADS = 16
ROWS = 64
NOPE = 128
VDIM = 128
ROPE = 64
KVL = 512
PAGE = 128
SUF = 64
UNIT = PAGE + PAGE * ROPE // KVL
QN = HEADS * NOPE
QR = HEADS * ROPE
PAY = QN + QR + 128
SLOTS = 256
PAIRS = 16
EARLY = 10
LATE = PAIRS - EARLY
SCALE = (NOPE + ROPE) ** -0.5
OUT = HEADS * VDIM
RET = OUT + 128
LOG2E = 1.4426950408889634
LAST = (((1,), (1,)), ((), ()))
FIRST = (((0,), (0,)), ((), ()))


def dot(a, b, dims=(((1,), (0,)), ((), ())), precision=None):
    return lax.dot_general(a, b, dims, preferred_element_type=F32, precision=precision)


def iota(shape, axis):
    return lax.broadcasted_iota(I32, shape, axis)


def params(mib):
    return pltpu.CompilerParams(vmem_limit_bytes=mib << 20)


VMEM = pl.BlockSpec(memory_space=pltpu.VMEM)
SMEM = pl.BlockSpec(memory_space=pltpu.SMEM)
ANY = pl.BlockSpec(memory_space=pl.ANY)
HBM = pl.BlockSpec(memory_space=pltpu.HBM)


def load_all(pairs, sems):
    copies = [pltpu.make_async_copy(src, dst, sems.at[i]) for i, (src, dst) in enumerate(pairs)]
    for copy in copies:
        copy.start()
    return copies


def pack_kernel(
    pattern, page_slot, rope_in, latent_in, q_nope, q_rope, w_uk, w_uv, pages, pay, weights, rope, sems
):
    core, heads = lax.rem(lax.axis_index("rows"), NC), HEADS // 2
    copies = load_all(
        [
            (rope_in, rope),
            (latent_in, pages.at[:, :PAGE, :]),
            (q_nope, pay.at[:, :QN]),
            (q_rope, pay.at[:, QN : QN + QR]),
        ]
        + [
            (full.at[pl.ds(to * HEADS + heads * core, heads)], weights.at[pl.ds((2 * to + i) * heads, heads)])
            for i, full in enumerate((w_uk, w_uv))
            for to in range(NY)
        ],
        sems,
    )
    copies[0].wait()
    flat = rope[...].astype(F32)
    half = PAGE // 2
    sub = iota((8, 128), 0)
    even = (iota((half, PAGE), 1) == 2 * iota((half, PAGE), 0)).astype(F32)
    odd = (iota((half, PAGE), 1) == 2 * iota((half, PAGE), 0) + 1).astype(F32)
    for page in range(2):
        tiles = []
        for tile in range(half // 8):
            piece = jnp.zeros((8, 128), F32)
            for row in range(8):
                at = (tile * 8 + row) * 128
                piece = jnp.where(sub == row, flat[page : page + 1, at : at + 128], piece)
            tiles.append(piece)
        two_tokens = jnp.concatenate(tiles, axis=0)
        turned = dot(two_tokens[:, :ROPE], even, FIRST) + dot(two_tokens[:, ROPE:], odd, FIRST)
        turned = jnp.concatenate([turned[16 * i : 16 * i + 16] for i in range(4)], axis=1)
        pages[page, PAGE:, :] = turned.astype(BF16)
    lane = iota((ROWS, 128), 1)
    across = iota((ROWS, ROWS), 0) == iota((ROWS, ROWS), 1)
    slot_row = page_slot[...].astype(F32)
    slots, owners = [], []
    for k in range(2):
        names = pattern[k : k + 1, :].astype(F32)
        names = jnp.sum(jnp.where(across, names, 0.0), axis=1, keepdims=True).astype(I32)
        named = lane == names
        slot = jnp.sum(jnp.where(named, slot_row, 0.0), axis=1, keepdims=True)
        slots.append(slot)
        owners.append((lane == lax.shift_right_logical(slot.astype(I32), 1)).astype(F32))
    below = (iota((ROWS, ROWS), 0) > iota((ROWS, ROWS), 1)).astype(F32)
    before0 = dot(below, owners[0])
    before1 = dot(below, owners[1]) + jnp.sum(owners[0], axis=0, keepdims=True)
    rank0 = jnp.sum(owners[0] * before0, axis=1, keepdims=True)
    rank1 = jnp.sum(owners[1] * before1, axis=1, keepdims=True)
    code = jnp.zeros((ROWS, 128), F32)
    for at, value in enumerate((slots[0], slots[1], rank0, rank1)):
        code = jnp.where(lane == at, value, code)
    pay[:, QN + QR :] = code.astype(BF16)
    for copy in copies[1:]:
        copy.wait()


def gather_weights(place, both, half_swap, second, whole, sems):
    core, heads = place[2], HEADS // 2
    pairs = []
    for which, part in ((core, both), (1 - core, half_swap)):
        for y in range(NY):
            to = whole.at[pl.ds(which * heads, heads), :, y * 128 : (y + 1) * 128]
            at = (2 * y + second) * heads if part is both else y * heads
            pairs.append((part.at[pl.ds(at, heads)], to))
    return load_all(pairs, sems)


def gather_kernel(
    place, p0, p1, p2, p3, q_nope, q_rot, page_bit, pick_out, partner_out, chosen_out, flags, turned
):
    z, x, core = place[0], place[1], place[2]
    pays = (p0, p1, p2, p3)
    missing = []
    lane = iota((ROWS, 128), 1)
    wide = iota((ROWS, SLOTS), 1)
    picks, bits, places = ([], []), ([], []), []
    for peer, part in enumerate(pays):
        code = part[:, QN + QR :].astype(F32)
        columns = [
            jnp.sum(jnp.where(lane == at, code, 0.0), axis=1, keepdims=True).astype(I32) for at in range(4)
        ]
        found = []
        for k in range(2):
            slot, rank = columns[k], columns[2 + k]
            away = (z - lax.shift_right_logical(slot, 4)) * (1 - 2 * core)
            away = lax.bitwise_and(away, NZ - 1)
            order = jnp.where(away < 3, away, jnp.where(away >= 6, away - 3, away + 2))
            other = jnp.where(lax.bitwise_and(lax.shift_right_logical(slot, 1), 1) != core, 1, 0)
            here = lax.bitwise_and(lax.shift_right_logical(slot, 2), 3) == x
            at = jnp.where(here, (order * 2 + other) * 16 + peer * 4 + rank, -1)
            picks[k].append((wide == at).astype(F32))
            bits[k].append(lax.bitwise_and(slot, 1).astype(F32) * jnp.ones((1, 128), F32))
            found.append(jnp.where(here, 1.0, 0.0))
        missing.append(jnp.concatenate(found, axis=1))
    pick = [jnp.concatenate(p, axis=0) for p in picks]
    bit = [jnp.concatenate(b, axis=0) for b in bits]
    page_bit[...] = dot(pick[0], bit[0], FIRST) + dot(pick[1], bit[1], FIRST)
    turned[...] = jnp.transpose(pick[0] + pick[1]).astype(BF16)
    pick_out[...] = (pick[0] + pick[1]).astype(BF16)
    pair = dot(pick[0], pick[1], FIRST) + dot(pick[1], pick[0], FIRST)
    partner_out[...] = pair.astype(BF16)
    found = jnp.concatenate(missing, axis=0)
    chosen_out[...] = (pick[0] + pick[1] * (1.0 - found[:, 0:1])).astype(BF16)
    flags[:, :128] = jnp.sum(pair, axis=1, keepdims=True) * jnp.ones((1, 128), F32)
    flags[:, 128:] = jnp.maximum(found[:, 0:1], found[:, 1:2]) * jnp.ones((1, 128), F32)

    def two_heads(i, carry):
        rot = pl.ds(pl.multiple_of(QN + i * 128, 128), 128)
        gathered = dot(turned[...], jnp.concatenate([p[:, rot] for p in pays], axis=0)).astype(BF16)
        at = pl.ds(pl.multiple_of(i * 2 * NOPE, 128), 2 * NOPE)
        q_nope[:, at] = dot(turned[...], jnp.concatenate([p[:, at] for p in pays], axis=0)).astype(BF16)
        for k in range(2):
            q_rot[2 * i + k] = gathered[:, k * ROPE : (k + 1) * ROPE]
        return carry

    lax.fori_loop(0, HEADS // 2, two_heads, 0)


def query_kernel(place, q_nope, both, k_swap, q_lat, whole, sems):
    for copy in gather_weights(place, both, k_swap, 0, whole, sems):
        copy.wait()

    def two_heads(i, carry):
        left = q_nope[:, pl.ds(pl.multiple_of(i * 2 * NOPE, 128), 2 * NOPE)]
        for k in range(2):
            q_lat[2 * i + k] = dot(left[:, k * NOPE : (k + 1) * NOPE], whole[2 * i + k]).astype(BF16)
        return carry

    lax.fori_loop(0, HEADS // 2, two_heads, 0)


def start_units(units, held, sems):
    copies = [pltpu.make_async_copy(unit, held.at[i], sems.at[i]) for i, unit in enumerate(units)]
    for copy in copies:
        copy.start()


def attend_units(count, base, unit0, q_lat, q_rot, page_bit, held, sems, result, logs):
    lane = iota((16, 128), 1)

    def block(i):
        unit = held.at[i]
        latent = unit[:, :PAGE, :].reshape(2 * PAGE, KVL)
        rot = unit[:, PAGE:, :]
        keys = jnp.concatenate(
            [
                jnp.concatenate([rot[page, :, 128 * j : 128 * j + 128] for j in range(4)], axis=0)
                for page in range(2)
            ],
            axis=1,
        )
        at = pl.ds(pl.multiple_of((base + i) * 16, 16), 16)
        query = q_lat[:, at, :].reshape(HEADS * 16, KVL)
        query_rot = q_rot[:, at, :].reshape(HEADS * 16, ROPE)
        scores = dot(query, latent, LAST) + dot(query_rot, keys)
        bit = page_bit[at, :]
        bias = jnp.concatenate(
            [jnp.where(bit < 0.5, 0.0, LOW), jnp.where(bit < 0.5, LOW, 0.0)], axis=1
        )
        scores = (scores.reshape(HEADS, 16, 2 * PAGE) + bias[None]).reshape(HEADS * 16, 2 * PAGE)
        top = jnp.max(scores, axis=1, keepdims=True)
        raw = jnp.exp2((scores - top) * (SCALE * LOG2E))
        total = jnp.sum(raw, axis=1, keepdims=True)
        summed = dot(raw.astype(BF16), latent) * (1.0 / total)
        out_at = pl.ds(pl.multiple_of(i * 16, 16), 16)
        result[:, out_at, :] = summed.astype(BF16).reshape(HEADS, 16, KVL)
        log = (top * SCALE + jnp.log(total)).reshape(HEADS, 16, 1)
        spread = jnp.zeros((16, 128), F32)
        for head in range(HEADS):
            mine = (lax.bitwise_and(lane, 15) == head) & (lane < 48)
            spread = jnp.where(mine, log[head], spread)
        logs[out_at, :] = spread

    def body(i, carry):
        for k in range(2):
            pltpu.make_async_copy(unit0, held.at[2 * i + k], sems.at[2 * i + k]).wait()
        for k in range(2):
            block(2 * i + k)
        return carry

    lax.fori_loop(0, count // 2, body, 0)


def early_kernel(*refs):
    units = refs[:EARLY]
    q_lat, q_rot, page_bit, result, logs, held, sems = refs[EARLY:]
    start_units(units, held, sems)
    attend_units(EARLY, 0, units[0], q_lat, q_rot, page_bit, held, sems, result, logs)


def pack_log(log):
    lane = iota(log.shape, 1)
    high = log.astype(BF16).astype(F32)
    rest = log - high
    middle = rest.astype(BF16).astype(F32)
    packed = jnp.where(lane < 16, high, jnp.where(lane < 32, middle, rest - middle))
    return jnp.where(lane < 48, packed, 0.0).astype(BF16)


def late_kernel(*refs):
    units = refs[:LATE]
    (
        place, q_lat, q_rot, page_bit, pick, partner, chosen, flags, early, early_logs, weights, v_swap,
        r0, r1, r2, r3, held, result, logs, whole, parts, sems, w_sems,
    ) = refs[LATE:]
    start_units(units, held, sems)
    copies = gather_weights(place, weights, v_swap, 1, whole, w_sems)
    attend_units(LATE, EARLY, units[0], q_lat, q_rot, page_bit, held, sems, result, logs)
    log = jnp.concatenate([early_logs[...], logs[...]], axis=0)
    other = (flags[:, :128] - 1.0) * (-LOW)
    rest = log
    for _ in range(3):
        part = rest.astype(BF16)
        rest = rest - part.astype(F32)
        other = other + dot(partner[...], part)
    top = jnp.maximum(log, other)
    mine = jnp.exp(log - top)
    both = mine + jnp.exp(other - top)
    weight = mine / both
    merged = top + jnp.log(both)
    for copy in copies:
        copy.wait()
    for head in range(HEADS):
        mixed = jnp.concatenate([early[head], result[head]], axis=0)
        part = dot(mixed, whole[head], LAST) * weight[:, head : head + 1]
        parts[:, head * VDIM : (head + 1) * VDIM] = part.astype(BF16)
    lane = iota((SLOTS, 128), 1)
    empty = jnp.where(lane < 16, LOW, 0.0)
    packed = dot(chosen[...], pack_log(merged))
    packed = jnp.where(flags[:, 128:] > 0.5, packed, empty).astype(BF16)
    for peer, out in enumerate((r0, r1, r2, r3)):
        rows = slice(peer * ROWS, (peer + 1) * ROWS)
        out[:, :OUT] = dot(pick[rows, :], parts[...]).astype(BF16)
        out[:, OUT:] = packed[rows]


def suffix_kernel(
    place, live, q_nope_in, q_rope_in, latent_in, rope_in, both, k_swap, v_swap,
    out, q_nope, q_rope, latent, rope, rope32, query32, rot32, result, logs, whole_k, whole_v,
    k_sems, v_sems, q_sems, lat_sems,
):
    q_copies = load_all([(q_nope_in, q_nope), (q_rope_in, q_rope), (rope_in, rope)], q_sems)
    k_copies = gather_weights(place, both, k_swap, 0, whole_k, k_sems)
    for i in range(ROWS // 8):
        pltpu.make_async_copy(latent_in.at[pl.ds(8 * i, 8)], latent.at[pl.ds(8 * i, 8)], lat_sems.at[i]).start()
    v_copies = gather_weights(place, both, v_swap, 1, whole_v, v_sems)
    for copy in q_copies:
        copy.wait()
    rope32[...] = rope[...].astype(F32)
    across = iota((ROWS, ROWS), 0) == iota((ROWS, ROWS), 1)
    length = jnp.sum(jnp.where(across, live[...].astype(F32), 0.0), axis=1, keepdims=True)
    for copy in k_copies:
        copy.wait()
    for head in range(HEADS):
        projected = dot(q_nope[:, head * NOPE : (head + 1) * NOPE], whole_k[head])
        query32[head] = projected.astype(BF16).astype(F32)
        rot32[head] = q_rope[:, head * ROPE : (head + 1) * ROPE].astype(F32)
    keys, pairs = 8 * SUF, 8 * SUF // 2
    key, pair = iota((keys, pairs), 0), iota((keys, pairs), 1)
    same = lax.shift_right_logical(key, 6) == lax.bitwise_and(pair, 7)
    first = 2 * lax.shift_right_logical(pair, 3)
    even = (same & (lax.bitwise_and(key, SUF - 1) == first)).astype(BF16)
    odd = (same & (lax.bitwise_and(key, SUF - 1) == first + 1)).astype(BF16)
    lane = iota((8, 128), 1)
    col, row = iota((8, keys), 1), iota((8, keys), 0)

    def block(i, live_rows):
        rows = pl.ds(pl.multiple_of(i * 8, 8), 8)
        query = query32[:, rows, :].reshape(HEADS * 8, KVL).astype(BF16)
        query_rot = rot32[:, rows, :].reshape(HEADS * 8, ROPE).astype(BF16)
        lat = latent[rows].reshape(keys, KVL)
        rot = rope32[rows, :]
        rot = jnp.concatenate([rot[:, 128 * j : 128 * j + 128] for j in range(SUF // 2)], axis=0).astype(BF16)
        rot_keys = (dot(even, rot[:, :ROPE]) + dot(odd, rot[:, ROPE:])).astype(BF16)
        scores = dot(query, lat, LAST) + dot(query_rot, rot_keys, LAST)
        seen = (lax.shift_right_logical(col, 6) == row) & (lax.bitwise_and(col, SUF - 1).astype(F32) < live_rows)
        bias = jnp.where(seen, 0.0, LOW)
        scores = (scores.reshape(HEADS, 8, keys) + bias[None]).reshape(HEADS * 8, keys)
        top = jnp.max(scores, axis=1, keepdims=True)
        raw = jnp.exp2((scores - top) * (SCALE * LOG2E))
        total = jnp.sum(raw, axis=1, keepdims=True)
        summed = dot(raw.astype(BF16), lat) * (1.0 / total)
        result[:, rows, :] = summed.reshape(HEADS, 8, KVL)
        log = (top * SCALE + jnp.log(total)).reshape(HEADS, 8, 1)
        spread = jnp.zeros((8, 128), F32)
        for head in range(HEADS):
            spread = jnp.where(lax.bitwise_and(lane, 15) == head, log[head], spread)
        logs[rows, :] = spread

    for i in range(0, ROWS // 8, 2):
        for k in range(2):
            at = latent.at[pl.ds(8 * (i + k), 8)]
            pltpu.make_async_copy(latent_in.at[pl.ds(8 * (i + k), 8)], at, lat_sems.at[i + k]).wait()
        for k in range(2):
            block(i + k, length[8 * (i + k) : 8 * (i + k) + 8])
    for copy in v_copies:
        copy.wait()
    for head in range(HEADS):
        part = dot(result[head].astype(BF16), whole_v[head], LAST)
        out[:, head * VDIM : (head + 1) * VDIM] = part.astype(BF16)
    out[:, OUT:] = pack_log(logs[...])


def final_kernel(own, r0, r1, r2, r3, out):
    gather = (
        (lax.bitwise_and(iota((128, 128), 0), 15) == iota((128, 128), 1)) & (iota((128, 128), 0) < 48)
    ).astype(BF16)
    parts = (own, r0, r1, r2, r3)
    logs = [dot(part[:, OUT:], gather) for part in parts]
    top = functools.reduce(jnp.maximum, logs)
    weights = [jnp.exp(log - top) for log in logs]
    total = 1.0 / functools.reduce(jnp.add, weights)
    weights = [w * total for w in weights]
    for head in range(HEADS):
        at = slice(head * VDIM, (head + 1) * VDIM)
        scaled = [part[:, at].astype(F32) * weight[:, head : head + 1] for part, weight in zip(parts, weights)]
        out[:, at] = functools.reduce(jnp.add, scaled).astype(BF16)


def row_of(z, x, c):
    return ((z % NZ) * NX + x % NX) * NC + c


CHIPS = [(z, x, c) for z in range(NZ) for x in range(NX) for c in range(NC)]


def ring_z(a):
    return lax.ppermute(a, "rows", [(row_of(z, x, c), row_of(z + 1 - 2 * c, x, c)) for z, x, c in CHIPS])


def ring_x(a, steps=1):
    return lax.ppermute(a, "rows", [(row_of(z, x, c), row_of(z, x + steps * (1 - 2 * c), c)) for z, x, c in CHIPS])


def back_x(a, steps=1):
    return ring_x(a, -steps)


def swap(a):
    return lax.ppermute(a, "rows", [(row_of(z, x, c), row_of(z, x, 1 - c)) for z, x, c in CHIPS])


def cost(us):
    return pl.CostEstimate(flops=int(us * 1e6), bytes_accessed=int(us * 3.0e6), transcendentals=0)


def struct(*shape, dtype=BF16):
    return jax.ShapeDtypeStruct(shape, dtype)


def shards(
    q_nope, q_rope, w_uk, w_uv, prefix_latent, prefix_rope, suffix_latent, suffix_rope, page_slot, page_pattern, suffix_len
):
    row, y = lax.axis_index("rows"), lax.axis_index("proj")
    place = jnp.stack([row // (NX * NC), row // NC % NX, row % NC, y]).astype(I32)

    def exchange(a):
        return lax.all_to_all(a, "proj", split_axis=0, concat_axis=0, tiled=True)

    def after(a, *others):
        return lax.optimization_barrier((a, *others))[0]

    pages, pay, both = pl.pallas_call(
        pack_kernel,
        out_shape=(struct(2, UNIT, KVL), struct(ROWS, PAY), struct(NY * HEADS, NOPE, 128)),
        in_specs=[VMEM] * 2 + [HBM] * 6,
        out_specs=(VMEM,) * 3,
        scratch_shapes=[pltpu.VMEM((2, PAGE * ROPE), BF16), pltpu.SemaphoreType.DMA((4 + 2 * NY,))],
        compiler_params=params(60),
        cost_estimate=cost(2),
        name="pack",
    )(page_pattern.T, page_slot.reshape(1, -1), prefix_rope, prefix_latent, q_nope, q_rope, w_uk, w_uv)
    both = exchange(both)

    a, b = [pages], [swap(pages)]
    a_pay, b_pay = [pay], [swap(pay)]
    a.append(ring_z(a[0]))
    a_pay.append(ring_x(pay))
    b.append(ring_z(b[0]))
    b_pay.append(ring_x(b_pay[0]))
    a.append(ring_z(after(a[1], a_pay[1])))
    a_pay.append(ring_x(after(a_pay[1], a[1])))
    b.append(ring_z(after(b[1], b_pay[1])))
    pays = [pay, a_pay[1], a_pay[2], swap(b_pay[1])]
    a.append(ring_z(after(a[2], b[1], b_pay[1])))
    b.append(ring_z(b[2]))
    a_swap, b_swap = [None, swap(a[1])], [None, swap(b[1])]
    square = (SLOTS, SLOTS)
    q_slots, q_rot, page_bit, *ties = pl.pallas_call(
        gather_kernel,
        out_shape=(
            struct(SLOTS, QN), struct(HEADS, SLOTS, ROPE), struct(SLOTS, 128, dtype=F32),
            struct(*square), struct(*square), struct(*square), struct(*square, dtype=F32),
        ),
        in_specs=[SMEM] + [VMEM] * 4,
        out_specs=(VMEM,) * 7,
        scratch_shapes=[pltpu.VMEM(square, BF16)],
        compiler_params=params(60),
        cost_estimate=cost(3),
        name="gather",
    )(place, after(pays[0], a_swap[1], b_swap[1]), *pays[1:])

    split = both.reshape(NY, HEADS, NOPE, 128)
    k_part, v_part = split[:, : HEADS // 2], split[:, HEADS // 2 :]
    k_swap = swap(after(k_part.reshape(NY * HEADS // 2, NOPE, 128), a[3], b[2], q_slots))
    v_swap = swap(v_part.reshape(NY * HEADS // 2, NOPE, 128))

    q_lat = pl.pallas_call(
        query_kernel,
        out_shape=struct(HEADS, SLOTS, KVL),
        in_specs=[SMEM, VMEM] + [ANY] * 2,
        out_specs=VMEM,
        scratch_shapes=[pltpu.VMEM((HEADS, NOPE, KVL), BF16), pltpu.SemaphoreType.DMA((8,))],
        compiler_params=params(20),
        cost_estimate=cost(3),
        name="queries",
    )(place, q_slots, both, k_swap)

    a.append(ring_z(after(a[3], b[2], a_pay[2])))
    a_swap += [swap(a[2]), swap(a[3])]
    b_swap.append(swap(b[2]))
    early_units = [a[0], b[0], a[1], b[1], a[2], b[2], b_swap[2], a_swap[2], b_swap[1], a_swap[1]]

    early, early_logs = pl.pallas_call(
        early_kernel,
        out_shape=(struct(HEADS, EARLY * 16, KVL), struct(EARLY * 16, 128, dtype=F32)),
        in_specs=[ANY] * EARLY + [VMEM] * 3,
        out_specs=(VMEM, VMEM),
        scratch_shapes=[pltpu.VMEM((EARLY, 2, UNIT, KVL), BF16), pltpu.SemaphoreType.DMA((EARLY,))],
        compiler_params=params(20),
        cost_estimate=cost(1),
        name="early_pages",
    )(*early_units, q_lat, q_rot, page_bit)

    a_swap.append(swap(after(a[4], early_logs)))
    b_swap.append(swap(after(b[3], early_logs)))
    late_units = [a[3], b[3], a[4], a_swap[4], b_swap[3], a_swap[3]]
    returns = pl.pallas_call(
        late_kernel,
        out_shape=(struct(ROWS, RET),) * 4,
        in_specs=[ANY] * LATE + [SMEM] + [VMEM] * 9 + [ANY] * 2,
        out_specs=(VMEM,) * 4,
        scratch_shapes=[
            pltpu.VMEM((LATE, 2, UNIT, KVL), BF16), pltpu.VMEM((HEADS, LATE * 16, KVL), BF16),
            pltpu.VMEM((LATE * 16, 128), F32), pltpu.VMEM((HEADS, VDIM, KVL), BF16), pltpu.VMEM((SLOTS, OUT), BF16),
            pltpu.SemaphoreType.DMA((LATE,)), pltpu.SemaphoreType.DMA((8,)),
        ],
        compiler_params=params(20),
        cost_estimate=cost(7),
        name="late_pages",
    )(*late_units, place, q_lat, q_rot, page_bit, *ties, early, early_logs, both, v_swap)

    backs = [returns[0], back_x(returns[1]), back_x(returns[2], 2), ring_x(returns[3])]
    k_swap, returns = lax.optimization_barrier((k_swap, returns))
    own = pl.pallas_call(
        suffix_kernel,
        out_shape=struct(ROWS, RET),
        in_specs=[SMEM, VMEM] + [HBM] * 4 + [ANY] * 3,
        out_specs=VMEM,
        scratch_shapes=[
            pltpu.VMEM((ROWS, QN), BF16), pltpu.VMEM((ROWS, QR), BF16),
            pltpu.VMEM((ROWS, SUF, KVL), BF16), pltpu.VMEM((ROWS, SUF * ROPE), BF16),
            pltpu.VMEM((ROWS, SUF * ROPE), F32), pltpu.VMEM((HEADS, ROWS, KVL), F32),
            pltpu.VMEM((HEADS, ROWS, ROPE), F32), pltpu.VMEM((HEADS, ROWS, KVL), F32), pltpu.VMEM((ROWS, 128), F32),
            pltpu.VMEM((HEADS, NOPE, KVL), BF16), pltpu.VMEM((HEADS, VDIM, KVL), BF16),
            pltpu.SemaphoreType.DMA((8,)), pltpu.SemaphoreType.DMA((8,)),
            pltpu.SemaphoreType.DMA((3,)), pltpu.SemaphoreType.DMA((8,)),
        ],
        compiler_params=params(34),
        cost_estimate=cost(8),
        name="suffix",
    )(place, suffix_len.reshape(1, -1), q_nope, q_rope, suffix_latent, suffix_rope, both, k_swap, v_swap)

    return pl.pallas_call(
        final_kernel,
        out_shape=struct(ROWS, OUT),
        in_specs=[VMEM] * 5,
        out_specs=VMEM,
        compiler_params=params(16),
        cost_estimate=cost(2),
        name="combine",
    )(own, *backs)


def solution(mesh):
    return jax.shard_map(
        shards,
        mesh=mesh,
        in_specs=(
            P("rows", "proj"), P("rows", "proj"), P(None, None, "proj"), P(None, None, "proj"),
            P("rows", None, None), P("rows", None), P("rows", None, None), P("rows", None),
            P(), P("rows", None), P("rows"),
        ),
        out_specs=P("rows", "proj"),
        check_vma=False,
    )
```

```python
import functools

import jax
import jax.numpy as jnp
from jax import lax
from jax.experimental import pallas as pl
from jax.experimental.pallas import tpu as pltpu
from jax.sharding import PartitionSpec as P

F32, BF16, I32 = jnp.float32, jnp.bfloat16, jnp.int32
LOW = -1e30

NZ, NX, NC, NY = 8, 4, 2, 4
HEADS = 16
ROWS = 64
NOPE = 128
VDIM = 128
ROPE = 64
KVL = 512
PAGE = 128
SUF = 64
UNIT = PAGE + PAGE * ROPE // KVL
QN = HEADS * NOPE
QR = HEADS * ROPE
PAY = QN + QR + 128
SLOTS = 256
PAIRS = 16
EARLY = 10
LATE = PAIRS - EARLY
SCALE = (NOPE + ROPE) ** -0.5
OUT = HEADS * VDIM
RET = OUT + 128
LOG2E = 1.4426950408889634
LAST = (((1,), (1,)), ((), ()))
FIRST = (((0,), (0,)), ((), ()))


def dot(a, b, dims=(((1,), (0,)), ((), ())), precision=None):
    return lax.dot_general(a, b, dims, preferred_element_type=F32, precision=precision)


def iota(shape, axis):
    return lax.broadcasted_iota(I32, shape, axis)


def params(mib):
    return pltpu.CompilerParams(vmem_limit_bytes=mib << 20)


VMEM = pl.BlockSpec(memory_space=pltpu.VMEM)
SMEM = pl.BlockSpec(memory_space=pltpu.SMEM)
ANY = pl.BlockSpec(memory_space=pl.ANY)
HBM = pl.BlockSpec(memory_space=pltpu.HBM)


def load_all(pairs, sems):
    copies = [pltpu.make_async_copy(src, dst, sems.at[i]) for i, (src, dst) in enumerate(pairs)]
    for copy in copies:
        copy.start()
    return copies


def pack_kernel(
    pattern, page_slot, rope_in, latent_in, q_nope, q_rope, w_uk, w_uv, pages, pay, weights, rope, sems
):
    core, heads = lax.rem(lax.axis_index("rows"), NC), HEADS // 2
    copies = load_all(
        [
            (rope_in, rope),
            (latent_in, pages.at[:, :PAGE, :]),
            (q_nope, pay.at[:, :QN]),
            (q_rope, pay.at[:, QN : QN + QR]),
        ]
        + [
            (full.at[pl.ds(to * HEADS + heads * core, heads)], weights.at[pl.ds((2 * to + i) * heads, heads)])
            for i, full in enumerate((w_uk, w_uv))
            for to in range(NY)
        ],
        sems,
    )
    copies[0].wait()
    flat = rope[...].astype(F32)
    half = PAGE // 2
    sub = iota((8, 128), 0)
    even = (iota((half, PAGE), 1) == 2 * iota((half, PAGE), 0)).astype(F32)
    odd = (iota((half, PAGE), 1) == 2 * iota((half, PAGE), 0) + 1).astype(F32)
    for page in range(2):
        tiles = []
        for tile in range(half // 8):
            piece = jnp.zeros((8, 128), F32)
            for row in range(8):
                at = (tile * 8 + row) * 128
                piece = jnp.where(sub == row, flat[page : page + 1, at : at + 128], piece)
            tiles.append(piece)
        two_tokens = jnp.concatenate(tiles, axis=0)
        turned = dot(two_tokens[:, :ROPE], even, FIRST) + dot(two_tokens[:, ROPE:], odd, FIRST)
        turned = jnp.concatenate([turned[16 * i : 16 * i + 16] for i in range(4)], axis=1)
        pages[page, PAGE:, :] = turned.astype(BF16)
    lane = iota((ROWS, 128), 1)
    across = iota((ROWS, ROWS), 0) == iota((ROWS, ROWS), 1)
    slot_row = page_slot[...].astype(F32)
    slots, owners = [], []
    for k in range(2):
        names = pattern[k : k + 1, :].astype(F32)
        names = jnp.sum(jnp.where(across, names, 0.0), axis=1, keepdims=True).astype(I32)
        named = lane == names
        slot = jnp.sum(jnp.where(named, slot_row, 0.0), axis=1, keepdims=True)
        slots.append(slot)
        owners.append((lane == lax.shift_right_logical(slot.astype(I32), 1)).astype(F32))
    below = (iota((ROWS, ROWS), 0) > iota((ROWS, ROWS), 1)).astype(F32)
    before0 = dot(below, owners[0])
    before1 = dot(below, owners[1]) + jnp.sum(owners[0], axis=0, keepdims=True)
    rank0 = jnp.sum(owners[0] * before0, axis=1, keepdims=True)
    rank1 = jnp.sum(owners[1] * before1, axis=1, keepdims=True)
    code = jnp.zeros((ROWS, 128), F32)
    for at, value in enumerate((slots[0], slots[1], rank0, rank1)):
        code = jnp.where(lane == at, value, code)
    pay[:, QN + QR :] = code.astype(BF16)
    for copy in copies[1:]:
        copy.wait()


def gather_weights(place, both, half_swap, second, whole, sems):
    core, heads = place[2], HEADS // 2
    pairs = []
    for which, part in ((core, both), (1 - core, half_swap)):
        for y in range(NY):
            to = whole.at[pl.ds(which * heads, heads), :, y * 128 : (y + 1) * 128]
            at = (2 * y + second) * heads if part is both else y * heads
            pairs.append((part.at[pl.ds(at, heads)], to))
    return load_all(pairs, sems)


def gather_kernel(
    place, p0, p1, p2, p3, q_nope, q_rot, page_bit, pick_out, partner_out, chosen_out, flags, turned
):
    z, x, core = place[0], place[1], place[2]
    pays = (p0, p1, p2, p3)
    missing = []
    lane = iota((ROWS, 128), 1)
    wide = iota((ROWS, SLOTS), 1)
    picks, bits, places = ([], []), ([], []), []
    for peer, part in enumerate(pays):
        code = part[:, QN + QR :].astype(F32)
        columns = [
            jnp.sum(jnp.where(lane == at, code, 0.0), axis=1, keepdims=True).astype(I32) for at in range(4)
        ]
        found = []
        for k in range(2):
            slot, rank = columns[k], columns[2 + k]
            away = (z - lax.shift_right_logical(slot, 4)) * (1 - 2 * core)
            away = lax.bitwise_and(away, NZ - 1)
            order = jnp.where(away < 3, away, jnp.where(away >= 6, away - 3, away + 2))
            other = jnp.where(lax.bitwise_and(lax.shift_right_logical(slot, 1), 1) != core, 1, 0)
            here = lax.bitwise_and(lax.shift_right_logical(slot, 2), 3) == x
            at = jnp.where(here, (order * 2 + other) * 16 + peer * 4 + rank, -1)
            picks[k].append((wide == at).astype(F32))
            bits[k].append(lax.bitwise_and(slot, 1).astype(F32) * jnp.ones((1, 128), F32))
            found.append(jnp.where(here, 1.0, 0.0))
        missing.append(jnp.concatenate(found, axis=1))
    pick = [jnp.concatenate(p, axis=0) for p in picks]
    bit = [jnp.concatenate(b, axis=0) for b in bits]
    page_bit[...] = dot(pick[0], bit[0], FIRST) + dot(pick[1], bit[1], FIRST)
    turned[...] = jnp.transpose(pick[0] + pick[1]).astype(BF16)
    pick_out[...] = (pick[0] + pick[1]).astype(BF16)
    pair = dot(pick[0], pick[1], FIRST) + dot(pick[1], pick[0], FIRST)
    partner_out[...] = pair.astype(BF16)
    found = jnp.concatenate(missing, axis=0)
    chosen_out[...] = (pick[0] + pick[1] * (1.0 - found[:, 0:1])).astype(BF16)
    flags[:, :128] = jnp.sum(pair, axis=1, keepdims=True) * jnp.ones((1, 128), F32)
    flags[:, 128:] = jnp.maximum(found[:, 0:1], found[:, 1:2]) * jnp.ones((1, 128), F32)

    def two_heads(i, carry):
        rot = pl.ds(pl.multiple_of(QN + i * 128, 128), 128)
        gathered = dot(turned[...], jnp.concatenate([p[:, rot] for p in pays], axis=0)).astype(BF16)
        at = pl.ds(pl.multiple_of(i * 2 * NOPE, 128), 2 * NOPE)
        q_nope[:, at] = dot(turned[...], jnp.concatenate([p[:, at] for p in pays], axis=0)).astype(BF16)
        for k in range(2):
            q_rot[2 * i + k] = gathered[:, k * ROPE : (k + 1) * ROPE]
        return carry

    lax.fori_loop(0, HEADS // 2, two_heads, 0)


def query_kernel(place, q_nope, both, k_swap, q_lat, whole, sems):
    for copy in gather_weights(place, both, k_swap, 0, whole, sems):
        copy.wait()

    def two_heads(i, carry):
        left = q_nope[:, pl.ds(pl.multiple_of(i * 2 * NOPE, 128), 2 * NOPE)]
        for k in range(2):
            q_lat[2 * i + k] = dot(left[:, k * NOPE : (k + 1) * NOPE], whole[2 * i + k]).astype(BF16)
        return carry

    lax.fori_loop(0, HEADS // 2, two_heads, 0)


def start_units(units, held, sems):
    copies = [pltpu.make_async_copy(unit, held.at[i], sems.at[i]) for i, unit in enumerate(units)]
    for copy in copies:
        copy.start()


def attend_units(count, base, unit0, q_lat, q_rot, page_bit, held, sems, result, logs):
    lane = iota((16, 128), 1)

    def block(i):
        unit = held.at[i]
        latent = unit[:, :PAGE, :].reshape(2 * PAGE, KVL)
        rot = unit[:, PAGE:, :]
        keys = jnp.concatenate(
            [
                jnp.concatenate([rot[page, :, 128 * j : 128 * j + 128] for j in range(4)], axis=0)
                for page in range(2)
            ],
            axis=1,
        )
        at = pl.ds(pl.multiple_of((base + i) * 16, 16), 16)
        query = q_lat[:, at, :].reshape(HEADS * 16, KVL)
        query_rot = q_rot[:, at, :].reshape(HEADS * 16, ROPE)
        scores = dot(query, latent, LAST) + dot(query_rot, keys)
        bit = page_bit[at, :]
        bias = jnp.concatenate(
            [jnp.where(bit < 0.5, 0.0, LOW), jnp.where(bit < 0.5, LOW, 0.0)], axis=1
        )
        scores = (scores.reshape(HEADS, 16, 2 * PAGE) + bias[None]).reshape(HEADS * 16, 2 * PAGE)
        top = jnp.max(scores, axis=1, keepdims=True)
        raw = jnp.exp2((scores - top) * (SCALE * LOG2E))
        total = jnp.sum(raw, axis=1, keepdims=True)
        summed = dot(raw.astype(BF16), latent) * (1.0 / total)
        out_at = pl.ds(pl.multiple_of(i * 16, 16), 16)
        result[:, out_at, :] = summed.astype(BF16).reshape(HEADS, 16, KVL)
        log = (top * SCALE + jnp.log(total)).reshape(HEADS, 16, 1)
        spread = jnp.zeros((16, 128), F32)
        for head in range(HEADS):
            mine = (lax.bitwise_and(lane, 15) == head) & (lane < 48)
            spread = jnp.where(mine, log[head], spread)
        logs[out_at, :] = spread

    def body(i, carry):
        for k in range(2):
            pltpu.make_async_copy(unit0, held.at[2 * i + k], sems.at[2 * i + k]).wait()
        for k in range(2):
            block(2 * i + k)
        return carry

    lax.fori_loop(0, count // 2, body, 0)


def early_kernel(*refs):
    units = refs[:EARLY]
    q_lat, q_rot, page_bit, result, logs, held, sems = refs[EARLY:]
    start_units(units, held, sems)
    attend_units(EARLY, 0, units[0], q_lat, q_rot, page_bit, held, sems, result, logs)


def pack_log(log):
    lane = iota(log.shape, 1)
    high = log.astype(BF16).astype(F32)
    rest = log - high
    middle = rest.astype(BF16).astype(F32)
    packed = jnp.where(lane < 16, high, jnp.where(lane < 32, middle, rest - middle))
    return jnp.where(lane < 48, packed, 0.0).astype(BF16)


def late_kernel(*refs):
    units = refs[:LATE]
    (
        place, q_lat, q_rot, page_bit, pick, partner, chosen, flags, early, early_logs, weights, v_swap,
        r0, r1, r2, r3, held, result, logs, whole, parts, sems, w_sems,
    ) = refs[LATE:]
    start_units(units, held, sems)
    copies = gather_weights(place, weights, v_swap, 1, whole, w_sems)
    attend_units(LATE, EARLY, units[0], q_lat, q_rot, page_bit, held, sems, result, logs)
    log = jnp.concatenate([early_logs[...], logs[...]], axis=0)
    other = (flags[:, :128] - 1.0) * (-LOW)
    rest = log
    for _ in range(3):
        part = rest.astype(BF16)
        rest = rest - part.astype(F32)
        other = other + dot(partner[...], part)
    top = jnp.maximum(log, other)
    mine = jnp.exp(log - top)
    both = mine + jnp.exp(other - top)
    weight = mine / both
    merged = top + jnp.log(both)
    for copy in copies:
        copy.wait()
    for head in range(HEADS):
        mixed = jnp.concatenate([early[head], result[head]], axis=0)
        part = dot(mixed, whole[head], LAST) * weight[:, head : head + 1]
        parts[:, head * VDIM : (head + 1) * VDIM] = part.astype(BF16)
    lane = iota((SLOTS, 128), 1)
    empty = jnp.where(lane < 16, LOW, 0.0)
    packed = dot(chosen[...], pack_log(merged))
    packed = jnp.where(flags[:, 128:] > 0.5, packed, empty).astype(BF16)
    for peer, out in enumerate((r0, r1, r2, r3)):
        rows = slice(peer * ROWS, (peer + 1) * ROWS)
        out[:, :OUT] = dot(pick[rows, :], parts[...]).astype(BF16)
        out[:, OUT:] = packed[rows]


def suffix_kernel(
    place, live, q_nope_in, q_rope_in, latent_in, rope_in, both, k_swap, v_swap,
    out, q_nope, q_rope, latent, rope, rope32, query32, rot32, result, logs, whole_k, whole_v,
    k_sems, v_sems, q_sems, lat_sems,
):
    q_copies = load_all([(q_nope_in, q_nope), (q_rope_in, q_rope), (rope_in, rope)], q_sems)
    k_copies = gather_weights(place, both, k_swap, 0, whole_k, k_sems)
    for i in range(ROWS // 8):
        pltpu.make_async_copy(latent_in.at[pl.ds(8 * i, 8)], latent.at[pl.ds(8 * i, 8)], lat_sems.at[i]).start()
    v_copies = gather_weights(place, both, v_swap, 1, whole_v, v_sems)
    for copy in q_copies:
        copy.wait()
    rope32[...] = rope[...].astype(F32)
    across = iota((ROWS, ROWS), 0) == iota((ROWS, ROWS), 1)
    length = jnp.sum(jnp.where(across, live[...].astype(F32), 0.0), axis=1, keepdims=True)
    for copy in k_copies:
        copy.wait()
    for head in range(HEADS):
        projected = dot(q_nope[:, head * NOPE : (head + 1) * NOPE], whole_k[head])
        query32[head] = projected.astype(BF16).astype(F32)
        rot32[head] = q_rope[:, head * ROPE : (head + 1) * ROPE].astype(F32)
    keys, pairs = 8 * SUF, 8 * SUF // 2
    key, pair = iota((keys, pairs), 0), iota((keys, pairs), 1)
    same = lax.shift_right_logical(key, 6) == lax.bitwise_and(pair, 7)
    first = 2 * lax.shift_right_logical(pair, 3)
    even = (same & (lax.bitwise_and(key, SUF - 1) == first)).astype(BF16)
    odd = (same & (lax.bitwise_and(key, SUF - 1) == first + 1)).astype(BF16)
    lane = iota((8, 128), 1)
    col, row = iota((8, keys), 1), iota((8, keys), 0)

    def block(i, live_rows):
        rows = pl.ds(pl.multiple_of(i * 8, 8), 8)
        query = query32[:, rows, :].reshape(HEADS * 8, KVL).astype(BF16)
        query_rot = rot32[:, rows, :].reshape(HEADS * 8, ROPE).astype(BF16)
        lat = latent[rows].reshape(keys, KVL)
        rot = rope32[rows, :]
        rot = jnp.concatenate([rot[:, 128 * j : 128 * j + 128] for j in range(SUF // 2)], axis=0).astype(BF16)
        rot_keys = (dot(even, rot[:, :ROPE]) + dot(odd, rot[:, ROPE:])).astype(BF16)
        scores = dot(query, lat, LAST) + dot(query_rot, rot_keys, LAST)
        seen = (lax.shift_right_logical(col, 6) == row) & (lax.bitwise_and(col, SUF - 1).astype(F32) < live_rows)
        bias = jnp.where(seen, 0.0, LOW)
        scores = (scores.reshape(HEADS, 8, keys) + bias[None]).reshape(HEADS * 8, keys)
        top = jnp.max(scores, axis=1, keepdims=True)
        raw = jnp.exp2((scores - top) * (SCALE * LOG2E))
        total = jnp.sum(raw, axis=1, keepdims=True)
        summed = dot(raw.astype(BF16), lat) * (1.0 / total)
        result[:, rows, :] = summed.reshape(HEADS, 8, KVL)
        log = (top * SCALE + jnp.log(total)).reshape(HEADS, 8, 1)
        spread = jnp.zeros((8, 128), F32)
        for head in range(HEADS):
            spread = jnp.where(lax.bitwise_and(lane, 15) == head, log[head], spread)
        logs[rows, :] = spread

    for i in range(0, ROWS // 8, 2):
        for k in range(2):
            at = latent.at[pl.ds(8 * (i + k), 8)]
            pltpu.make_async_copy(latent_in.at[pl.ds(8 * (i + k), 8)], at, lat_sems.at[i + k]).wait()
        for k in range(2):
            block(i + k, length[8 * (i + k) : 8 * (i + k) + 8])
    for copy in v_copies:
        copy.wait()
    for head in range(HEADS):
        part = dot(result[head].astype(BF16), whole_v[head], LAST)
        out[:, head * VDIM : (head + 1) * VDIM] = part.astype(BF16)
    out[:, OUT:] = pack_log(logs[...])


def final_kernel(own, r0, r1, r2, r3, out):
    gather = (
        (lax.bitwise_and(iota((128, 128), 0), 15) == iota((128, 128), 1)) & (iota((128, 128), 0) < 48)
    ).astype(BF16)
    parts = (own, r0, r1, r2, r3)
    logs = [dot(part[:, OUT:], gather) for part in parts]
    top = functools.reduce(jnp.maximum, logs)
    weights = [jnp.exp(log - top) for log in logs]
    total = 1.0 / functools.reduce(jnp.add, weights)
    weights = [w * total for w in weights]
    for head in range(HEADS):
        at = slice(head * VDIM, (head + 1) * VDIM)
        scaled = [part[:, at].astype(F32) * weight[:, head : head + 1] for part, weight in zip(parts, weights)]
        out[:, at] = functools.reduce(jnp.add, scaled).astype(BF16)


def row_of(z, x, c):
    return ((z % NZ) * NX + x % NX) * NC + c


CHIPS = [(z, x, c) for z in range(NZ) for x in range(NX) for c in range(NC)]


def ring_z(a):
    return lax.ppermute(a, "rows", [(row_of(z, x, c), row_of(z + 1 - 2 * c, x, c)) for z, x, c in CHIPS])


def ring_x(a, steps=1):
    return lax.ppermute(a, "rows", [(row_of(z, x, c), row_of(z, x + steps * (1 - 2 * c), c)) for z, x, c in CHIPS])


def back_x(a, steps=1):
    return ring_x(a, -steps)


def swap(a):
    return lax.ppermute(a, "rows", [(row_of(z, x, c), row_of(z, x, 1 - c)) for z, x, c in CHIPS])


def cost(us):
    return pl.CostEstimate(flops=int(us * 1e6), bytes_accessed=int(us * 3.0e6), transcendentals=0)


def struct(*shape, dtype=BF16):
    return jax.ShapeDtypeStruct(shape, dtype)


def shards(
    q_nope, q_rope, w_uk, w_uv, prefix_latent, prefix_rope, suffix_latent, suffix_rope, page_slot, page_pattern, suffix_len
):
    row, y = lax.axis_index("rows"), lax.axis_index("proj")
    place = jnp.stack([row // (NX * NC), row // NC % NX, row % NC, y]).astype(I32)

    def exchange(a):
        return lax.all_to_all(a, "proj", split_axis=0, concat_axis=0, tiled=True)

    def after(a, *others):
        return lax.optimization_barrier((a, *others))[0]

    pages, pay, both = pl.pallas_call(
        pack_kernel,
        out_shape=(struct(2, UNIT, KVL), struct(ROWS, PAY), struct(NY * HEADS, NOPE, 128)),
        in_specs=[VMEM] * 2 + [HBM] * 6,
        out_specs=(VMEM,) * 3,
        scratch_shapes=[pltpu.VMEM((2, PAGE * ROPE), BF16), pltpu.SemaphoreType.DMA((4 + 2 * NY,))],
        compiler_params=params(60),
        cost_estimate=cost(2),
        name="pack",
    )(page_pattern.T, page_slot.reshape(1, -1), prefix_rope, prefix_latent, q_nope, q_rope, w_uk, w_uv)
    both = exchange(both)

    a, b = [pages], [swap(pages)]
    a_pay, b_pay = [pay], [swap(pay)]
    a.append(ring_z(a[0]))
    a_pay.append(ring_x(pay))
    b.append(ring_z(b[0]))
    b_pay.append(ring_x(b_pay[0]))
    a.append(ring_z(after(a[1], a_pay[1])))
    a_pay.append(ring_x(after(a_pay[1], a[1])))
    b.append(ring_z(after(b[1], b_pay[1])))
    pays = [pay, a_pay[1], a_pay[2], swap(b_pay[1])]
    a.append(ring_z(after(a[2], b[1], b_pay[1])))
    b.append(ring_z(b[2]))
    a_swap, b_swap = [None, swap(a[1])], [None, swap(b[1])]
    square = (SLOTS, SLOTS)
    q_slots, q_rot, page_bit, *ties = pl.pallas_call(
        gather_kernel,
        out_shape=(
            struct(SLOTS, QN), struct(HEADS, SLOTS, ROPE), struct(SLOTS, 128, dtype=F32),
            struct(*square), struct(*square), struct(*square), struct(*square, dtype=F32),
        ),
        in_specs=[SMEM] + [VMEM] * 4,
        out_specs=(VMEM,) * 7,
        scratch_shapes=[pltpu.VMEM(square, BF16)],
        compiler_params=params(60),
        cost_estimate=cost(3),
        name="gather",
    )(place, after(pays[0], a_swap[1], b_swap[1]), *pays[1:])

    split = both.reshape(NY, HEADS, NOPE, 128)
    k_part, v_part = split[:, : HEADS // 2], split[:, HEADS // 2 :]
    k_swap = swap(after(k_part.reshape(NY * HEADS // 2, NOPE, 128), a[3], q_slots))
    v_swap = swap(v_part.reshape(NY * HEADS // 2, NOPE, 128))

    q_lat = pl.pallas_call(
        query_kernel,
        out_shape=struct(HEADS, SLOTS, KVL),
        in_specs=[SMEM, VMEM] + [ANY] * 2,
        out_specs=VMEM,
        scratch_shapes=[pltpu.VMEM((HEADS, NOPE, KVL), BF16), pltpu.SemaphoreType.DMA((8,))],
        compiler_params=params(20),
        cost_estimate=cost(3),
        name="queries",
    )(place, q_slots, both, k_swap)

    a.append(ring_z(after(a[3], b[2], a_pay[2])))
    a_swap += [swap(a[2]), swap(a[3])]
    b_swap.append(swap(b[2]))
    early_units = [a[0], b[0], a[1], b[1], a[2], b[2], b_swap[2], a_swap[2], b_swap[1], a_swap[1]]

    early, early_logs = pl.pallas_call(
        early_kernel,
        out_shape=(struct(HEADS, EARLY * 16, KVL), struct(EARLY * 16, 128, dtype=F32)),
        in_specs=[ANY] * EARLY + [VMEM] * 3,
        out_specs=(VMEM, VMEM),
        scratch_shapes=[pltpu.VMEM((EARLY, 2, UNIT, KVL), BF16), pltpu.SemaphoreType.DMA((EARLY,))],
        compiler_params=params(20),
        cost_estimate=cost(1),
        name="early_pages",
    )(*early_units, q_lat, q_rot, page_bit)

    a_swap.append(swap(after(a[4], early_logs)))
    b_swap.append(swap(after(b[3], early_logs)))
    late_units = [a[3], b[3], a[4], a_swap[4], b_swap[3], a_swap[3]]
    returns = pl.pallas_call(
        late_kernel,
        out_shape=(struct(ROWS, RET),) * 4,
        in_specs=[ANY] * LATE + [SMEM] + [VMEM] * 9 + [ANY] * 2,
        out_specs=(VMEM,) * 4,
        scratch_shapes=[
            pltpu.VMEM((LATE, 2, UNIT, KVL), BF16), pltpu.VMEM((HEADS, LATE * 16, KVL), BF16),
            pltpu.VMEM((LATE * 16, 128), F32), pltpu.VMEM((HEADS, VDIM, KVL), BF16), pltpu.VMEM((SLOTS, OUT), BF16),
            pltpu.SemaphoreType.DMA((LATE,)), pltpu.SemaphoreType.DMA((8,)),
        ],
        compiler_params=params(20),
        cost_estimate=cost(7),
        name="late_pages",
    )(*late_units, place, q_lat, q_rot, page_bit, *ties, early, early_logs, both, v_swap)

    backs = [returns[0], back_x(returns[1]), back_x(returns[2], 2), ring_x(returns[3])]
    k_swap, returns = lax.optimization_barrier((k_swap, returns))
    own = pl.pallas_call(
        suffix_kernel,
        out_shape=struct(ROWS, RET),
        in_specs=[SMEM, VMEM] + [HBM] * 4 + [ANY] * 3,
        out_specs=VMEM,
        scratch_shapes=[
            pltpu.VMEM((ROWS, QN), BF16), pltpu.VMEM((ROWS, QR), BF16),
            pltpu.VMEM((ROWS, SUF, KVL), BF16), pltpu.VMEM((ROWS, SUF * ROPE), BF16),
            pltpu.VMEM((ROWS, SUF * ROPE), F32), pltpu.VMEM((HEADS, ROWS, KVL), F32),
            pltpu.VMEM((HEADS, ROWS, ROPE), F32), pltpu.VMEM((HEADS, ROWS, KVL), F32), pltpu.VMEM((ROWS, 128), F32),
            pltpu.VMEM((HEADS, NOPE, KVL), BF16), pltpu.VMEM((HEADS, VDIM, KVL), BF16),
            pltpu.SemaphoreType.DMA((8,)), pltpu.SemaphoreType.DMA((8,)),
            pltpu.SemaphoreType.DMA((3,)), pltpu.SemaphoreType.DMA((8,)),
        ],
        compiler_params=params(34),
        cost_estimate=cost(8),
        name="suffix",
    )(place, suffix_len.reshape(1, -1), q_nope, q_rope, suffix_latent, suffix_rope, both, k_swap, v_swap)

    return pl.pallas_call(
        final_kernel,
        out_shape=struct(ROWS, OUT),
        in_specs=[VMEM] * 5,
        out_specs=VMEM,
        compiler_params=params(16),
        cost_estimate=cost(2),
        name="combine",
    )(own, *backs)


def solution(mesh):
    return jax.shard_map(
        shards,
        mesh=mesh,
        in_specs=(
            P("rows", "proj"), P("rows", "proj"), P(None, None, "proj"), P(None, None, "proj"),
            P("rows", None, None), P("rows", None), P("rows", None, None), P("rows", None),
            P(), P("rows", None), P("rows"),
        ),
        out_specs=P("rows", "proj"),
        check_vma=False,
    )
```

```python
import functools

import jax
import jax.numpy as jnp
from jax import lax
from jax.experimental import pallas as pl
from jax.experimental.pallas import tpu as pltpu
from jax.sharding import PartitionSpec as P

F32, BF16, I32 = jnp.float32, jnp.bfloat16, jnp.int32
LOW = -1e30

NZ, NX, NC, NY = 8, 4, 2, 4
HEADS = 16
ROWS = 64
NOPE = 128
VDIM = 128
ROPE = 64
KVL = 512
PAGE = 128
SUF = 64
UNIT = PAGE + PAGE * ROPE // KVL
QN = HEADS * NOPE
QR = HEADS * ROPE
PAY = QN + QR + 128
SLOTS = 256
PAIRS = 16
EARLY = 10
MID = 4
LATE = PAIRS - EARLY - MID
SCALE = (NOPE + ROPE) ** -0.5
OUT = HEADS * VDIM
RET = OUT + 128
LOG2E = 1.4426950408889634
LAST = (((1,), (1,)), ((), ()))
FIRST = (((0,), (0,)), ((), ()))


def dot(a, b, dims=(((1,), (0,)), ((), ())), precision=None):
    return lax.dot_general(a, b, dims, preferred_element_type=F32, precision=precision)


def iota(shape, axis):
    return lax.broadcasted_iota(I32, shape, axis)


def params(mib):
    return pltpu.CompilerParams(vmem_limit_bytes=mib << 20)


VMEM = pl.BlockSpec(memory_space=pltpu.VMEM)
SMEM = pl.BlockSpec(memory_space=pltpu.SMEM)
ANY = pl.BlockSpec(memory_space=pl.ANY)
HBM = pl.BlockSpec(memory_space=pltpu.HBM)


def load_all(pairs, sems):
    copies = [pltpu.make_async_copy(src, dst, sems.at[i]) for i, (src, dst) in enumerate(pairs)]
    for copy in copies:
        copy.start()
    return copies


def pack_kernel(
    pattern, page_slot, rope_in, latent_in, q_nope, q_rope, w_uk, w_uv, pages, pay, weights, rope, sems
):
    core, heads = lax.rem(lax.axis_index("rows"), NC), HEADS // 2
    copies = load_all(
        [
            (rope_in, rope),
            (latent_in, pages.at[:, :PAGE, :]),
            (q_nope, pay.at[:, :QN]),
            (q_rope, pay.at[:, QN : QN + QR]),
        ]
        + [
            (full.at[pl.ds(to * HEADS + heads * core, heads)], weights.at[pl.ds((2 * to + i) * heads, heads)])
            for i, full in enumerate((w_uk, w_uv))
            for to in range(NY)
        ],
        sems,
    )
    copies[0].wait()
    flat = rope[...].astype(F32)
    half = PAGE // 2
    sub = iota((8, 128), 0)
    even = (iota((half, PAGE), 1) == 2 * iota((half, PAGE), 0)).astype(F32)
    odd = (iota((half, PAGE), 1) == 2 * iota((half, PAGE), 0) + 1).astype(F32)
    for page in range(2):
        tiles = []
        for tile in range(half // 8):
            piece = jnp.zeros((8, 128), F32)
            for row in range(8):
                at = (tile * 8 + row) * 128
                piece = jnp.where(sub == row, flat[page : page + 1, at : at + 128], piece)
            tiles.append(piece)
        two_tokens = jnp.concatenate(tiles, axis=0)
        turned = dot(two_tokens[:, :ROPE], even, FIRST) + dot(two_tokens[:, ROPE:], odd, FIRST)
        turned = jnp.concatenate([turned[16 * i : 16 * i + 16] for i in range(4)], axis=1)
        pages[page, PAGE:, :] = turned.astype(BF16)
    lane = iota((ROWS, 128), 1)
    across = iota((ROWS, ROWS), 0) == iota((ROWS, ROWS), 1)
    slot_row = page_slot[...].astype(F32)
    slots, owners = [], []
    for k in range(2):
        names = pattern[k : k + 1, :].astype(F32)
        names = jnp.sum(jnp.where(across, names, 0.0), axis=1, keepdims=True).astype(I32)
        named = lane == names
        slot = jnp.sum(jnp.where(named, slot_row, 0.0), axis=1, keepdims=True)
        slots.append(slot)
        owners.append((lane == lax.shift_right_logical(slot.astype(I32), 1)).astype(F32))
    below = (iota((ROWS, ROWS), 0) > iota((ROWS, ROWS), 1)).astype(F32)
    before0 = dot(below, owners[0])
    before1 = dot(below, owners[1]) + jnp.sum(owners[0], axis=0, keepdims=True)
    rank0 = jnp.sum(owners[0] * before0, axis=1, keepdims=True)
    rank1 = jnp.sum(owners[1] * before1, axis=1, keepdims=True)
    code = jnp.zeros((ROWS, 128), F32)
    for at, value in enumerate((slots[0], slots[1], rank0, rank1)):
        code = jnp.where(lane == at, value, code)
    pay[:, QN + QR :] = code.astype(BF16)
    for copy in copies[1:]:
        copy.wait()


def gather_weights(place, both, half_swap, second, whole, sems):
    core, heads = place[2], HEADS // 2
    pairs = []
    for which, part in ((core, both), (1 - core, half_swap)):
        for y in range(NY):
            to = whole.at[pl.ds(which * heads, heads), :, y * 128 : (y + 1) * 128]
            at = (2 * y + second) * heads if part is both else y * heads
            pairs.append((part.at[pl.ds(at, heads)], to))
    return load_all(pairs, sems)


def gather_kernel(
    place, p0, p1, p2, p3, q_nope, q_rot, page_bit, pick_out, partner_out, chosen_out, flags, turned
):
    z, x, core = place[0], place[1], place[2]
    pays = (p0, p1, p2, p3)
    missing = []
    lane = iota((ROWS, 128), 1)
    wide = iota((ROWS, SLOTS), 1)
    picks, bits, places = ([], []), ([], []), []
    for peer, part in enumerate(pays):
        code = part[:, QN + QR :].astype(F32)
        columns = [
            jnp.sum(jnp.where(lane == at, code, 0.0), axis=1, keepdims=True).astype(I32) for at in range(4)
        ]
        found = []
        for k in range(2):
            slot, rank = columns[k], columns[2 + k]
            away = (z - lax.shift_right_logical(slot, 4)) * (1 - 2 * core)
            away = lax.bitwise_and(away, NZ - 1)
            order = jnp.where(away < 3, away, jnp.where(away >= 6, away - 3, away + 2))
            other = jnp.where(lax.bitwise_and(lax.shift_right_logical(slot, 1), 1) != core, 1, 0)
            here = lax.bitwise_and(lax.shift_right_logical(slot, 2), 3) == x
            order = order * 2 + other
            order = jnp.where(order == 13, 15, jnp.where(order == 15, 13, order))
            at = jnp.where(here, order * 16 + peer * 4 + rank, -1)
            picks[k].append((wide == at).astype(F32))
            bits[k].append(lax.bitwise_and(slot, 1).astype(F32) * jnp.ones((1, 128), F32))
            found.append(jnp.where(here, 1.0, 0.0))
        missing.append(jnp.concatenate(found, axis=1))
    pick = [jnp.concatenate(p, axis=0) for p in picks]
    bit = [jnp.concatenate(b, axis=0) for b in bits]
    page_bit[...] = dot(pick[0], bit[0], FIRST) + dot(pick[1], bit[1], FIRST)
    turned[...] = jnp.transpose(pick[0] + pick[1]).astype(BF16)
    pick_out[...] = (pick[0] + pick[1]).astype(BF16)
    pair = dot(pick[0], pick[1], FIRST) + dot(pick[1], pick[0], FIRST)
    partner_out[...] = pair.astype(BF16)
    found = jnp.concatenate(missing, axis=0)
    chosen_out[...] = (pick[0] + pick[1] * (1.0 - found[:, 0:1])).astype(BF16)
    flags[:, :128] = jnp.sum(pair, axis=1, keepdims=True) * jnp.ones((1, 128), F32)
    flags[:, 128:] = jnp.maximum(found[:, 0:1], found[:, 1:2]) * jnp.ones((1, 128), F32)

    def two_heads(i, carry):
        rot = pl.ds(pl.multiple_of(QN + i * 128, 128), 128)
        gathered = dot(turned[...], jnp.concatenate([p[:, rot] for p in pays], axis=0)).astype(BF16)
        at = pl.ds(pl.multiple_of(i * 2 * NOPE, 128), 2 * NOPE)
        q_nope[:, at] = dot(turned[...], jnp.concatenate([p[:, at] for p in pays], axis=0)).astype(BF16)
        for k in range(2):
            q_rot[2 * i + k] = gathered[:, k * ROPE : (k + 1) * ROPE]
        return carry

    lax.fori_loop(0, HEADS // 2, two_heads, 0)


def query_kernel(place, q_nope, both, k_swap, q_lat, whole, sems):
    for copy in gather_weights(place, both, k_swap, 0, whole, sems):
        copy.wait()

    def two_heads(i, carry):
        left = q_nope[:, pl.ds(pl.multiple_of(i * 2 * NOPE, 128), 2 * NOPE)]
        for k in range(2):
            q_lat[2 * i + k] = dot(left[:, k * NOPE : (k + 1) * NOPE], whole[2 * i + k]).astype(BF16)
        return carry

    lax.fori_loop(0, HEADS // 2, two_heads, 0)


def start_units(units, held, sems):
    copies = [pltpu.make_async_copy(unit, held.at[i], sems.at[i]) for i, unit in enumerate(units)]
    for copy in copies:
        copy.start()


def attend_units(count, base, unit0, q_lat, q_rot, page_bit, held, sems, result, logs):
    lane = iota((16, 128), 1)

    def block(i):
        unit = held.at[i]
        latent = unit[:, :PAGE, :].reshape(2 * PAGE, KVL)
        rot = unit[:, PAGE:, :]
        keys = jnp.concatenate(
            [
                jnp.concatenate([rot[page, :, 128 * j : 128 * j + 128] for j in range(4)], axis=0)
                for page in range(2)
            ],
            axis=1,
        )
        at = pl.ds(pl.multiple_of((base + i) * 16, 16), 16)
        query = q_lat[:, at, :].reshape(HEADS * 16, KVL)
        query_rot = q_rot[:, at, :].reshape(HEADS * 16, ROPE)
        scores = dot(query, latent, LAST) + dot(query_rot, keys)
        bit = page_bit[at, :]
        bias = jnp.concatenate(
            [jnp.where(bit < 0.5, 0.0, LOW), jnp.where(bit < 0.5, LOW, 0.0)], axis=1
        )
        scores = (scores.reshape(HEADS, 16, 2 * PAGE) + bias[None]).reshape(HEADS * 16, 2 * PAGE)
        top = jnp.max(scores, axis=1, keepdims=True)
        raw = jnp.exp2((scores - top) * (SCALE * LOG2E))
        total = jnp.sum(raw, axis=1, keepdims=True)
        summed = dot(raw.astype(BF16), latent) * (1.0 / total)
        out_at = pl.ds(pl.multiple_of(i * 16, 16), 16)
        result[:, out_at, :] = summed.astype(BF16).reshape(HEADS, 16, KVL)
        log = (top * SCALE + jnp.log(total)).reshape(HEADS, 16, 1)
        spread = jnp.zeros((16, 128), F32)
        for head in range(HEADS):
            mine = (lax.bitwise_and(lane, 15) == head) & (lane < 48)
            spread = jnp.where(mine, log[head], spread)
        logs[out_at, :] = spread

    def body(i, carry):
        for k in range(2):
            pltpu.make_async_copy(unit0, held.at[2 * i + k], sems.at[2 * i + k]).wait()
        for k in range(2):
            block(2 * i + k)
        return carry

    lax.fori_loop(0, count // 2, body, 0)


def units_kernel(count, base, *refs):
    units = refs[:count]
    q_lat, q_rot, page_bit, result, logs, held, sems = refs[count:]
    start_units(units, held, sems)
    attend_units(count, base, units[0], q_lat, q_rot, page_bit, held, sems, result, logs)


def pack_log(log):
    lane = iota(log.shape, 1)
    high = log.astype(BF16).astype(F32)
    rest = log - high
    middle = rest.astype(BF16).astype(F32)
    packed = jnp.where(lane < 16, high, jnp.where(lane < 32, middle, rest - middle))
    return jnp.where(lane < 48, packed, 0.0).astype(BF16)


def late_kernel(*refs):
    units = refs[:LATE]
    (
        place, q_lat, q_rot, page_bit, pick, partner, chosen, flags, early, early_logs, mid, mid_logs, weights, v_swap,
        r0, r1, r2, r3, held, result, logs, whole, parts, sems, w_sems,
    ) = refs[LATE:]
    start_units(units, held, sems)
    copies = gather_weights(place, weights, v_swap, 1, whole, w_sems)
    attend_units(LATE, EARLY + MID, units[0], q_lat, q_rot, page_bit, held, sems, result, logs)
    log = jnp.concatenate([early_logs[...], mid_logs[...], logs[...]], axis=0)
    other = (flags[:, :128] - 1.0) * (-LOW)
    rest = log
    for _ in range(3):
        part = rest.astype(BF16)
        rest = rest - part.astype(F32)
        other = other + dot(partner[...], part)
    top = jnp.maximum(log, other)
    mine = jnp.exp(log - top)
    both = mine + jnp.exp(other - top)
    weight = mine / both
    merged = top + jnp.log(both)
    for copy in copies:
        copy.wait()
    for head in range(HEADS):
        mixed = jnp.concatenate([early[head], mid[head], result[head]], axis=0)
        part = dot(mixed, whole[head], LAST) * weight[:, head : head + 1]
        parts[:, head * VDIM : (head + 1) * VDIM] = part.astype(BF16)
    lane = iota((SLOTS, 128), 1)
    empty = jnp.where(lane < 16, LOW, 0.0)
    packed = dot(chosen[...], pack_log(merged))
    packed = jnp.where(flags[:, 128:] > 0.5, packed, empty).astype(BF16)
    for peer, out in enumerate((r0, r1, r2, r3)):
        rows = slice(peer * ROWS, (peer + 1) * ROWS)
        out[:, :OUT] = dot(pick[rows, :], parts[...]).astype(BF16)
        out[:, OUT:] = packed[rows]


def suffix_kernel(
    place, live, q_nope_in, q_rope_in, latent_in, rope_in, both, k_swap, v_swap,
    out, q_nope, q_rope, latent, rope, rope32, query32, rot32, result, logs, whole_k, whole_v,
    k_sems, v_sems, q_sems, lat_sems,
):
    q_copies = load_all([(q_nope_in, q_nope), (q_rope_in, q_rope), (rope_in, rope)], q_sems)
    k_copies = gather_weights(place, both, k_swap, 0, whole_k, k_sems)
    for i in range(ROWS // 8):
        pltpu.make_async_copy(latent_in.at[pl.ds(8 * i, 8)], latent.at[pl.ds(8 * i, 8)], lat_sems.at[i]).start()
    v_copies = gather_weights(place, both, v_swap, 1, whole_v, v_sems)
    for copy in q_copies:
        copy.wait()
    rope32[...] = rope[...].astype(F32)
    across = iota((ROWS, ROWS), 0) == iota((ROWS, ROWS), 1)
    length = jnp.sum(jnp.where(across, live[...].astype(F32), 0.0), axis=1, keepdims=True)
    for copy in k_copies:
        copy.wait()
    for head in range(HEADS):
        projected = dot(q_nope[:, head * NOPE : (head + 1) * NOPE], whole_k[head])
        query32[head] = projected.astype(BF16).astype(F32)
        rot32[head] = q_rope[:, head * ROPE : (head + 1) * ROPE].astype(F32)
    keys, pairs = 8 * SUF, 8 * SUF // 2
    key, pair = iota((keys, pairs), 0), iota((keys, pairs), 1)
    same = lax.shift_right_logical(key, 6) == lax.bitwise_and(pair, 7)
    first = 2 * lax.shift_right_logical(pair, 3)
    even = (same & (lax.bitwise_and(key, SUF - 1) == first)).astype(BF16)
    odd = (same & (lax.bitwise_and(key, SUF - 1) == first + 1)).astype(BF16)
    lane = iota((8, 128), 1)
    col, row = iota((8, keys), 1), iota((8, keys), 0)

    def block(i, live_rows):
        rows = pl.ds(pl.multiple_of(i * 8, 8), 8)
        query = query32[:, rows, :].reshape(HEADS * 8, KVL).astype(BF16)
        query_rot = rot32[:, rows, :].reshape(HEADS * 8, ROPE).astype(BF16)
        lat = latent[rows].reshape(keys, KVL)
        rot = rope32[rows, :]
        rot = jnp.concatenate([rot[:, 128 * j : 128 * j + 128] for j in range(SUF // 2)], axis=0).astype(BF16)
        rot_keys = (dot(even, rot[:, :ROPE]) + dot(odd, rot[:, ROPE:])).astype(BF16)
        scores = dot(query, lat, LAST) + dot(query_rot, rot_keys, LAST)
        seen = (lax.shift_right_logical(col, 6) == row) & (lax.bitwise_and(col, SUF - 1).astype(F32) < live_rows)
        bias = jnp.where(seen, 0.0, LOW)
        scores = (scores.reshape(HEADS, 8, keys) + bias[None]).reshape(HEADS * 8, keys)
        top = jnp.max(scores, axis=1, keepdims=True)
        raw = jnp.exp2((scores - top) * (SCALE * LOG2E))
        total = jnp.sum(raw, axis=1, keepdims=True)
        summed = dot(raw.astype(BF16), lat) * (1.0 / total)
        result[:, rows, :] = summed.reshape(HEADS, 8, KVL)
        log = (top * SCALE + jnp.log(total)).reshape(HEADS, 8, 1)
        spread = jnp.zeros((8, 128), F32)
        for head in range(HEADS):
            spread = jnp.where(lax.bitwise_and(lane, 15) == head, log[head], spread)
        logs[rows, :] = spread

    for i in range(0, ROWS // 8, 2):
        for k in range(2):
            at = latent.at[pl.ds(8 * (i + k), 8)]
            pltpu.make_async_copy(latent_in.at[pl.ds(8 * (i + k), 8)], at, lat_sems.at[i + k]).wait()
        for k in range(2):
            block(i + k, length[8 * (i + k) : 8 * (i + k) + 8])
    for copy in v_copies:
        copy.wait()
    for head in range(HEADS):
        part = dot(result[head].astype(BF16), whole_v[head], LAST)
        out[:, head * VDIM : (head + 1) * VDIM] = part.astype(BF16)
    out[:, OUT:] = pack_log(logs[...])


def final_kernel(own, r0, r1, r2, r3, out):
    gather = (
        (lax.bitwise_and(iota((128, 128), 0), 15) == iota((128, 128), 1)) & (iota((128, 128), 0) < 48)
    ).astype(BF16)
    parts = (own, r0, r1, r2, r3)
    logs = [dot(part[:, OUT:], gather) for part in parts]
    top = functools.reduce(jnp.maximum, logs)
    weights = [jnp.exp(log - top) for log in logs]
    total = 1.0 / functools.reduce(jnp.add, weights)
    weights = [w * total for w in weights]
    for head in range(HEADS):
        at = slice(head * VDIM, (head + 1) * VDIM)
        scaled = [part[:, at].astype(F32) * weight[:, head : head + 1] for part, weight in zip(parts, weights)]
        out[:, at] = functools.reduce(jnp.add, scaled).astype(BF16)


def row_of(z, x, c):
    return ((z % NZ) * NX + x % NX) * NC + c


CHIPS = [(z, x, c) for z in range(NZ) for x in range(NX) for c in range(NC)]


def ring_z(a):
    return lax.ppermute(a, "rows", [(row_of(z, x, c), row_of(z + 1 - 2 * c, x, c)) for z, x, c in CHIPS])


def ring_x(a, steps=1):
    return lax.ppermute(a, "rows", [(row_of(z, x, c), row_of(z, x + steps * (1 - 2 * c), c)) for z, x, c in CHIPS])


def back_x(a, steps=1):
    return ring_x(a, -steps)


def swap(a):
    return lax.ppermute(a, "rows", [(row_of(z, x, c), row_of(z, x, 1 - c)) for z, x, c in CHIPS])


def cost(us):
    return pl.CostEstimate(flops=int(us * 1e6), bytes_accessed=int(us * 3.0e6), transcendentals=0)


def struct(*shape, dtype=BF16):
    return jax.ShapeDtypeStruct(shape, dtype)


def shards(
    q_nope, q_rope, w_uk, w_uv, prefix_latent, prefix_rope, suffix_latent, suffix_rope, page_slot, page_pattern, suffix_len
):
    row, y = lax.axis_index("rows"), lax.axis_index("proj")
    place = jnp.stack([row // (NX * NC), row // NC % NX, row % NC, y]).astype(I32)

    def exchange(a):
        return lax.all_to_all(a, "proj", split_axis=0, concat_axis=0, tiled=True)

    def after(a, *others):
        return lax.optimization_barrier((a, *others))[0]

    pages, pay, both = pl.pallas_call(
        pack_kernel,
        out_shape=(struct(2, UNIT, KVL), struct(ROWS, PAY), struct(NY * HEADS, NOPE, 128)),
        in_specs=[VMEM] * 2 + [HBM] * 6,
        out_specs=(VMEM,) * 3,
        scratch_shapes=[pltpu.VMEM((2, PAGE * ROPE), BF16), pltpu.SemaphoreType.DMA((4 + 2 * NY,))],
        compiler_params=params(60),
        cost_estimate=cost(2),
        name="pack",
    )(page_pattern.T, page_slot.reshape(1, -1), prefix_rope, prefix_latent, q_nope, q_rope, w_uk, w_uv)
    both = exchange(both)

    a, b = [pages], [swap(pages)]
    a_pay, b_pay = [pay], [swap(pay)]
    a.append(ring_z(a[0]))
    a_pay.append(ring_x(pay))
    b.append(ring_z(b[0]))
    b_pay.append(ring_x(b_pay[0]))
    a.append(ring_z(after(a[1], a_pay[1])))
    a_pay.append(ring_x(after(a_pay[1], a[1])))
    b.append(ring_z(after(b[1], b_pay[1])))
    pays = [pay, a_pay[1], a_pay[2], swap(b_pay[1])]
    a.append(ring_z(after(a[2], b[1], b_pay[1])))
    b.append(ring_z(b[2]))
    a_swap, b_swap = [None, swap(a[1])], [None, swap(b[1])]
    square = (SLOTS, SLOTS)
    q_slots, q_rot, page_bit, *ties = pl.pallas_call(
        gather_kernel,
        out_shape=(
            struct(SLOTS, QN), struct(HEADS, SLOTS, ROPE), struct(SLOTS, 128, dtype=F32),
            struct(*square), struct(*square), struct(*square), struct(*square, dtype=F32),
        ),
        in_specs=[SMEM] + [VMEM] * 4,
        out_specs=(VMEM,) * 7,
        scratch_shapes=[pltpu.VMEM(square, BF16)],
        compiler_params=params(60),
        cost_estimate=cost(3),
        name="gather",
    )(place, after(pays[0], a_swap[1], b_swap[1]), *pays[1:])

    split = both.reshape(NY, HEADS, NOPE, 128)
    k_part, v_part = split[:, : HEADS // 2], split[:, HEADS // 2 :]
    k_swap = swap(after(k_part.reshape(NY * HEADS // 2, NOPE, 128), a[3], b[2], q_slots))
    v_swap = swap(v_part.reshape(NY * HEADS // 2, NOPE, 128))

    q_lat = pl.pallas_call(
        query_kernel,
        out_shape=struct(HEADS, SLOTS, KVL),
        in_specs=[SMEM, VMEM] + [ANY] * 2,
        out_specs=VMEM,
        scratch_shapes=[pltpu.VMEM((HEADS, NOPE, KVL), BF16), pltpu.SemaphoreType.DMA((8,))],
        compiler_params=params(20),
        cost_estimate=cost(3),
        name="queries",
    )(place, q_slots, both, k_swap)

    a.append(ring_z(after(a[3], b[2], a_pay[2])))
    a_swap += [swap(a[2]), swap(a[3])]
    b_swap.append(swap(b[2]))
    early_units = [a[0], b[0], a[1], b[1], a[2], b[2], b_swap[2], a_swap[2], b_swap[1], a_swap[1]]

    def attend(units, base, bits, name):
        count = len(units)
        return pl.pallas_call(
            functools.partial(units_kernel, count, base),
            out_shape=(struct(HEADS, count * 16, KVL), struct(count * 16, 128, dtype=F32)),
            in_specs=[ANY] * count + [VMEM] * 3,
            out_specs=(VMEM, VMEM),
            scratch_shapes=[pltpu.VMEM((count, 2, UNIT, KVL), BF16), pltpu.SemaphoreType.DMA((count,))],
            compiler_params=params(20),
            cost_estimate=cost(1 if base == 0 else 3),
            name=name,
        )(*units, q_lat, q_rot, bits)

    early, early_logs = attend(early_units, 0, page_bit, "early_pages")
    a_swap.append(swap(after(a[4], early_logs)))
    b_swap.append(swap(after(b[3], early_logs)))
    mid_units = [a[3], b[3], a[4], a_swap[3]]
    mid, mid_logs = attend(mid_units, EARLY, after(page_bit, early_logs), "mid_pages")
    late_units = [b_swap[3], a_swap[4]]
    returns = pl.pallas_call(
        late_kernel,
        out_shape=(struct(ROWS, RET),) * 4,
        in_specs=[ANY] * LATE + [SMEM] + [VMEM] * 11 + [ANY] * 2,
        out_specs=(VMEM,) * 4,
        scratch_shapes=[
            pltpu.VMEM((LATE, 2, UNIT, KVL), BF16), pltpu.VMEM((HEADS, LATE * 16, KVL), BF16),
            pltpu.VMEM((LATE * 16, 128), F32), pltpu.VMEM((HEADS, VDIM, KVL), BF16), pltpu.VMEM((SLOTS, OUT), BF16),
            pltpu.SemaphoreType.DMA((LATE,)), pltpu.SemaphoreType.DMA((8,)),
        ],
        compiler_params=params(20),
        cost_estimate=cost(7),
        name="late_pages",
    )(*late_units, place, q_lat, q_rot, page_bit, *ties, early, early_logs, mid, mid_logs, both, v_swap)

    backs = [returns[0], back_x(returns[1]), back_x(returns[2], 2), ring_x(returns[3])]
    k_swap, returns = lax.optimization_barrier((k_swap, returns))
    own = pl.pallas_call(
        suffix_kernel,
        out_shape=struct(ROWS, RET),
        in_specs=[SMEM, VMEM] + [HBM] * 4 + [ANY] * 3,
        out_specs=VMEM,
        scratch_shapes=[
            pltpu.VMEM((ROWS, QN), BF16), pltpu.VMEM((ROWS, QR), BF16),
            pltpu.VMEM((ROWS, SUF, KVL), BF16), pltpu.VMEM((ROWS, SUF * ROPE), BF16),
            pltpu.VMEM((ROWS, SUF * ROPE), F32), pltpu.VMEM((HEADS, ROWS, KVL), F32),
            pltpu.VMEM((HEADS, ROWS, ROPE), F32), pltpu.VMEM((HEADS, ROWS, KVL), F32), pltpu.VMEM((ROWS, 128), F32),
            pltpu.VMEM((HEADS, NOPE, KVL), BF16), pltpu.VMEM((HEADS, VDIM, KVL), BF16),
            pltpu.SemaphoreType.DMA((8,)), pltpu.SemaphoreType.DMA((8,)),
            pltpu.SemaphoreType.DMA((3,)), pltpu.SemaphoreType.DMA((8,)),
        ],
        compiler_params=params(34),
        cost_estimate=cost(8),
        name="suffix",
    )(place, suffix_len.reshape(1, -1), q_nope, q_rope, suffix_latent, suffix_rope, both, k_swap, v_swap)

    return pl.pallas_call(
        final_kernel,
        out_shape=struct(ROWS, OUT),
        in_specs=[VMEM] * 5,
        out_specs=VMEM,
        compiler_params=params(16),
        cost_estimate=cost(2),
        name="combine",
    )(own, *backs)


def solution(mesh):
    return jax.shard_map(
        shards,
        mesh=mesh,
        in_specs=(
            P("rows", "proj"), P("rows", "proj"), P(None, None, "proj"), P(None, None, "proj"),
            P("rows", None, None), P("rows", None), P("rows", None, None), P("rows", None),
            P(), P("rows", None), P("rows"),
        ),
        out_specs=P("rows", "proj"),
        check_vma=False,
    )
```

```python
import functools

import jax
import jax.numpy as jnp
from jax import lax
from jax.experimental import pallas as pl
from jax.experimental.pallas import tpu as pltpu
from jax.sharding import PartitionSpec as P

F32, BF16, I32 = jnp.float32, jnp.bfloat16, jnp.int32
LOW = -1e30

NZ, NX, NC, NY = 8, 4, 2, 4
HEADS = 16
ROWS = 64
NOPE = 128
VDIM = 128
ROPE = 64
KVL = 512
PAGE = 128
SUF = 64
UNIT = PAGE + PAGE * ROPE // KVL
QN = HEADS * NOPE
QR = HEADS * ROPE
PAY = QN + QR + 128
SLOTS = 256
PAIRS = 16
EARLY = 10
MID = 4
LATE = PAIRS - EARLY - MID
SCALE = (NOPE + ROPE) ** -0.5
OUT = HEADS * VDIM
RET = OUT + 128
LOG2E = 1.4426950408889634
LAST = (((1,), (1,)), ((), ()))
FIRST = (((0,), (0,)), ((), ()))


def dot(a, b, dims=(((1,), (0,)), ((), ())), precision=None):
    return lax.dot_general(a, b, dims, preferred_element_type=F32, precision=precision)


def iota(shape, axis):
    return lax.broadcasted_iota(I32, shape, axis)


def params(mib):
    return pltpu.CompilerParams(vmem_limit_bytes=mib << 20)


VMEM = pl.BlockSpec(memory_space=pltpu.VMEM)
SMEM = pl.BlockSpec(memory_space=pltpu.SMEM)
ANY = pl.BlockSpec(memory_space=pl.ANY)
HBM = pl.BlockSpec(memory_space=pltpu.HBM)


def load_all(pairs, sems):
    copies = [pltpu.make_async_copy(src, dst, sems.at[i]) for i, (src, dst) in enumerate(pairs)]
    for copy in copies:
        copy.start()
    return copies


def pack_kernel(
    pattern, page_slot, rope_in, latent_in, q_nope, q_rope, w_uk, w_uv, pages, pay, weights, rope, sems
):
    core, heads = lax.rem(lax.axis_index("rows"), NC), HEADS // 2
    copies = load_all(
        [
            (rope_in, rope),
            (latent_in, pages.at[:, :PAGE, :]),
            (q_nope, pay.at[:, :QN]),
            (q_rope, pay.at[:, QN : QN + QR]),
        ]
        + [
            (full.at[pl.ds(to * HEADS + heads * core, heads)], weights.at[pl.ds((2 * to + i) * heads, heads)])
            for i, full in enumerate((w_uk, w_uv))
            for to in range(NY)
        ],
        sems,
    )
    copies[0].wait()
    flat = rope[...].astype(F32)
    half = PAGE // 2
    sub = iota((8, 128), 0)
    even = (iota((half, PAGE), 1) == 2 * iota((half, PAGE), 0)).astype(F32)
    odd = (iota((half, PAGE), 1) == 2 * iota((half, PAGE), 0) + 1).astype(F32)
    for page in range(2):
        tiles = []
        for tile in range(half // 8):
            piece = jnp.zeros((8, 128), F32)
            for row in range(8):
                at = (tile * 8 + row) * 128
                piece = jnp.where(sub == row, flat[page : page + 1, at : at + 128], piece)
            tiles.append(piece)
        two_tokens = jnp.concatenate(tiles, axis=0)
        turned = dot(two_tokens[:, :ROPE], even, FIRST) + dot(two_tokens[:, ROPE:], odd, FIRST)
        turned = jnp.concatenate([turned[16 * i : 16 * i + 16] for i in range(4)], axis=1)
        pages[page, PAGE:, :] = turned.astype(BF16)
    lane = iota((ROWS, 128), 1)
    across = iota((ROWS, ROWS), 0) == iota((ROWS, ROWS), 1)
    slot_row = page_slot[...].astype(F32)
    slots, owners = [], []
    for k in range(2):
        names = pattern[k : k + 1, :].astype(F32)
        names = jnp.sum(jnp.where(across, names, 0.0), axis=1, keepdims=True).astype(I32)
        named = lane == names
        slot = jnp.sum(jnp.where(named, slot_row, 0.0), axis=1, keepdims=True)
        slots.append(slot)
        owners.append((lane == lax.shift_right_logical(slot.astype(I32), 1)).astype(F32))
    below = (iota((ROWS, ROWS), 0) > iota((ROWS, ROWS), 1)).astype(F32)
    before0 = dot(below, owners[0])
    before1 = dot(below, owners[1]) + jnp.sum(owners[0], axis=0, keepdims=True)
    rank0 = jnp.sum(owners[0] * before0, axis=1, keepdims=True)
    rank1 = jnp.sum(owners[1] * before1, axis=1, keepdims=True)
    code = jnp.zeros((ROWS, 128), F32)
    for at, value in enumerate((slots[0], slots[1], rank0, rank1)):
        code = jnp.where(lane == at, value, code)
    pay[:, QN + QR :] = code.astype(BF16)
    for copy in copies[1:]:
        copy.wait()


def gather_weights(place, both, half_swap, second, whole, sems):
    core, heads = place[2], HEADS // 2
    pairs = []
    for which, part in ((core, both), (1 - core, half_swap)):
        for y in range(NY):
            to = whole.at[pl.ds(which * heads, heads), :, y * 128 : (y + 1) * 128]
            at = (2 * y + second) * heads if part is both else y * heads
            pairs.append((part.at[pl.ds(at, heads)], to))
    return load_all(pairs, sems)


def gather_kernel(
    place, p0, p1, p2, p3, q_nope, q_rot, page_bit, pick_out, partner_out, chosen_out, flags, turned
):
    z, x, core = place[0], place[1], place[2]
    pays = (p0, p1, p2, p3)
    missing = []
    lane = iota((ROWS, 128), 1)
    wide = iota((ROWS, SLOTS), 1)
    picks, bits, places = ([], []), ([], []), []
    for peer, part in enumerate(pays):
        code = part[:, QN + QR :].astype(F32)
        columns = [
            jnp.sum(jnp.where(lane == at, code, 0.0), axis=1, keepdims=True).astype(I32) for at in range(4)
        ]
        found = []
        for k in range(2):
            slot, rank = columns[k], columns[2 + k]
            away = (z - lax.shift_right_logical(slot, 4)) * (1 - 2 * core)
            away = lax.bitwise_and(away, NZ - 1)
            order = jnp.where(away < 3, away, jnp.where(away >= 6, away - 3, away + 2))
            other = jnp.where(lax.bitwise_and(lax.shift_right_logical(slot, 1), 1) != core, 1, 0)
            here = lax.bitwise_and(lax.shift_right_logical(slot, 2), 3) == x
            order = order * 2 + other
            order = jnp.where(order == 13, 15, jnp.where(order == 15, 13, order))
            at = jnp.where(here, order * 16 + peer * 4 + rank, -1)
            picks[k].append((wide == at).astype(F32))
            bits[k].append(lax.bitwise_and(slot, 1).astype(F32) * jnp.ones((1, 128), F32))
            found.append(jnp.where(here, 1.0, 0.0))
        missing.append(jnp.concatenate(found, axis=1))
    pick = [jnp.concatenate(p, axis=0) for p in picks]
    bit = [jnp.concatenate(b, axis=0) for b in bits]
    page_bit[...] = dot(pick[0], bit[0], FIRST) + dot(pick[1], bit[1], FIRST)
    turned[...] = jnp.transpose(pick[0] + pick[1]).astype(BF16)
    pick_out[...] = (pick[0] + pick[1]).astype(BF16)
    pair = dot(pick[0], pick[1], FIRST) + dot(pick[1], pick[0], FIRST)
    partner_out[...] = pair.astype(BF16)
    found = jnp.concatenate(missing, axis=0)
    chosen_out[...] = (pick[0] + pick[1] * (1.0 - found[:, 0:1])).astype(BF16)
    flags[:, :128] = jnp.sum(pair, axis=1, keepdims=True) * jnp.ones((1, 128), F32)
    flags[:, 128:] = jnp.maximum(found[:, 0:1], found[:, 1:2]) * jnp.ones((1, 128), F32)

    def two_heads(i, carry):
        rot = pl.ds(pl.multiple_of(QN + i * 128, 128), 128)
        gathered = dot(turned[...], jnp.concatenate([p[:, rot] for p in pays], axis=0)).astype(BF16)
        at = pl.ds(pl.multiple_of(i * 2 * NOPE, 128), 2 * NOPE)
        q_nope[:, at] = dot(turned[...], jnp.concatenate([p[:, at] for p in pays], axis=0)).astype(BF16)
        for k in range(2):
            q_rot[2 * i + k] = gathered[:, k * ROPE : (k + 1) * ROPE]
        return carry

    lax.fori_loop(0, HEADS // 2, two_heads, 0)


def query_kernel(place, q_nope, both, k_swap, q_lat, whole, sems):
    for copy in gather_weights(place, both, k_swap, 0, whole, sems):
        copy.wait()

    def two_heads(i, carry):
        left = q_nope[:, pl.ds(pl.multiple_of(i * 2 * NOPE, 128), 2 * NOPE)]
        for k in range(2):
            q_lat[2 * i + k] = dot(left[:, k * NOPE : (k + 1) * NOPE], whole[2 * i + k]).astype(BF16)
        return carry

    lax.fori_loop(0, HEADS // 2, two_heads, 0)


def start_units(units, held, sems):
    copies = [pltpu.make_async_copy(unit, held.at[i], sems.at[i]) for i, unit in enumerate(units)]
    for copy in copies:
        copy.start()


def attend_units(count, base, unit0, q_lat, q_rot, page_bit, held, sems, result, logs):
    lane = iota((16, 128), 1)

    def block(i):
        unit = held.at[i]
        latent = unit[:, :PAGE, :].reshape(2 * PAGE, KVL)
        rot = unit[:, PAGE:, :]
        keys = jnp.concatenate(
            [
                jnp.concatenate([rot[page, :, 128 * j : 128 * j + 128] for j in range(4)], axis=0)
                for page in range(2)
            ],
            axis=1,
        )
        at = pl.ds(pl.multiple_of((base + i) * 16, 16), 16)
        query = q_lat[:, at, :].reshape(HEADS * 16, KVL)
        query_rot = q_rot[:, at, :].reshape(HEADS * 16, ROPE)
        scores = dot(query, latent, LAST) + dot(query_rot, keys)
        bit = page_bit[at, :]
        bias = jnp.concatenate(
            [jnp.where(bit < 0.5, 0.0, LOW), jnp.where(bit < 0.5, LOW, 0.0)], axis=1
        )
        scores = (scores.reshape(HEADS, 16, 2 * PAGE) + bias[None]).reshape(HEADS * 16, 2 * PAGE)
        top = jnp.max(scores, axis=1, keepdims=True)
        raw = jnp.exp2((scores - top) * (SCALE * LOG2E))
        total = jnp.sum(raw, axis=1, keepdims=True)
        summed = dot(raw.astype(BF16), latent) * (1.0 / total)
        out_at = pl.ds(pl.multiple_of(i * 16, 16), 16)
        result[:, out_at, :] = summed.astype(BF16).reshape(HEADS, 16, KVL)
        log = (top * SCALE + jnp.log(total)).reshape(HEADS, 16, 1)
        spread = jnp.zeros((16, 128), F32)
        for head in range(HEADS):
            mine = (lax.bitwise_and(lane, 15) == head) & (lane < 48)
            spread = jnp.where(mine, log[head], spread)
        logs[out_at, :] = spread

    def body(i, carry):
        for k in range(2):
            pltpu.make_async_copy(unit0, held.at[2 * i + k], sems.at[2 * i + k]).wait()
        for k in range(2):
            block(2 * i + k)
        return carry

    lax.fori_loop(0, count // 2, body, 0)


def units_kernel(count, base, *refs):
    units = refs[:count]
    q_lat, q_rot, page_bit, result, logs, held, sems = refs[count:]
    start_units(units, held, sems)
    attend_units(count, base, units[0], q_lat, q_rot, page_bit, held, sems, result, logs)


def pack_log(log):
    lane = iota(log.shape, 1)
    high = log.astype(BF16).astype(F32)
    rest = log - high
    middle = rest.astype(BF16).astype(F32)
    packed = jnp.where(lane < 16, high, jnp.where(lane < 32, middle, rest - middle))
    return jnp.where(lane < 48, packed, 0.0).astype(BF16)


def late_kernel(*refs):
    units = refs[:LATE]
    (
        place, q_lat, q_rot, page_bit, pick, partner, chosen, flags, early, early_logs, mid, mid_logs, weights, v_swap,
        r0, r1, r2, r3, held, result, logs, whole, parts, sems, w_sems,
    ) = refs[LATE:]
    start_units(units, held, sems)
    copies = gather_weights(place, weights, v_swap, 1, whole, w_sems)
    attend_units(LATE, EARLY + MID, units[0], q_lat, q_rot, page_bit, held, sems, result, logs)
    log = jnp.concatenate([early_logs[...], mid_logs[...], logs[...]], axis=0)
    other = (flags[:, :128] - 1.0) * (-LOW)
    rest = log
    for _ in range(3):
        part = rest.astype(BF16)
        rest = rest - part.astype(F32)
        other = other + dot(partner[...], part)
    top = jnp.maximum(log, other)
    mine = jnp.exp(log - top)
    both = mine + jnp.exp(other - top)
    weight = mine / both
    merged = top + jnp.log(both)
    for copy in copies:
        copy.wait()
    for head in range(HEADS):
        mixed = jnp.concatenate([early[head], mid[head], result[head]], axis=0)
        part = dot(mixed, whole[head], LAST) * weight[:, head : head + 1]
        parts[:, head * VDIM : (head + 1) * VDIM] = part.astype(BF16)
    lane = iota((SLOTS, 128), 1)
    empty = jnp.where(lane < 16, LOW, 0.0)
    packed = dot(chosen[...], pack_log(merged))
    packed = jnp.where(flags[:, 128:] > 0.5, packed, empty).astype(BF16)
    for peer, out in enumerate((r0, r1, r2, r3)):
        rows = slice(peer * ROWS, (peer + 1) * ROWS)
        out[:, :OUT] = dot(pick[rows, :], parts[...]).astype(BF16)
        out[:, OUT:] = packed[rows]


def suffix_kernel(
    place, live, q_nope_in, q_rope_in, latent_in, rope_in, both, k_swap, v_swap,
    out, q_nope, q_rope, latent, rope, rope32, query32, rot32, result, logs, whole_k, whole_v,
    k_sems, v_sems, q_sems, lat_sems,
):
    q_copies = load_all([(q_nope_in, q_nope), (q_rope_in, q_rope), (rope_in, rope)], q_sems)
    k_copies = gather_weights(place, both, k_swap, 0, whole_k, k_sems)
    for i in range(ROWS // 8):
        pltpu.make_async_copy(latent_in.at[pl.ds(8 * i, 8)], latent.at[pl.ds(8 * i, 8)], lat_sems.at[i]).start()
    v_copies = gather_weights(place, both, v_swap, 1, whole_v, v_sems)
    for copy in q_copies:
        copy.wait()
    rope32[...] = rope[...].astype(F32)
    across = iota((ROWS, ROWS), 0) == iota((ROWS, ROWS), 1)
    length = jnp.sum(jnp.where(across, live[...].astype(F32), 0.0), axis=1, keepdims=True)
    for copy in k_copies:
        copy.wait()
    for head in range(HEADS):
        projected = dot(q_nope[:, head * NOPE : (head + 1) * NOPE], whole_k[head])
        query32[head] = projected.astype(BF16).astype(F32)
        rot32[head] = q_rope[:, head * ROPE : (head + 1) * ROPE].astype(F32)
    keys, pairs = 8 * SUF, 8 * SUF // 2
    key, pair = iota((keys, pairs), 0), iota((keys, pairs), 1)
    same = lax.shift_right_logical(key, 6) == lax.bitwise_and(pair, 7)
    first = 2 * lax.shift_right_logical(pair, 3)
    even = (same & (lax.bitwise_and(key, SUF - 1) == first)).astype(BF16)
    odd = (same & (lax.bitwise_and(key, SUF - 1) == first + 1)).astype(BF16)
    lane = iota((8, 128), 1)
    col, row = iota((8, keys), 1), iota((8, keys), 0)

    def block(i, live_rows):
        rows = pl.ds(pl.multiple_of(i * 8, 8), 8)
        query = query32[:, rows, :].reshape(HEADS * 8, KVL).astype(BF16)
        query_rot = rot32[:, rows, :].reshape(HEADS * 8, ROPE).astype(BF16)
        lat = latent[rows].reshape(keys, KVL)
        rot = rope32[rows, :]
        rot = jnp.concatenate([rot[:, 128 * j : 128 * j + 128] for j in range(SUF // 2)], axis=0).astype(BF16)
        rot_keys = (dot(even, rot[:, :ROPE]) + dot(odd, rot[:, ROPE:])).astype(BF16)
        scores = dot(query, lat, LAST) + dot(query_rot, rot_keys, LAST)
        seen = (lax.shift_right_logical(col, 6) == row) & (lax.bitwise_and(col, SUF - 1).astype(F32) < live_rows)
        bias = jnp.where(seen, 0.0, LOW)
        scores = (scores.reshape(HEADS, 8, keys) + bias[None]).reshape(HEADS * 8, keys)
        top = jnp.max(scores, axis=1, keepdims=True)
        raw = jnp.exp2((scores - top) * (SCALE * LOG2E))
        total = jnp.sum(raw, axis=1, keepdims=True)
        summed = dot(raw.astype(BF16), lat) * (1.0 / total)
        result[:, rows, :] = summed.reshape(HEADS, 8, KVL)
        log = (top * SCALE + jnp.log(total)).reshape(HEADS, 8, 1)
        spread = jnp.zeros((8, 128), F32)
        for head in range(HEADS):
            spread = jnp.where(lax.bitwise_and(lane, 15) == head, log[head], spread)
        logs[rows, :] = spread

    for i in range(0, ROWS // 8, 2):
        for k in range(2):
            at = latent.at[pl.ds(8 * (i + k), 8)]
            pltpu.make_async_copy(latent_in.at[pl.ds(8 * (i + k), 8)], at, lat_sems.at[i + k]).wait()
        for k in range(2):
            block(i + k, length[8 * (i + k) : 8 * (i + k) + 8])
    for copy in v_copies:
        copy.wait()
    for head in range(HEADS):
        part = dot(result[head].astype(BF16), whole_v[head], LAST)
        out[:, head * VDIM : (head + 1) * VDIM] = part.astype(BF16)
    out[:, OUT:] = pack_log(logs[...])


def final_kernel(own, r0, r1, r2, r3, out):
    gather = (
        (lax.bitwise_and(iota((128, 128), 0), 15) == iota((128, 128), 1)) & (iota((128, 128), 0) < 48)
    ).astype(BF16)
    parts = (own, r0, r1, r2, r3)
    logs = [dot(part[:, OUT:], gather) for part in parts]
    top = functools.reduce(jnp.maximum, logs)
    weights = [jnp.exp(log - top) for log in logs]
    total = 1.0 / functools.reduce(jnp.add, weights)
    weights = [w * total for w in weights]
    for head in range(HEADS):
        at = slice(head * VDIM, (head + 1) * VDIM)
        scaled = [part[:, at].astype(F32) * weight[:, head : head + 1] for part, weight in zip(parts, weights)]
        out[:, at] = functools.reduce(jnp.add, scaled).astype(BF16)


def row_of(z, x, c):
    return ((z % NZ) * NX + x % NX) * NC + c


CHIPS = [(z, x, c) for z in range(NZ) for x in range(NX) for c in range(NC)]


def ring_z(a):
    return lax.ppermute(a, "rows", [(row_of(z, x, c), row_of(z + 1 - 2 * c, x, c)) for z, x, c in CHIPS])


def ring_x(a, steps=1):
    return lax.ppermute(a, "rows", [(row_of(z, x, c), row_of(z, x + steps * (1 - 2 * c), c)) for z, x, c in CHIPS])


def back_x(a, steps=1):
    return ring_x(a, -steps)


def swap(a):
    return lax.ppermute(a, "rows", [(row_of(z, x, c), row_of(z, x, 1 - c)) for z, x, c in CHIPS])


def cost(us):
    return pl.CostEstimate(flops=int(us * 1e6), bytes_accessed=int(us * 3.0e6), transcendentals=0)


def struct(*shape, dtype=BF16):
    return jax.ShapeDtypeStruct(shape, dtype)


def shards(
    q_nope, q_rope, w_uk, w_uv, prefix_latent, prefix_rope, suffix_latent, suffix_rope, page_slot, page_pattern, suffix_len
):
    row, y = lax.axis_index("rows"), lax.axis_index("proj")
    place = jnp.stack([row // (NX * NC), row // NC % NX, row % NC, y]).astype(I32)

    def exchange(a):
        return lax.all_to_all(a, "proj", split_axis=0, concat_axis=0, tiled=True)

    def after(a, *others):
        return lax.optimization_barrier((a, *others))[0]

    pages, pay, both = pl.pallas_call(
        pack_kernel,
        out_shape=(struct(2, UNIT, KVL), struct(ROWS, PAY), struct(NY * HEADS, NOPE, 128)),
        in_specs=[VMEM] * 2 + [HBM] * 6,
        out_specs=(VMEM,) * 3,
        scratch_shapes=[pltpu.VMEM((2, PAGE * ROPE), BF16), pltpu.SemaphoreType.DMA((4 + 2 * NY,))],
        compiler_params=params(60),
        cost_estimate=cost(2),
        name="pack",
    )(page_pattern.T, page_slot.reshape(1, -1), prefix_rope, prefix_latent, q_nope, q_rope, w_uk, w_uv)
    both = exchange(both)

    a, b = [pages], [swap(pages)]
    a_pay, b_pay = [pay], [swap(pay)]
    a.append(ring_z(a[0]))
    a_pay.append(ring_x(pay))
    b.append(ring_z(b[0]))
    b_pay.append(ring_x(b_pay[0]))
    a.append(ring_z(after(a[1], a_pay[1])))
    a_pay.append(ring_x(after(a_pay[1], a[1])))
    b.append(ring_z(after(b[1], b_pay[1])))
    pays = [pay, a_pay[1], a_pay[2], swap(b_pay[1])]
    a.append(ring_z(after(a[2], b[1], b_pay[1])))
    b.append(ring_z(b[2]))
    a_swap, b_swap = [None, swap(a[1])], [None, swap(b[1])]
    square = (SLOTS, SLOTS)
    q_slots, q_rot, page_bit, *ties = pl.pallas_call(
        gather_kernel,
        out_shape=(
            struct(SLOTS, QN), struct(HEADS, SLOTS, ROPE), struct(SLOTS, 128, dtype=F32),
            struct(*square), struct(*square), struct(*square), struct(*square, dtype=F32),
        ),
        in_specs=[SMEM] + [VMEM] * 4,
        out_specs=(VMEM,) * 7,
        scratch_shapes=[pltpu.VMEM(square, BF16)],
        compiler_params=params(60),
        cost_estimate=cost(0.3),
        name="gather",
    )(place, after(pays[0], a_swap[1], b_swap[1]), *pays[1:])

    split = both.reshape(NY, HEADS, NOPE, 128)
    k_part, v_part = split[:, : HEADS // 2], split[:, HEADS // 2 :]
    k_swap = swap(after(k_part.reshape(NY * HEADS // 2, NOPE, 128), a[3], q_slots))
    v_swap = swap(v_part.reshape(NY * HEADS // 2, NOPE, 128))

    q_lat = pl.pallas_call(
        query_kernel,
        out_shape=struct(HEADS, SLOTS, KVL),
        in_specs=[SMEM, VMEM] + [ANY] * 2,
        out_specs=VMEM,
        scratch_shapes=[pltpu.VMEM((HEADS, NOPE, KVL), BF16), pltpu.SemaphoreType.DMA((8,))],
        compiler_params=params(20),
        cost_estimate=cost(3),
        name="queries",
    )(place, after(q_slots, b[2]), both, k_swap)

    a.append(ring_z(after(a[3], b[2], a_pay[2])))
    a_swap += [swap(a[2]), swap(a[3])]
    b_swap.append(swap(b[2]))
    early_units = [a[0], b[0], a[1], b[1], a[2], b[2], b_swap[2], a_swap[2], b_swap[1], a_swap[1]]

    def attend(units, base, bits, name):
        count = len(units)
        return pl.pallas_call(
            functools.partial(units_kernel, count, base),
            out_shape=(struct(HEADS, count * 16, KVL), struct(count * 16, 128, dtype=F32)),
            in_specs=[ANY] * count + [VMEM] * 3,
            out_specs=(VMEM, VMEM),
            scratch_shapes=[pltpu.VMEM((count, 2, UNIT, KVL), BF16), pltpu.SemaphoreType.DMA((count,))],
            compiler_params=params(20),
            cost_estimate=cost(1 if base == 0 else 3),
            name=name,
        )(*units, q_lat, q_rot, bits)

    early, early_logs = attend(early_units, 0, page_bit, "early_pages")
    a_swap.append(swap(after(a[4], early_logs)))
    b_swap.append(swap(after(b[3], early_logs)))
    mid_units = [a[3], b[3], a[4], a_swap[3]]
    mid, mid_logs = attend(mid_units, EARLY, after(page_bit, early_logs), "mid_pages")
    late_units = [b_swap[3], a_swap[4]]
    returns = pl.pallas_call(
        late_kernel,
        out_shape=(struct(ROWS, RET),) * 4,
        in_specs=[ANY] * LATE + [SMEM] + [VMEM] * 11 + [ANY] * 2,
        out_specs=(VMEM,) * 4,
        scratch_shapes=[
            pltpu.VMEM((LATE, 2, UNIT, KVL), BF16), pltpu.VMEM((HEADS, LATE * 16, KVL), BF16),
            pltpu.VMEM((LATE * 16, 128), F32), pltpu.VMEM((HEADS, VDIM, KVL), BF16), pltpu.VMEM((SLOTS, OUT), BF16),
            pltpu.SemaphoreType.DMA((LATE,)), pltpu.SemaphoreType.DMA((8,)),
        ],
        compiler_params=params(20),
        cost_estimate=cost(7),
        name="late_pages",
    )(*late_units, place, q_lat, q_rot, page_bit, *ties, early, early_logs, mid, mid_logs, both, v_swap)

    backs = [returns[0], back_x(returns[1]), back_x(returns[2], 2), ring_x(returns[3])]
    k_swap, returns = lax.optimization_barrier((k_swap, returns))
    own = pl.pallas_call(
        suffix_kernel,
        out_shape=struct(ROWS, RET),
        in_specs=[SMEM, VMEM] + [HBM] * 4 + [ANY] * 3,
        out_specs=VMEM,
        scratch_shapes=[
            pltpu.VMEM((ROWS, QN), BF16), pltpu.VMEM((ROWS, QR), BF16),
            pltpu.VMEM((ROWS, SUF, KVL), BF16), pltpu.VMEM((ROWS, SUF * ROPE), BF16),
            pltpu.VMEM((ROWS, SUF * ROPE), F32), pltpu.VMEM((HEADS, ROWS, KVL), F32),
            pltpu.VMEM((HEADS, ROWS, ROPE), F32), pltpu.VMEM((HEADS, ROWS, KVL), F32), pltpu.VMEM((ROWS, 128), F32),
            pltpu.VMEM((HEADS, NOPE, KVL), BF16), pltpu.VMEM((HEADS, VDIM, KVL), BF16),
            pltpu.SemaphoreType.DMA((8,)), pltpu.SemaphoreType.DMA((8,)),
            pltpu.SemaphoreType.DMA((3,)), pltpu.SemaphoreType.DMA((8,)),
        ],
        compiler_params=params(34),
        cost_estimate=cost(8),
        name="suffix",
    )(place, suffix_len.reshape(1, -1), q_nope, q_rope, suffix_latent, suffix_rope, both, k_swap, v_swap)

    return pl.pallas_call(
        final_kernel,
        out_shape=struct(ROWS, OUT),
        in_specs=[VMEM] * 5,
        out_specs=VMEM,
        compiler_params=params(16),
        cost_estimate=cost(2),
        name="combine",
    )(own, *backs)


def solution(mesh):
    return jax.shard_map(
        shards,
        mesh=mesh,
        in_specs=(
            P("rows", "proj"), P("rows", "proj"), P(None, None, "proj"), P(None, None, "proj"),
            P("rows", None, None), P("rows", None), P("rows", None, None), P("rows", None),
            P(), P("rows", None), P("rows"),
        ),
        out_specs=P("rows", "proj"),
        check_vma=False,
    )
```
